256 devices in a mesh: pipe: 16 (over z, y_hi), seq: 16 (over x, y_lo, core).
Axes of the slice: x: 4, y: 4 (y_hi: 2, y_lo: 2; y = y_hi * 2 + y_lo), z: 8, core: 2. Of those that a mesh axis runs over, the one named last changes fastest.
Arguments:
- hidden_in: bfloat16 [16, 2048, 3072], P('pipe', 'seq'), may hold values from -6 to 6
- queries: bfloat16 [16, 2, 2048, 2048], P('pipe', None, 'seq'), may hold values from -40 to 40
- keys: bfloat16 [16, 2, 2048, 2048], P('pipe', None, 'seq'), may hold values from -40 to 40
- values: bfloat16 [16, 2, 2048, 2048], P('pipe', None, 'seq'), may hold values from -6 to 6
- segments: int32 [16, 2, 2048], P('pipe', None, 'seq'), may hold values from 0 to 3, never falling along the last dimension, each value on 1 to 1024 neighbouring positions
- gates: float32 [16, 2, 4, 3072], P('pipe'), may hold values from -32 to 32
- out_weight: bfloat16 [16, 2048, 3072], P('pipe', 'seq'), may hold values from -0.125 to 0.125
- upstream: bfloat16 [16, 2048, 3072], P('pipe', 'seq'), may hold values from -6 to 6
- fresh: bfloat16 [2048, 3072], P('seq'), may hold values from -6 to 6
- loss_grad: bfloat16 [2048, 3072], P('seq'), may hold values from -6 to 6
Outputs:
- next_act: bfloat16 [16, 2048, 3072], P('pipe', 'seq')
- next_grad: bfloat16 [16, 2048, 3072], P('pipe', 'seq')
- qkv_grads: bfloat16 [16, 3, 2048, 2048], P('pipe', None, 'seq')
The draws below stay inside these ranges and needn't reach their ends.
All inputs are finite; a program needn't handle non-finite values.
Results may differ from the reference program's by a relative error of at most 0.029.
Values may be sent and summed in bfloat16 or wider, within the bound.
No kernel may reach another device: no remote copies, remote signals or barrier semaphores. Data moves between devices by JAX's collectives and lax.ppermute only.
A program may use at most 128 MiB of HBM per device.

```python
import math
import jax
import jax.numpy as jnp
import numpy as np
from jax import lax

D = 3072
HEADS = 16
HD = 128
E = 2048
SEGS = 4
TOKENS = 2048
SECTIONS = 16


def common_rows(key):
    return jnp.clip(jax.random.normal(jax.random.fold_in(key, 101), (SECTIONS, 2, TOKENS, E), jnp.float32), -5.0, 5.0)


def draw_queries(key, part):
    key = jax.random.fold_in(key, 1)
    result = jnp.clip(jax.random.normal(key, (SECTIONS, 2, TOKENS, E), jnp.float32), -5.0, 5.0)
    return result.astype(jnp.bfloat16)


def draw_keys(key, part):
    base = common_rows(key)
    result = base
    return result.astype(jnp.bfloat16)


def levels(own_key, shape, cuts, smallest, largest):
    def one(axis_at, parts):
        draws = jax.random.uniform(jax.random.fold_in(jax.random.fold_in(own_key, 6), axis_at), (parts,), jnp.float32, smallest / len(cuts), largest / len(cuts))
        return jnp.repeat(jnp.exp(draws), shape[axis_at] // parts).reshape((-1,) + (1,) * (len(shape) - axis_at - 1))

    level = one(*cuts[0])
    for cut in cuts[1:]:
        level = level * one(*cut)
    return level


def length_profile(amount, total, bound, slope):
    weights = [(1 << 20) // math.isqrt(rank ** slope) + 1 for rank in range(2, amount + 1)]
    spare, holding = total - bound - (amount - 1), [1] * (amount - 1)
    while spare > 0:
        movable = [i for i in range(amount - 1) if holding[i] < bound]
        mass, remaining = sum([weights[i] for i in movable]), spare
        for i in movable:
            addition = min(bound - holding[i], max(1, remaining * weights[i] // mass), spare)
            holding[i] = holding[i] + addition
            spare = spare - addition
    return np.array([bound] + holding)


def ragged_sizes(own_key, amount, total, most, slope):
    if amount == 2:
        one = jax.random.randint(own_key, (), max(1, total - most), min(most, total - 1) + 1)
        return jnp.stack([one, total - one])
    sizes = jnp.asarray(length_profile(amount, total, most, slope), jnp.int32)
    pairs = (amount - 1) // 2
    donor, taker = sizes[1:1 + 2 * pairs:2], sizes[2:2 + 2 * pairs:2]
    slack = jnp.minimum(donor - 1, most - taker)
    moved = jax.random.randint(jax.random.fold_in(own_key, 1), (pairs,), 0, 1 << 20) % (slack + 1)
    sizes = sizes.at[1:1 + 2 * pairs:2].set(donor - moved).at[2:2 + 2 * pairs:2].set(taker + moved)
    return sizes[jax.random.permutation(jax.random.fold_in(own_key, 2), amount)]


def gaussian(stream_key, dims, scale, most, shards=(), kind=jnp.bfloat16):
    factor_of = levels(stream_key, dims, shards, -0.22, 0.18) if shards else 1.0
    drawn = jax.random.normal(stream_key, dims, jnp.float32) * scale * factor_of
    return jnp.minimum(jnp.maximum(drawn, -most), most).astype(kind)


def setup_inputs(seed: int = 0) -> dict:
    key_list = jax.random.split(jax.random.key(seed), 11)
    hidden_in = gaussian(key_list[0], (SECTIONS, TOKENS, D), 1.0, 6.0, ((0, 16), (1, 16)))
    queries = draw_queries(jax.random.fold_in(key_list[10], 71), 0)
    keys = draw_keys(jax.random.fold_in(key_list[10], 71), 0)
    values = gaussian(key_list[3], (SECTIONS, 2, TOKENS, E), 1.0, 6.0, ((0, 16), (2, 16)))
    segments = jax.vmap(lambda own: jnp.searchsorted(jnp.cumsum(ragged_sizes(own, SEGS, TOKENS, TOKENS // 2, 2)), jnp.arange(TOKENS), side="right"))(jax.random.split(key_list[4], SECTIONS * 2)).reshape((SECTIONS, 2, TOKENS)).astype(jnp.int32)
    gates = gaussian(key_list[5], (SECTIONS, 2, SEGS, D), 8.0, 32.0, ((0, 16),), jnp.float32)
    out_weight = gaussian(key_list[6], (SECTIONS, E, D), E ** -0.5, 0.125, ((0, 16), (1, 16)))
    upstream = gaussian(key_list[7], (SECTIONS, TOKENS, D), 1.0, 6.0, ((0, 16), (1, 16)))
    fresh = gaussian(key_list[8], (TOKENS, D), 1.0, 6.0, ((0, 16),))
    loss_grad = gaussian(key_list[9], (TOKENS, D), 1.0, 6.0, ((0, 16),))
    return dict(hidden_in=hidden_in, queries=queries, keys=keys, values=values, segments=segments, gates=gates, out_weight=out_weight, upstream=upstream, fresh=fresh, loss_grad=loss_grad)


def head_probs(query, key_rows, mask):
    scores = jnp.dot(query, key_rows.T, preferred_element_type=jnp.float32) * (HD ** -0.5)
    scores = jnp.where(mask, scores, -1e30)
    return jax.nn.softmax(scores, axis=-1)


def head_forward(query, key_rows, value_rows, mask):
    probs = head_probs(query, key_rows, mask)
    return jnp.dot(probs.astype(jnp.bfloat16), value_rows, preferred_element_type=jnp.float32).astype(jnp.bfloat16)


def head_backward(query, key_rows, value_rows, grad_out, mask):
    probs = head_probs(query, key_rows, mask)
    probs_b = probs.astype(jnp.bfloat16)
    dprobs = jnp.dot(grad_out, value_rows.T, preferred_element_type=jnp.float32)
    dvalue = jnp.dot(probs_b.T, grad_out, preferred_element_type=jnp.float32).astype(jnp.bfloat16)
    delta = jnp.sum(probs * dprobs, axis=-1, keepdims=True)
    dscores = (probs * (dprobs - delta)).astype(jnp.bfloat16)
    dquery = (jnp.dot(dscores, key_rows, preferred_element_type=jnp.float32) * (HD ** -0.5)).astype(jnp.bfloat16)
    dkey = (jnp.dot(dscores.T, query, preferred_element_type=jnp.float32) * (HD ** -0.5)).astype(jnp.bfloat16)
    return dquery, dkey, dvalue


def split_heads(array):
    return array.reshape(TOKENS, HEADS, HD).transpose(1, 0, 2)


def join_heads(array):
    return array.transpose(1, 0, 2).reshape(TOKENS, E)


def per_sample(seg, table):
    onehot = (seg[:, None] == jnp.arange(SEGS, dtype=jnp.int32)[None, :]).astype(jnp.float32)
    return jnp.sum(onehot[:, :, None] * table[None, :, :], axis=1)


def section_tick(inputs):
    hidden, query, key_rows, value_rows, seg, gate, weight, grad_in = inputs
    mask_fwd = seg[0][:, None] == seg[0][None, :]
    attn_heads = lax.map(lambda t: head_forward(t[0], t[1], t[2], mask_fwd),
                         (split_heads(query[0]), split_heads(key_rows[0]), split_heads(value_rows[0])))
    attn = join_heads(attn_heads)
    proj = jnp.dot(attn, weight, preferred_element_type=jnp.float32)
    out = (hidden.astype(jnp.float32) + per_sample(seg[0], gate[0]) * proj).astype(jnp.bfloat16)
    g_scaled = (per_sample(seg[1], gate[1]) * grad_in.astype(jnp.float32)).astype(jnp.bfloat16)
    g_attn = jnp.dot(g_scaled, weight.T, preferred_element_type=jnp.float32).astype(jnp.bfloat16)
    mask_bwd = seg[1][:, None] == seg[1][None, :]
    dquery, dkey, dvalue = lax.map(lambda t: head_backward(t[0], t[1], t[2], t[3], mask_bwd),
                                   (split_heads(query[1]), split_heads(key_rows[1]), split_heads(value_rows[1]), split_heads(g_attn)))
    grads = jnp.stack([join_heads(dquery), join_heads(dkey), join_heads(dvalue)], axis=0)
    return out, grads


def reference(hidden_in, queries, keys, values, segments, gates, out_weight, upstream, fresh, loss_grad):
    outs, grads = lax.map(section_tick, (hidden_in, queries, keys, values, segments, gates, out_weight, upstream))
    next_act = jnp.concatenate([fresh[None], outs[:-1]], axis=0)
    next_grad = jnp.concatenate([upstream[1:], loss_grad[None]], axis=0)
    return next_act, next_grad, grads
```

```python
import functools

import jax
import jax.numpy as jnp
from jax import lax
from jax.experimental import pallas as pl
from jax.experimental.pallas import tpu as pltpu
from jax.sharding import PartitionSpec as P

HD = 128
SCALE = HD ** (-0.5)
EXP2 = SCALE * 1.4426950408889634
LOW = -1e30
QB = 256
KT = 512
SEG_ROWS = 16
F32 = jnp.float32
BF16 = jnp.bfloat16

XN, YN = 4, 2
CHIPS = XN * YN
SAME_CORE = [[2 * i + c for i in range(CHIPS)] for c in range(2)]
CORE = [(i, i ^ 1) for i in range(2 * CHIPS)]
YSWAP = [(i, i ^ 2) for i in range(2 * CHIPS)]
XUP = [(i, (i + 4) % 16) for i in range(2 * CHIPS)]
XDOWN = [(i, (i - 4) % 16) for i in range(2 * CHIPS)]


def params(mib):
    return pltpu.CompilerParams(vmem_limit_bytes=mib * 1024 * 1024)


def whole(count):
    return [pl.BlockSpec(memory_space=pltpu.VMEM)] * count


def cost(flops, nbytes):
    return pl.CostEstimate(flops=flops, bytes_accessed=nbytes, transcendentals=0)


def dot(a, b, dims):
    return lax.dot_general(a, b, (dims, ((), ())), preferred_element_type=F32)


def pack_kernel(seg_ref, q_ref, k_ref, v_ref, out_ref):
    rows = q_ref.shape[0]
    for h in range(out_ref.shape[0]):
        cols = slice(h * HD, (h + 1) * HD)
        out_ref[h, 0:rows, :] = q_ref[:, cols]
        out_ref[h, rows:2 * rows, :] = k_ref[:, cols]
        out_ref[h, 2 * rows:3 * rows, :] = v_ref[:, cols]
        out_ref[h, 3 * rows:, :] = jnp.broadcast_to(
            seg_ref[...].astype(F32), (SEG_ROWS, HD)
        ).astype(BF16)


def pack(queries, keys, values, segments, batch):
    rows, width = queries.shape[2], queries.shape[3]
    heads = width // HD
    block = pl.BlockSpec((None, None, rows, width), lambda i: (0, batch, 0, 0))
    return pl.pallas_call(
        pack_kernel,
        grid=(1,),
        out_shape=jax.ShapeDtypeStruct((heads, 3 * rows + SEG_ROWS, HD), BF16),
        in_specs=[pl.BlockSpec((1, rows), lambda i: (0, 0)), block, block, block],
        out_specs=pl.BlockSpec((heads, 3 * rows + SEG_ROWS, HD), lambda i: (0, 0, 0)),
        compiler_params=params(24),
        cost_estimate=cost(0, 6 * rows * width * 2),
        name="pack",
    )(segments[0, batch][None], queries, keys, values)


def sample_starts(in_ref, rows):
    ids = in_ref[:, 3 * rows:, :].astype(F32)
    return [
        jnp.sum(jnp.where(ids < s, 1.0, 0.0)).astype(jnp.int32) // SEG_ROWS for s in (1, 2, 3)
    ]


def sample_of(position, starts):
    return sum(jnp.where(position >= b, 1.0, 0.0) for b in starts)


def tile_range(first, last, starts, total):
    low, high = 0, total
    for b in starts:
        low = jnp.maximum(low, jnp.where(b <= first, b, 0))
        high = jnp.minimum(high, jnp.where(b > last, b, total))
    return low // KT, (high + KT - 1) // KT


def block_rows(ref, index, count, start, rows):
    per = count // rows
    return ref[pl.ds(index * per, per), start:start + rows, :].reshape(count, HD)


def fill_samples(seg_s, starts):
    total = seg_s.shape[0]
    for i in range(total // 256):
        position = i * 256 + lax.broadcasted_iota(jnp.int32, (256, HD), 0)
        seg_s[i * 256:(i + 1) * 256, :] = sample_of(position, starts)


def forward_kernel(in_ref, out_ref, vt_s, seg_s):
    blocks, rows = in_ref.shape[0], 128
    total = blocks * rows
    starts = sample_starts(in_ref, rows)
    fill_samples(seg_s, starts)
    for i in range(blocks):
        vt_s[:, i * rows:(i + 1) * rows] = in_ref[i, 2 * rows:3 * rows, :].T

    def per_block(i, _):
        q = block_rows(in_ref, i, QB, 0, rows)
        first = i * QB
        seg_q = sample_of(first + lax.broadcasted_iota(jnp.int32, (1, QB), 1), starts)
        begin, end = tile_range(first, first + QB - 1, starts, total)

        def per_tile(t, carry):
            m, l, acc = carry
            k = block_rows(in_ref, t, KT, rows, rows)
            s = dot(k, q, ((1,), (1,)))
            seg_k = seg_s[pl.ds(pl.multiple_of(t * KT, KT), KT), :]
            s = jnp.where(jnp.concatenate([seg_k, seg_k], axis=1) == seg_q, s, LOW)
            m_new = jnp.maximum(m, jnp.max(s, axis=0, keepdims=True))
            p = jnp.exp2((s - m_new) * EXP2)
            alpha = jnp.exp2((m - m_new) * EXP2)
            l = l * alpha + jnp.sum(p, axis=0, keepdims=True)
            vt = vt_s[:, pl.ds(pl.multiple_of(t * KT, KT), KT)]
            acc = acc * alpha + dot(vt, p.astype(BF16), ((1,), (0,)))
            return m_new, l, acc

        m0 = jnp.full((1, QB), LOW, F32)
        l0 = jnp.zeros((1, QB), F32)
        m, l, acc = lax.fori_loop(begin, end, per_tile, (m0, l0, jnp.zeros((HD, QB), F32)))
        out_ref[i] = (acc / l).T.astype(BF16)
        return 0

    lax.fori_loop(0, total // QB, per_block, 0)


def attention_forward(packed):
    blocks = packed.shape[0]
    total = blocks * 128
    return pl.pallas_call(
        forward_kernel,
        out_shape=jax.ShapeDtypeStruct((total // QB, QB, HD), BF16),
        in_specs=whole(1),
        out_specs=whole(1)[0],
        scratch_shapes=[pltpu.VMEM((HD, total), BF16), pltpu.VMEM((total, HD), F32)],
        compiler_params=params(24),
        cost_estimate=cost(4 * total * total * HD, 4 * total * HD * 2),
        name="attention_forward",
    )(packed)


def backward_kernel(in_ref, g_ref, out_ref, kt_s, seg_s, s_s, dp_s, dk_s, dv_s):
    blocks, rows = in_ref.shape[0], 128
    total = blocks * rows
    starts = sample_starts(in_ref, rows)
    fill_samples(seg_s, starts)
    for i in range(blocks):
        kt_s[:, i * rows:(i + 1) * rows] = in_ref[i, rows:2 * rows, :].T
    dk_s[...] = jnp.zeros_like(dk_s)
    dv_s[...] = jnp.zeros_like(dv_s)

    def per_block(i, _):
        q = block_rows(in_ref, i, QB, 0, rows)
        g = g_ref[i]
        first = i * QB
        seg_q = sample_of(first + lax.broadcasted_iota(jnp.int32, (1, QB), 1), starts)
        begin, end = tile_range(first, first + QB - 1, starts, total)

        def scores(t, carry):
            m, l, d = carry
            here = pl.ds(pl.multiple_of(t * KT, KT), KT)
            s = dot(block_rows(in_ref, t, KT, rows, rows), q, ((1,), (1,)))
            dp = dot(block_rows(in_ref, t, KT, 2 * rows, rows), g, ((1,), (1,)))
            seg_k = seg_s[here, :]
            s = jnp.where(jnp.concatenate([seg_k, seg_k], axis=1) == seg_q, s, LOW)
            s_s[here, :] = s
            dp_s[here, :] = dp
            m_new = jnp.maximum(m, jnp.max(s, axis=0, keepdims=True))
            p = jnp.exp2((s - m_new) * EXP2)
            alpha = jnp.exp2((m - m_new) * EXP2)
            l = l * alpha + jnp.sum(p, axis=0, keepdims=True)
            d = d * alpha + jnp.sum(p * dp, axis=0, keepdims=True)
            return m_new, l, d

        zero = jnp.zeros((1, QB), F32)
        m, l, d = lax.fori_loop(begin, end, scores, (jnp.full((1, QB), LOW, F32), zero, zero))
        inverse = 1.0 / l
        delta = d * inverse

        def grads(t, acc):
            here = pl.ds(pl.multiple_of(t * KT, KT), KT)
            p = jnp.exp2((s_s[here, :] - m) * EXP2) * inverse
            ds = (p * (dp_s[here, :] - delta)).astype(BF16)
            dv_s[here, :] += dot(p.astype(BF16), g, ((1,), (0,)))
            dk_s[here, :] += dot(ds, q, ((1,), (0,)))
            return acc + dot(kt_s[:, here], ds, ((1,), (0,)))

        acc = lax.fori_loop(begin, end, grads, jnp.zeros((HD, QB), F32))
        dq = (acc * SCALE).T.astype(BF16)
        per = QB // rows
        out_ref[pl.ds(i * per, per), 0:rows, :] = dq.reshape(per, rows, HD)
        return 0

    lax.fori_loop(0, total // QB, per_block, 0)
    for i in range(blocks):
        here = slice(i * rows, (i + 1) * rows)
        out_ref[i, rows:2 * rows, :] = (dk_s[here, :] * SCALE).astype(BF16)
        out_ref[i, 2 * rows:3 * rows, :] = dv_s[here, :].astype(BF16)


def attention_backward(packed, grad):
    blocks = packed.shape[0]
    total = blocks * 128
    return pl.pallas_call(
        backward_kernel,
        out_shape=jax.ShapeDtypeStruct((blocks, 3 * 128, HD), BF16),
        in_specs=whole(2),
        out_specs=whole(1)[0],
        scratch_shapes=[
            pltpu.VMEM((HD, total), BF16),
            pltpu.VMEM((total, HD), F32),
            pltpu.VMEM((total, QB), F32),
            pltpu.VMEM((total, QB), F32),
            pltpu.VMEM((total, HD), F32),
            pltpu.VMEM((total, HD), F32),
        ],
        compiler_params=params(32),
        cost_estimate=cost(10 * total * total * HD, 7 * total * HD * 2),
        name="attention_backward",
    )(packed, grad)


def grad_kernel(place_ref, own_ref, other_ref, *refs):
    pieces, out_ref, g_s = refs[:CHIPS], refs[CHIPS], refs[CHIPS + 1]
    rows = own_ref.shape[0]
    core = place_ref[CHIPS]
    g_s[pl.ds(pl.multiple_of(core * rows, rows), rows), :] = own_ref[...]
    g_s[pl.ds(pl.multiple_of((1 - core) * rows, rows), rows), :] = other_ref[...]
    for j in range(0, CHIPS, 2):
        w = jnp.concatenate([pieces[j][...], pieces[j + 1][...]], axis=0)
        r = dot(g_s[...], w, ((1,), (1,))).astype(BF16)
        out_ref[place_ref[j]] = r[:, :HD]
        out_ref[place_ref[j + 1]] = r[:, HD:]


def attention_grad(place, own, other, pieces):
    rows, width = own.shape
    return pl.pallas_call(
        grad_kernel,
        out_shape=jax.ShapeDtypeStruct((CHIPS, 2 * rows, HD), BF16),
        in_specs=[pl.BlockSpec(memory_space=pltpu.SMEM)] + whole(2 + CHIPS),
        out_specs=whole(1)[0],
        scratch_shapes=[pltpu.VMEM((2 * rows, width), BF16)],
        compiler_params=params(32),
        cost_estimate=cost(4 * rows * width * HD * CHIPS, CHIPS * HD * width * 2),
        name="attention_grad",
    )(place, own, other, *pieces)


def project_kernel(place_ref, attn_ref, *refs):
    pieces, own_ref, other_ref, a_s = refs[:CHIPS], refs[CHIPS], refs[CHIPS + 1], refs[CHIPS + 2]
    rows, width = own_ref.shape
    core = place_ref[CHIPS]
    for half, at in ((0, core), (1, 1 - core)):
        src = pl.ds(pl.multiple_of(at * rows, rows), rows)
        for j in range(CHIPS):
            a_s[half * rows:(half + 1) * rows, j * HD:(j + 1) * HD] = attn_ref[place_ref[j], src, :]
    step = 512
    for n in range(0, width, step):
        acc = None
        for j in range(0, CHIPS, 2):
            w = jnp.concatenate([pieces[j][:, n:n + step], pieces[j + 1][:, n:n + step]], axis=0)
            r = dot(a_s[:, j * HD:(j + 2) * HD], w, ((1,), (0,)))
            acc = r if acc is None else acc + r
        own_ref[:, n:n + step] = acc[:rows]
        other_ref[:, n:n + step] = acc[rows:].astype(other_ref.dtype)


def project(place, attn, pieces):
    rows, width = pieces[0].shape
    return pl.pallas_call(
        project_kernel,
        out_shape=(
            jax.ShapeDtypeStruct((rows, width), F32),
            jax.ShapeDtypeStruct((rows, width), F32),
        ),
        in_specs=[pl.BlockSpec(memory_space=pltpu.SMEM)] + whole(1 + CHIPS),
        out_specs=tuple(whole(2)),
        scratch_shapes=[pltpu.VMEM((2 * rows, CHIPS * HD), BF16)],
        compiler_params=params(32),
        cost_estimate=cost(4 * rows * width * HD * CHIPS, CHIPS * HD * width * 2),
        name="project",
    )(place, attn, *pieces)


def unpack_kernel(in_ref, out_ref):
    rows = out_ref.shape[1]
    for h in range(in_ref.shape[0]):
        for t in range(3):
            out_ref[t, :, h * HD:(h + 1) * HD] = in_ref[h, t * rows:(t + 1) * rows, :]


def unpack(received):
    heads, rows = received.shape[0], received.shape[1] // 3
    return pl.pallas_call(
        unpack_kernel,
        out_shape=jax.ShapeDtypeStruct((3, rows, heads * HD), BF16),
        in_specs=whole(1),
        out_specs=whole(1)[0],
        compiler_params=params(24),
        cost_estimate=cost(0, 12 * rows * heads * HD),
        name="unpack",
    )(received)


def shifted(array, axis, by):
    length = lax.axis_size(axis)
    pairs = [(i, i + by) for i in range(length) if 0 <= i + by < length]
    return lax.ppermute(array, axis, pairs)


def per_sample(seg, table):
    onehot = (seg[:, None] == jnp.arange(table.shape[0], dtype=jnp.int32)[None, :]).astype(F32)
    return jnp.sum(onehot[:, :, None] * table[None, :, :], axis=1)


def exchange(array):
    return lax.all_to_all(array, "seq", 0, 0, tiled=True)


def exchange_same_core(array):
    return lax.all_to_all(array, "seq", 0, 0, tiled=True, axis_index_groups=SAME_CORE)


def body(hidden_in, queries, keys, values, segments, gates, out_weight, upstream, fresh, loss_grad):
    section = lax.axis_index("pipe")
    last_section = lax.axis_size("pipe") - 1
    position = lax.axis_index("seq")
    x, y, core = position // 4, (position // 2) % 2, position % 2

    own = out_weight[0]
    y_own = lax.ppermute(own, "seq", YSWAP)
    left = lax.ppermute(own, "seq", XUP)
    right = lax.ppermute(own, "seq", XDOWN)
    y_left = lax.ppermute(y_own, "seq", XUP)
    y_right = lax.ppermute(y_own, "seq", XDOWN)
    far = lax.ppermute(left, "seq", XUP)
    y_far = lax.ppermute(y_right, "seq", XDOWN)
    pieces = (own, y_own, left, y_left, right, y_right, far, y_far)
    offsets = ((0, 0), (0, 1), (3, 0), (3, 1), (1, 0), (1, 1), (2, 0), (2, 1))
    place = jnp.stack([((x + dx) % 4) * 2 + (y + dy) % 2 for dx, dy in offsets] + [core])

    local_seg = segments[0]
    g_scaled = (per_sample(local_seg[1], gates[0, 1]) * upstream[0].astype(F32)).astype(BF16)
    g_other = lax.ppermute(g_scaled, "seq", CORE)

    fwd = exchange(pack(queries, keys, values, segments, 0))
    bwd = exchange(pack(queries, keys, values, segments, 1))

    attn = exchange_same_core(attention_forward(fwd))
    g_heads = exchange_same_core(attention_grad(place, g_scaled, g_other, pieces))

    part, part_other = project(place, attn, pieces)
    proj = part + lax.ppermute(part_other, "seq", CORE)
    section_out = (
        hidden_in[0].astype(F32) + per_sample(local_seg[0], gates[0, 0]) * proj
    ).astype(BF16)
    moved = shifted(section_out, "pipe", 1)
    next_act = jnp.where(section == 0, fresh, moved)[None]

    qkv_grads = unpack(exchange(attention_backward(bwd, g_heads)))[None]
    moved_grad = shifted(upstream[0], "pipe", -1)
    next_grad = jnp.where(section == last_section, loss_grad, moved_grad)[None]
    return (next_act, next_grad, qkv_grads)


def solution(mesh):
    in_specs = (
        P("pipe", "seq", None),
        P("pipe", None, "seq", None),
        P("pipe", None, "seq", None),
        P("pipe", None, "seq", None),
        P("pipe", None, "seq"),
        P("pipe", None, None, None),
        P("pipe", "seq", None),
        P("pipe", "seq", None),
        P("seq", None),
        P("seq", None),
    )
    out_specs = (P("pipe", "seq", None), P("pipe", "seq", None), P("pipe", None, "seq", None))
    return jax.shard_map(body, mesh=mesh, in_specs=in_specs, out_specs=out_specs, check_vma=False)
```

```python
import functools

import jax
import jax.numpy as jnp
from jax import lax
from jax.experimental import pallas as pl
from jax.experimental.pallas import tpu as pltpu
from jax.sharding import PartitionSpec as P

HD = 128
SCALE = HD ** (-0.5)
EXP2 = SCALE * 1.4426950408889634
LOW = -1e30
QB = 256
KT = 512
SEG_ROWS = 16
F32 = jnp.float32
BF16 = jnp.bfloat16

XN, YN = 4, 2
CHIPS = XN * YN
SAME_CORE = [[2 * i + c for i in range(CHIPS)] for c in range(2)]
CORE = [(i, i ^ 1) for i in range(2 * CHIPS)]
YSWAP = [(i, i ^ 2) for i in range(2 * CHIPS)]
XUP = [(i, (i + 4) % 16) for i in range(2 * CHIPS)]
XDOWN = [(i, (i - 4) % 16) for i in range(2 * CHIPS)]


def params(mib):
    return pltpu.CompilerParams(vmem_limit_bytes=mib * 1024 * 1024)


def whole(count):
    return [pl.BlockSpec(memory_space=pltpu.VMEM)] * count


def anywhere(arrays):
    return [pl.BlockSpec(memory_space=pl.ANY)] * len(arrays)


def cost(microseconds):
    return pl.CostEstimate(
        flops=int(microseconds * 1e9), bytes_accessed=0, transcendentals=0
    )


def dot(a, b, dims):
    return lax.dot_general(a, b, (dims, ((), ())), preferred_element_type=F32)


def pack_kernel(seg_ref, q_ref, k_ref, v_ref, *refs):
    out_ref = refs[-1]
    rows = q_ref.shape[0]
    for h in range(out_ref.shape[0]):
        cols = slice(h * HD, (h + 1) * HD)
        out_ref[h, 0:rows, :] = q_ref[:, cols]
        out_ref[h, rows:2 * rows, :] = k_ref[:, cols]
        out_ref[h, 2 * rows:3 * rows, :] = v_ref[:, cols]
        out_ref[h, 3 * rows:, :] = jnp.broadcast_to(
            seg_ref[...].astype(F32), (SEG_ROWS, HD)
        ).astype(BF16)


def pack(queries, keys, values, segments, batch, *later):
    rows, width = queries.shape[2], queries.shape[3]
    heads = width // HD
    block = pl.BlockSpec((None, None, rows, width), lambda i: (0, batch, 0, 0))
    return pl.pallas_call(
        pack_kernel,
        grid=(1,),
        out_shape=jax.ShapeDtypeStruct((heads, 3 * rows + SEG_ROWS, HD), BF16),
        in_specs=[pl.BlockSpec((1, rows), lambda i: (0, 0)), block, block, block] + anywhere(later),
        out_specs=pl.BlockSpec((heads, 3 * rows + SEG_ROWS, HD), lambda i: (0, 0, 0)),
        compiler_params=params(24),
        cost_estimate=cost(2),
        name="pack",
    )(segments[0, batch][None], queries, keys, values, *later)


def sample_starts(in_ref, rows):
    ids = in_ref[:, 3 * rows:, :].astype(F32)
    return [
        jnp.sum(jnp.where(ids < s, 1.0, 0.0)).astype(jnp.int32) // SEG_ROWS for s in (1, 2, 3)
    ]


def sample_of(position, starts):
    return sum(jnp.where(position >= b, 1.0, 0.0) for b in starts)


def tile_range(first, last, starts, total):
    low, high = 0, total
    for b in starts:
        low = jnp.maximum(low, jnp.where(b <= first, b, 0))
        high = jnp.minimum(high, jnp.where(b > last, b, total))
    return low // KT, (high + KT - 1) // KT


def block_rows(ref, index, count, start, rows):
    per = count // rows
    return ref[pl.ds(index * per, per), start:start + rows, :].reshape(count, HD)


def fill_samples(seg_s, starts):
    total = seg_s.shape[0]
    for i in range(total // 256):
        position = i * 256 + lax.broadcasted_iota(jnp.int32, (256, HD), 0)
        seg_s[i * 256:(i + 1) * 256, :] = sample_of(position, starts)


def forward_kernel(in_ref, *refs):
    out_ref, vt_s, seg_s = refs[-3:]
    blocks, rows = in_ref.shape[0], 128
    total = blocks * rows
    starts = sample_starts(in_ref, rows)
    fill_samples(seg_s, starts)
    for i in range(blocks):
        vt_s[:, i * rows:(i + 1) * rows] = in_ref[i, 2 * rows:3 * rows, :].T

    def per_block(i, _):
        q = block_rows(in_ref, i, QB, 0, rows)
        first = i * QB
        seg_q = sample_of(first + lax.broadcasted_iota(jnp.int32, (1, QB), 1), starts)
        begin, end = tile_range(first, first + QB - 1, starts, total)

        def per_tile(t, carry):
            m, l, acc = carry
            k = block_rows(in_ref, t, KT, rows, rows)
            s = dot(k, q, ((1,), (1,)))
            seg_k = seg_s[pl.ds(pl.multiple_of(t * KT, KT), KT), :]
            s = jnp.where(jnp.concatenate([seg_k, seg_k], axis=1) == seg_q, s, LOW)
            m_new = jnp.maximum(m, jnp.max(s, axis=0, keepdims=True))
            p = jnp.exp2((s - m_new) * EXP2)
            alpha = jnp.exp2((m - m_new) * EXP2)
            l = l * alpha + jnp.sum(p, axis=0, keepdims=True)
            vt = vt_s[:, pl.ds(pl.multiple_of(t * KT, KT), KT)]
            acc = acc * alpha + dot(vt, p.astype(BF16), ((1,), (0,)))
            return m_new, l, acc

        m0 = jnp.full((1, QB), LOW, F32)
        l0 = jnp.zeros((1, QB), F32)
        m, l, acc = lax.fori_loop(begin, end, per_tile, (m0, l0, jnp.zeros((HD, QB), F32)))
        out_ref[i] = (acc / l).T.astype(BF16)
        return 0

    lax.fori_loop(0, total // QB, per_block, 0)


def attention_forward(packed, *later):
    blocks = packed.shape[0]
    total = blocks * 128
    return pl.pallas_call(
        forward_kernel,
        out_shape=jax.ShapeDtypeStruct((total // QB, QB, HD), BF16),
        in_specs=whole(1) + anywhere(later),
        out_specs=whole(1)[0],
        scratch_shapes=[pltpu.VMEM((HD, total), BF16), pltpu.VMEM((total, HD), F32)],
        compiler_params=params(24),
        cost_estimate=cost(0.2),
        name="attention_forward",
    )(packed, *later)


OFFSETS = ((0, 0), (0, 1), (3, 0), (1, 0), (3, 1), (1, 1), (2, 0), (2, 1))


def chip_at(position, offset):
    x, y = position // 4, (position // 2) % 2
    return ((x + offset[0]) % XN) * YN + (y + offset[1]) % YN


def backward_kernel(place_ref, in_ref, *refs):
    g_refs, (out_ref, g_ref, kt_s, seg_s, s_s, dp_s, dk_s, dv_s) = refs[:CHIPS], refs[-8:]
    blocks, rows = in_ref.shape[0], 128
    for offset, ref in zip(OFFSETS, g_refs):
        g_ref[chip_at(place_ref[0], (-offset[0] % XN, offset[1]))] = ref[...]
    total = blocks * rows
    starts = sample_starts(in_ref, rows)
    fill_samples(seg_s, starts)
    for i in range(blocks):
        kt_s[:, i * rows:(i + 1) * rows] = in_ref[i, rows:2 * rows, :].T
    dk_s[...] = jnp.zeros_like(dk_s)
    dv_s[...] = jnp.zeros_like(dv_s)

    def per_block(i, _):
        q = block_rows(in_ref, i, QB, 0, rows)
        g = g_ref[i]
        first = i * QB
        seg_q = sample_of(first + lax.broadcasted_iota(jnp.int32, (1, QB), 1), starts)
        begin, end = tile_range(first, first + QB - 1, starts, total)

        def scores(t, carry):
            m, l, d = carry
            here = pl.ds(pl.multiple_of(t * KT, KT), KT)
            s = dot(block_rows(in_ref, t, KT, rows, rows), q, ((1,), (1,)))
            dp = dot(block_rows(in_ref, t, KT, 2 * rows, rows), g, ((1,), (1,)))
            seg_k = seg_s[here, :]
            s = jnp.where(jnp.concatenate([seg_k, seg_k], axis=1) == seg_q, s, LOW)
            s_s[here, :] = s
            dp_s[here, :] = dp
            m_new = jnp.maximum(m, jnp.max(s, axis=0, keepdims=True))
            p = jnp.exp2((s - m_new) * EXP2)
            alpha = jnp.exp2((m - m_new) * EXP2)
            l = l * alpha + jnp.sum(p, axis=0, keepdims=True)
            d = d * alpha + jnp.sum(p * dp, axis=0, keepdims=True)
            return m_new, l, d

        zero = jnp.zeros((1, QB), F32)
        m, l, d = lax.fori_loop(begin, end, scores, (jnp.full((1, QB), LOW, F32), zero, zero))
        inverse = 1.0 / l
        delta = d * inverse

        def grads(t, acc):
            here = pl.ds(pl.multiple_of(t * KT, KT), KT)
            p = jnp.exp2((s_s[here, :] - m) * EXP2) * inverse
            ds = (p * (dp_s[here, :] - delta)).astype(BF16)
            dv_s[here, :] += dot(p.astype(BF16), g, ((1,), (0,)))
            dk_s[here, :] += dot(ds, q, ((1,), (0,)))
            return acc + dot(kt_s[:, here], ds, ((1,), (0,)))

        acc = lax.fori_loop(begin, end, grads, jnp.zeros((HD, QB), F32))
        dq = (acc * SCALE).T.astype(BF16)
        per = QB // rows
        out_ref[pl.ds(i * per, per), 0:rows, :] = dq.reshape(per, rows, HD)
        return 0

    lax.fori_loop(0, total // QB, per_block, 0)
    for i in range(blocks):
        here = slice(i * rows, (i + 1) * rows)
        out_ref[i, rows:2 * rows, :] = (dk_s[here, :] * SCALE).astype(BF16)
        out_ref[i, 2 * rows:3 * rows, :] = dv_s[here, :].astype(BF16)


def attention_backward(place, packed, grads, *later):
    blocks = packed.shape[0]
    total = blocks * 128
    return pl.pallas_call(
        backward_kernel,
        out_shape=jax.ShapeDtypeStruct((blocks, 3 * 128, HD), BF16),
        in_specs=[pl.BlockSpec(memory_space=pltpu.SMEM)] + whole(1 + CHIPS) + anywhere(later),
        out_specs=whole(1)[0],
        scratch_shapes=[
            pltpu.VMEM((total // QB, QB, HD), BF16),
            pltpu.VMEM((HD, total), BF16),
            pltpu.VMEM((total, HD), F32),
            pltpu.VMEM((total, QB), F32),
            pltpu.VMEM((total, QB), F32),
            pltpu.VMEM((total, HD), F32),
            pltpu.VMEM((total, HD), F32),
        ],
        compiler_params=params(32),
        cost_estimate=cost(30),
        name="attention_backward",
    )(place, packed, *grads, *later)


def grad_kernel(count, place_ref, own_ref, other_ref, *refs):
    pieces, outs, g_s = refs[:count], refs[-1 - count:-1], refs[-1]
    rows = own_ref.shape[0]
    core = place_ref[0] % 2
    g_s[pl.ds(pl.multiple_of(core * rows, rows), rows), :] = own_ref[...]
    g_s[pl.ds(pl.multiple_of((1 - core) * rows, rows), rows), :] = other_ref[...]
    for j in range(0, count, 2):
        w = jnp.concatenate([pieces[j][...], pieces[j + 1][...]], axis=0)
        r = dot(g_s[...], w, ((1,), (1,))).astype(BF16)
        outs[j][...] = r[:, :HD]
        outs[j + 1][...] = r[:, HD:]


def attention_grad(place, own, other, pieces, *later):
    rows, width = own.shape
    count = len(pieces)
    return pl.pallas_call(
        functools.partial(grad_kernel, count),
        out_shape=(jax.ShapeDtypeStruct((2 * rows, HD), BF16),) * count,
        in_specs=[pl.BlockSpec(memory_space=pltpu.SMEM)] + whole(2 + count) + anywhere(later),
        out_specs=tuple(whole(count)),
        scratch_shapes=[pltpu.VMEM((2 * rows, width), BF16)],
        compiler_params=params(32),
        cost_estimate=cost(0.2),
        name="attention_grad",
    )(place, own, other, *pieces, *later)


def project_kernel(place_ref, attn_ref, *refs):
    pieces, (own_ref, other_ref, a_s) = refs[:CHIPS], refs[-3:]
    rows, width = own_ref.shape
    core = place_ref[0] % 2
    for half, at in ((0, core), (1, 1 - core)):
        src = pl.ds(pl.multiple_of(at * rows, rows), rows)
        for j in range(CHIPS):
            a_s[half * rows:(half + 1) * rows, j * HD:(j + 1) * HD] = attn_ref[chip_at(place_ref[0], OFFSETS[j]), src, :]
    step = 512
    for n in range(0, width, step):
        acc = None
        for j in range(0, CHIPS, 2):
            w = jnp.concatenate([pieces[j][:, n:n + step], pieces[j + 1][:, n:n + step]], axis=0)
            r = dot(a_s[:, j * HD:(j + 2) * HD], w, ((1,), (0,)))
            acc = r if acc is None else acc + r
        own_ref[:, n:n + step] = acc[:rows]
        other_ref[:, n:n + step] = acc[rows:].astype(other_ref.dtype)


def project(place, attn, pieces, *later):
    rows, width = pieces[0].shape
    return pl.pallas_call(
        project_kernel,
        out_shape=(
            jax.ShapeDtypeStruct((rows, width), F32),
            jax.ShapeDtypeStruct((rows, width), F32),
        ),
        in_specs=[pl.BlockSpec(memory_space=pltpu.SMEM)] + whole(1 + CHIPS) + anywhere(later),
        out_specs=tuple(whole(2)),
        scratch_shapes=[pltpu.VMEM((2 * rows, CHIPS * HD), BF16)],
        compiler_params=params(32),
        cost_estimate=cost(0.2),
        name="project",
    )(place, attn, *pieces, *later)


def unpack_kernel(in_ref, out_ref):
    rows = out_ref.shape[1]
    for h in range(in_ref.shape[0]):
        for t in range(3):
            out_ref[t, :, h * HD:(h + 1) * HD] = in_ref[h, t * rows:(t + 1) * rows, :]


def unpack(received):
    heads, rows = received.shape[0], received.shape[1] // 3
    return pl.pallas_call(
        unpack_kernel,
        out_shape=jax.ShapeDtypeStruct((3, rows, heads * HD), BF16),
        in_specs=whole(1),
        out_specs=whole(1)[0],
        compiler_params=params(24),
        cost_estimate=cost(2),
        name="unpack",
    )(received)


def choose_kernel(section_ref, first_ref, second_ref, *refs):
    out_ref = refs[-1]
    out_ref[...] = jnp.where(section_ref[0] == section_ref[1], first_ref[...], second_ref[...])


def choose(sections, first, second, *later):
    return pl.pallas_call(
        choose_kernel,
        out_shape=jax.ShapeDtypeStruct(first.shape, first.dtype),
        in_specs=[pl.BlockSpec(memory_space=pltpu.SMEM)] + whole(2) + anywhere(later),
        out_specs=whole(1)[0],
        compiler_params=params(16),
        cost_estimate=cost(2),
        name="choose",
    )(sections, first, second, *later)


def rotated(array, axis, by):
    length = lax.axis_size(axis)
    return lax.ppermute(array, axis, [(i, (i + by) % length) for i in range(length)])


def per_sample(seg, table):
    onehot = (seg[:, None] == jnp.arange(table.shape[0], dtype=jnp.int32)[None, :]).astype(F32)
    return jnp.sum(onehot[:, :, None] * table[None, :, :], axis=1)


def to_chip(array, offset):
    if offset == (0, 0):
        return array
    pairs = [(i, 2 * chip_at(i, offset) + i % 2) for i in range(2 * CHIPS)]
    return lax.ppermute(array, "seq", pairs)


def exchange(array):
    return lax.all_to_all(array, "seq", 0, 0, tiled=True)


def exchange_same_core(array):
    return lax.all_to_all(array, "seq", 0, 0, tiled=True, axis_index_groups=SAME_CORE)


def body(hidden_in, queries, keys, values, segments, gates, out_weight, upstream, fresh, loss_grad):
    section = lax.axis_index("pipe")
    last_section = lax.axis_size("pipe") - 1
    place = lax.axis_index("seq")[None]

    own = out_weight[0]
    y_own = lax.ppermute(own, "seq", YSWAP)
    left = lax.ppermute(own, "seq", XUP)
    right = lax.ppermute(own, "seq", XDOWN)
    y_left = lax.ppermute(y_own, "seq", XUP)
    y_right = lax.ppermute(y_own, "seq", XDOWN)
    far = lax.ppermute(left, "seq", XUP)
    y_far = lax.ppermute(y_right, "seq", XDOWN)
    pieces = (own, y_own, left, right, y_left, y_right, far, y_far)

    local_seg = segments[0]
    g_scaled = (per_sample(local_seg[1], gates[0, 1]) * upstream[0].astype(F32)).astype(BF16)
    g_other = lax.ppermute(g_scaled, "seq", CORE)

    gate_tok = per_sample(local_seg[0], gates[0, 0])
    fwd = exchange(pack(queries, keys, values, segments, 0))
    packed = pack(queries, keys, values, segments, 1, fwd, right)
    bwd = exchange(packed)

    sections = jnp.stack([section, jnp.zeros_like(section)])
    turned = choose(sections, loss_grad, upstream[0], y_own)
    next_grad = rotated(turned, "pipe", -1)

    attn = exchange_same_core(attention_forward(fwd, packed, turned, gate_tok))
    near = attention_grad(place, g_scaled, g_other, pieces[:4])
    near = tuple(to_chip(g, o) for g, o in zip(near, OFFSETS[:4]))
    distant = attention_grad(place, g_scaled, g_other, pieces[4:], bwd, *near)
    distant = tuple(to_chip(g, o) for g, o in zip(distant, OFFSETS[4:]))
    part, part_other = project(place, attn, pieces, distant[0], next_grad)
    grads = attention_backward(place, bwd, near + distant)
    proj = part + lax.ppermute(part_other, "seq", CORE)
    section_out = (hidden_in[0].astype(F32) + gate_tok * proj).astype(BF16)
    next_act = rotated(jnp.where(section == last_section, fresh, section_out), "pipe", 1)[None]

    qkv_grads = unpack(exchange(grads))[None]
    return (next_act, next_grad[None], qkv_grads)


def solution(mesh):
    in_specs = (
        P("pipe", "seq", None),
        P("pipe", None, "seq", None),
        P("pipe", None, "seq", None),
        P("pipe", None, "seq", None),
        P("pipe", None, "seq"),
        P("pipe", None, None, None),
        P("pipe", "seq", None),
        P("pipe", "seq", None),
        P("seq", None),
        P("seq", None),
    )
    out_specs = (P("pipe", "seq", None), P("pipe", "seq", None), P("pipe", None, "seq", None))
    return jax.shard_map(body, mesh=mesh, in_specs=in_specs, out_specs=out_specs, check_vma=False)
```

```python
import functools

import jax
import jax.numpy as jnp
from jax import lax
from jax.experimental import pallas as pl
from jax.experimental.pallas import tpu as pltpu
from jax.sharding import PartitionSpec as P

HD = 128
SCALE = HD ** (-0.5)
EXP2 = SCALE * 1.4426950408889634
LOW = -1e30
QB = 256
KT = 512
SEG_ROWS = 16
F32 = jnp.float32
BF16 = jnp.bfloat16

XN, YN = 4, 2
CHIPS = XN * YN
SAME_CORE = [[2 * i + c for i in range(CHIPS)] for c in range(2)]
CORE = [(i, i ^ 1) for i in range(2 * CHIPS)]
YSWAP = [(i, i ^ 2) for i in range(2 * CHIPS)]
XUP = [(i, (i + 4) % 16) for i in range(2 * CHIPS)]
XDOWN = [(i, (i - 4) % 16) for i in range(2 * CHIPS)]


def params(mib):
    return pltpu.CompilerParams(vmem_limit_bytes=mib * 1024 * 1024)


def whole(count):
    return [pl.BlockSpec(memory_space=pltpu.VMEM)] * count


def anywhere(arrays):
    return [pl.BlockSpec(memory_space=pl.ANY)] * len(arrays)


def in_hbm(count):
    return [pl.BlockSpec(memory_space=pltpu.HBM)] * count


def batch_rows(packed, batch):
    heads, height = packed.shape[0], packed.shape[1] // 2
    return pl.BlockSpec((heads, height, HD), lambda i: (0, batch, 0))


def cost(microseconds):
    return pl.CostEstimate(
        flops=int(microseconds * 1e9), bytes_accessed=0, transcendentals=0
    )


def dot(a, b, dims):
    return lax.dot_general(a, b, (dims, ((), ())), preferred_element_type=F32)


def pack_kernel(seg_ref, q_ref, k_ref, v_ref, out_ref, ids_s, sems):
    batches, rows = q_ref.shape[1], q_ref.shape[2]
    heads = out_ref.shape[0]
    height = 3 * rows + SEG_ROWS
    for b in range(batches):
        ids = jnp.broadcast_to(seg_ref[b:b + 1, :].astype(F32), (SEG_ROWS, HD)).astype(BF16)
        for h in range(heads):
            ids_s[b, h] = ids
    for b in range(batches):
        for a, ref in enumerate((q_ref, k_ref, v_ref)):
            for h in range(heads):
                pltpu.make_async_copy(
                    ref.at[0, b, :, h * HD:(h + 1) * HD],
                    out_ref.at[h, b * height + a * rows:b * height + (a + 1) * rows, :],
                    sems.at[b * 4 + a],
                ).start()
        pltpu.make_async_copy(
            ids_s.at[b],
            out_ref.at[:, b * height + 3 * rows:(b + 1) * height, :],
            sems.at[b * 4 + 3],
        ).start()
    for b in range(batches):
        for a in range(3):
            done = out_ref.at[:, b * height + a * rows:b * height + (a + 1) * rows, :]
            pltpu.make_async_copy(done, done, sems.at[b * 4 + a]).wait()
        done = out_ref.at[:, b * height + 3 * rows:(b + 1) * height, :]
        pltpu.make_async_copy(ids_s.at[b], done, sems.at[b * 4 + 3]).wait()


def pack(queries, keys, values, segments):
    batches, rows, width = queries.shape[1:]
    heads = width // HD
    height = 3 * rows + SEG_ROWS
    return pl.pallas_call(
        pack_kernel,
        out_shape=jax.ShapeDtypeStruct((heads, batches * height, HD), BF16),
        in_specs=whole(1) + in_hbm(3),
        out_specs=in_hbm(1)[0],
        scratch_shapes=[
            pltpu.VMEM((batches, heads, SEG_ROWS, HD), BF16),
            pltpu.SemaphoreType.DMA((4 * batches,)),
        ],
        compiler_params=params(60),
        cost_estimate=cost(2),
        name="pack",
    )(segments[0], queries, keys, values)


def follow_kernel(array_ref, *refs):
    pass


def follow(array, *later):
    return pl.pallas_call(
        follow_kernel,
        out_shape=jax.ShapeDtypeStruct(array.shape, array.dtype),
        in_specs=anywhere((array,) + later),
        out_specs=pl.BlockSpec(memory_space=pl.ANY),
        input_output_aliases={0: 0},
        compiler_params=params(1),
        cost_estimate=cost(0.01),
        name="follow",
    )(array, *later)


def sample_starts(in_ref, rows):
    ids = in_ref[:, 3 * rows:, :].astype(F32)
    return [
        jnp.sum(jnp.where(ids < s, 1.0, 0.0)).astype(jnp.int32) // SEG_ROWS for s in (1, 2, 3)
    ]


def sample_of(position, starts):
    return sum(jnp.where(position >= b, 1.0, 0.0) for b in starts)


def tile_range(first, last, starts, total):
    low, high = 0, total
    for b in starts:
        low = jnp.maximum(low, jnp.where(b <= first, b, 0))
        high = jnp.minimum(high, jnp.where(b > last, b, total))
    return low // KT, (high + KT - 1) // KT


def block_rows(ref, index, count, start, rows):
    per = count // rows
    return ref[pl.ds(index * per, per), start:start + rows, :].reshape(count, HD)


def fill_samples(seg_s, starts):
    total = seg_s.shape[0]
    for i in range(total // 256):
        position = i * 256 + lax.broadcasted_iota(jnp.int32, (256, HD), 0)
        seg_s[i * 256:(i + 1) * 256, :] = sample_of(position, starts)


def forward_kernel(in_ref, *refs):
    out_ref, vt_s, seg_s = refs[-3:]
    blocks, rows = in_ref.shape[0], 128
    total = blocks * rows
    starts = sample_starts(in_ref, rows)
    fill_samples(seg_s, starts)
    for i in range(blocks):
        vt_s[:, i * rows:(i + 1) * rows] = in_ref[i, 2 * rows:3 * rows, :].T

    def per_block(i, _):
        q = block_rows(in_ref, i, QB, 0, rows)
        first = i * QB
        seg_q = sample_of(first + lax.broadcasted_iota(jnp.int32, (1, QB), 1), starts)
        begin, end = tile_range(first, first + QB - 1, starts, total)

        def per_tile(t, carry):
            m, l, acc = carry
            k = block_rows(in_ref, t, KT, rows, rows)
            s = dot(k, q, ((1,), (1,)))
            seg_k = seg_s[pl.ds(pl.multiple_of(t * KT, KT), KT), :]
            s = jnp.where(jnp.concatenate([seg_k, seg_k], axis=1) == seg_q, s, LOW)
            m_new = jnp.maximum(m, jnp.max(s, axis=0, keepdims=True))
            p = jnp.exp2((s - m_new) * EXP2)
            alpha = jnp.exp2((m - m_new) * EXP2)
            l = l * alpha + jnp.sum(p, axis=0, keepdims=True)
            vt = vt_s[:, pl.ds(pl.multiple_of(t * KT, KT), KT)]
            acc = acc * alpha + dot(vt, p.astype(BF16), ((1,), (0,)))
            return m_new, l, acc

        m0 = jnp.full((1, QB), LOW, F32)
        l0 = jnp.zeros((1, QB), F32)
        m, l, acc = lax.fori_loop(begin, end, per_tile, (m0, l0, jnp.zeros((HD, QB), F32)))
        out_ref[i] = (acc / l).T.astype(BF16)
        return 0

    lax.fori_loop(0, total // QB, per_block, 0)


def attention_forward(packed, *later):
    blocks = packed.shape[0]
    total = blocks * 128
    return pl.pallas_call(
        forward_kernel,
        out_shape=jax.ShapeDtypeStruct((total // QB, QB, HD), BF16),
        grid=(1,),
        in_specs=[batch_rows(packed, 0)] + anywhere(later),
        out_specs=whole(1)[0],
        scratch_shapes=[pltpu.VMEM((HD, total), BF16), pltpu.VMEM((total, HD), F32)],
        compiler_params=params(24),
        cost_estimate=cost(0.2),
        name="attention_forward",
    )(packed, *later)


OFFSETS = ((0, 0), (0, 1), (3, 0), (1, 0), (3, 1), (1, 1), (2, 0), (2, 1))


def chip_at(position, offset):
    x, y = position // 4, (position // 2) % 2
    return ((x + offset[0]) % XN) * YN + (y + offset[1]) % YN


def backward_kernel(place_ref, in_ref, *refs):
    g_refs = refs[:CHIPS]
    out_ref, g_ref, out_s, kt_s, seg_s, s_s, dp_s, dk_s, dv_s, in_sems, out_sem = refs[-11:]
    blocks, rows = in_ref.shape[0], 128
    arriving = []
    for n, (offset, ref) in enumerate(zip(OFFSETS, g_refs)):
        chip = chip_at(place_ref[0], (-offset[0] % XN, offset[1]))
        arriving.append(pltpu.make_async_copy(ref, g_ref.at[chip], in_sems.at[n]))
        arriving[-1].start()
    total = blocks * rows
    starts = sample_starts(in_ref, rows)
    fill_samples(seg_s, starts)
    for i in range(blocks):
        kt_s[:, i * rows:(i + 1) * rows] = in_ref[i, rows:2 * rows, :].T
    dk_s[...] = jnp.zeros_like(dk_s)
    dv_s[...] = jnp.zeros_like(dv_s)
    for copy in arriving:
        copy.wait()

    def per_block(i, _):
        q = block_rows(in_ref, i, QB, 0, rows)
        g = g_ref[i]
        first = i * QB
        seg_q = sample_of(first + lax.broadcasted_iota(jnp.int32, (1, QB), 1), starts)
        begin, end = tile_range(first, first + QB - 1, starts, total)

        def scores(t, carry):
            m, l, d = carry
            here = pl.ds(pl.multiple_of(t * KT, KT), KT)
            s = dot(block_rows(in_ref, t, KT, rows, rows), q, ((1,), (1,)))
            dp = dot(block_rows(in_ref, t, KT, 2 * rows, rows), g, ((1,), (1,)))
            seg_k = seg_s[here, :]
            s = jnp.where(jnp.concatenate([seg_k, seg_k], axis=1) == seg_q, s, LOW)
            s_s[here, :] = s
            dp_s[here, :] = dp
            m_new = jnp.maximum(m, jnp.max(s, axis=0, keepdims=True))
            p = jnp.exp2((s - m_new) * EXP2)
            alpha = jnp.exp2((m - m_new) * EXP2)
            l = l * alpha + jnp.sum(p, axis=0, keepdims=True)
            d = d * alpha + jnp.sum(p * dp, axis=0, keepdims=True)
            return m_new, l, d

        zero = jnp.zeros((1, QB), F32)
        m, l, d = lax.fori_loop(begin, end, scores, (jnp.full((1, QB), LOW, F32), zero, zero))
        inverse = 1.0 / l
        delta = d * inverse

        def grads(t, acc):
            here = pl.ds(pl.multiple_of(t * KT, KT), KT)
            p = jnp.exp2((s_s[here, :] - m) * EXP2) * inverse
            ds = (p * (dp_s[here, :] - delta)).astype(BF16)
            dv_s[here, :] += dot(p.astype(BF16), g, ((1,), (0,)))
            dk_s[here, :] += dot(ds, q, ((1,), (0,)))
            return acc + dot(kt_s[:, here], ds, ((1,), (0,)))

        acc = lax.fori_loop(begin, end, grads, jnp.zeros((HD, QB), F32))
        dq = (acc * SCALE).T.astype(BF16)
        per = QB // rows
        out_s[pl.ds(i * per, per), 0:rows, :] = dq.reshape(per, rows, HD)
        return 0

    lax.fori_loop(0, total // QB, per_block, 0)
    for i in range(blocks):
        here = slice(i * rows, (i + 1) * rows)
        out_s[i, rows:2 * rows, :] = (dk_s[here, :] * SCALE).astype(BF16)
        out_s[i, 2 * rows:3 * rows, :] = dv_s[here, :].astype(BF16)
        pltpu.make_async_copy(out_s.at[i], out_ref.at[i], out_sem).start()
    pltpu.make_async_copy(out_s, out_ref, out_sem).wait()


def attention_backward(place, packed, grads, *later):
    blocks = packed.shape[0]
    total = blocks * 128
    return pl.pallas_call(
        backward_kernel,
        out_shape=jax.ShapeDtypeStruct((blocks, 3 * 128, HD), BF16),
        grid=(1,),
        in_specs=[pl.BlockSpec(memory_space=pltpu.SMEM), batch_rows(packed, 1)]
        + in_hbm(CHIPS)
        + anywhere(later),
        out_specs=in_hbm(1)[0],
        scratch_shapes=[
            pltpu.VMEM((total // QB, QB, HD), BF16),
            pltpu.VMEM((blocks, 3 * 128, HD), BF16),
            pltpu.VMEM((HD, total), BF16),
            pltpu.VMEM((total, HD), F32),
            pltpu.VMEM((total, QB), F32),
            pltpu.VMEM((total, QB), F32),
            pltpu.VMEM((total, HD), F32),
            pltpu.VMEM((total, HD), F32),
            pltpu.SemaphoreType.DMA((CHIPS,)),
            pltpu.SemaphoreType.DMA,
        ],
        compiler_params=params(60),
        cost_estimate=cost(30),
        name="attention_backward",
    )(place, packed, *grads, *later)


def grad_kernel(count, place_ref, own_ref, other_ref, *refs):
    pieces, outs, g_s = refs[:count], refs[-1 - count:-1], refs[-1]
    rows = own_ref.shape[0]
    core = place_ref[0] % 2
    g_s[pl.ds(pl.multiple_of(core * rows, rows), rows), :] = own_ref[...]
    g_s[pl.ds(pl.multiple_of((1 - core) * rows, rows), rows), :] = other_ref[...]
    for j in range(0, count, 2):
        w = jnp.concatenate([pieces[j][...], pieces[j + 1][...]], axis=0)
        r = dot(g_s[...], w, ((1,), (1,))).astype(BF16)
        outs[j][...] = r[:, :HD]
        outs[j + 1][...] = r[:, HD:]


def attention_grad(place, own, other, pieces, *later):
    rows, width = own.shape
    count = len(pieces)
    return pl.pallas_call(
        functools.partial(grad_kernel, count),
        out_shape=(jax.ShapeDtypeStruct((2 * rows, HD), BF16),) * count,
        in_specs=[pl.BlockSpec(memory_space=pltpu.SMEM)] + whole(2 + count) + anywhere(later),
        out_specs=tuple(whole(count)),
        scratch_shapes=[pltpu.VMEM((2 * rows, width), BF16)],
        compiler_params=params(32),
        cost_estimate=cost(0.2),
        name="attention_grad",
    )(place, own, other, *pieces, *later)


def project_kernel(place_ref, attn_ref, *refs):
    pieces, (own_ref, other_ref, a_s) = refs[:CHIPS], refs[-3:]
    rows, width = own_ref.shape
    core = place_ref[0] % 2
    for half, at in ((0, core), (1, 1 - core)):
        src = pl.ds(pl.multiple_of(at * rows, rows), rows)
        for j in range(CHIPS):
            a_s[half * rows:(half + 1) * rows, j * HD:(j + 1) * HD] = attn_ref[chip_at(place_ref[0], OFFSETS[j]), src, :]
    step = 512
    for n in range(0, width, step):
        acc = None
        for j in range(0, CHIPS, 2):
            w = jnp.concatenate([pieces[j][:, n:n + step], pieces[j + 1][:, n:n + step]], axis=0)
            r = dot(a_s[:, j * HD:(j + 2) * HD], w, ((1,), (0,)))
            acc = r if acc is None else acc + r
        own_ref[:, n:n + step] = acc[:rows]
        other_ref[:, n:n + step] = acc[rows:].astype(other_ref.dtype)


def project(place, attn, pieces, *later):
    rows, width = pieces[0].shape
    return pl.pallas_call(
        project_kernel,
        out_shape=(
            jax.ShapeDtypeStruct((rows, width), F32),
            jax.ShapeDtypeStruct((rows, width), F32),
        ),
        in_specs=[pl.BlockSpec(memory_space=pltpu.SMEM)] + whole(1 + CHIPS) + anywhere(later),
        out_specs=tuple(whole(2)),
        scratch_shapes=[pltpu.VMEM((2 * rows, CHIPS * HD), BF16)],
        compiler_params=params(32),
        cost_estimate=cost(0.2),
        name="project",
    )(place, attn, *pieces, *later)


def unpack_kernel(in_ref, out_ref):
    rows = out_ref.shape[1]
    for h in range(in_ref.shape[0]):
        for t in range(3):
            out_ref[t, :, h * HD:(h + 1) * HD] = in_ref[h, t * rows:(t + 1) * rows, :]


def unpack(received):
    heads, rows = received.shape[0], received.shape[1] // 3
    return pl.pallas_call(
        unpack_kernel,
        out_shape=jax.ShapeDtypeStruct((3, rows, heads * HD), BF16),
        in_specs=whole(1),
        out_specs=whole(1)[0],
        compiler_params=params(24),
        cost_estimate=cost(2),
        name="unpack",
    )(received)


def choose_kernel(section_ref, first_ref, second_ref, *refs):
    out_ref = refs[-1]
    out_ref[...] = jnp.where(section_ref[0] == section_ref[1], first_ref[...], second_ref[...])


def choose(sections, first, second, *later):
    return pl.pallas_call(
        choose_kernel,
        out_shape=jax.ShapeDtypeStruct(first.shape, first.dtype),
        in_specs=[pl.BlockSpec(memory_space=pltpu.SMEM)] + whole(2) + anywhere(later),
        out_specs=whole(1)[0],
        compiler_params=params(16),
        cost_estimate=cost(2),
        name="choose",
    )(sections, first, second, *later)


def settle_kernel(in_ref, out_ref):
    out_ref[...] = in_ref[...]


def settle(array):
    return pl.pallas_call(
        settle_kernel,
        out_shape=jax.ShapeDtypeStruct(array.shape, array.dtype),
        in_specs=whole(1),
        out_specs=whole(1)[0],
        compiler_params=params(8),
        cost_estimate=cost(0.2),
        name="settle",
    )(array)


def rotated(array, axis, by):
    length = lax.axis_size(axis)
    return lax.ppermute(array, axis, [(i, (i + by) % length) for i in range(length)])


def per_sample(seg, table):
    onehot = (seg[:, None] == jnp.arange(table.shape[0], dtype=jnp.int32)[None, :]).astype(F32)
    return jnp.sum(onehot[:, :, None] * table[None, :, :], axis=1)


def to_chip(array, offset):
    if offset == (0, 0):
        return array
    pairs = [(i, 2 * chip_at(i, offset) + i % 2) for i in range(2 * CHIPS)]
    return lax.ppermute(array, "seq", pairs)


def exchange(array):
    return lax.all_to_all(array, "seq", 0, 0, tiled=True)


def exchange_same_core(array):
    return lax.all_to_all(array, "seq", 0, 0, tiled=True, axis_index_groups=SAME_CORE)


def body(hidden_in, queries, keys, values, segments, gates, out_weight, upstream, fresh, loss_grad):
    section = lax.axis_index("pipe")
    last_section = lax.axis_size("pipe") - 1
    place = lax.axis_index("seq")[None]

    packed = exchange(pack(queries, keys, values, segments))

    own = out_weight[0]
    y_own = lax.ppermute(own, "seq", YSWAP)
    left = lax.ppermute(own, "seq", XUP)
    right = lax.ppermute(own, "seq", XDOWN)
    y_left = lax.ppermute(y_own, "seq", XUP)
    y_right = lax.ppermute(y_own, "seq", XDOWN)
    far = lax.ppermute(left, "seq", XUP)

    local_seg = segments[0]
    gate_tok = per_sample(local_seg[0], gates[0, 0])
    g_scaled = (per_sample(local_seg[1], gates[0, 1]) * upstream[0].astype(F32)).astype(BF16)
    g_other = lax.ppermute(g_scaled, "seq", CORE)
    near = attention_grad(place, g_scaled, g_other, (own, y_own, left, right))
    near = tuple(to_chip(g, o) for g, o in zip(near, OFFSETS[:4]))

    sections = jnp.stack([section, jnp.zeros_like(section)])
    turned = choose(sections, loss_grad, upstream[0], y_own)
    next_grad = rotated(turned, "pipe", -1)

    heads = attention_forward(packed, turned, gate_tok)
    attn = exchange_same_core(heads)

    y_right = follow(y_right, heads, *near, y_left, far)
    y_far = lax.ppermute(y_right, "seq", XDOWN)
    pieces = (own, y_own, left, right, y_left, y_right, far, y_far)
    next_grad = settle(next_grad)
    distant = attention_grad(place, g_scaled, g_other, pieces[4:], next_grad)
    distant = tuple(to_chip(g, o) for g, o in zip(distant, OFFSETS[4:]))
    part, part_other = project(place, attn, pieces)
    part_other = lax.ppermute(follow(part_other, *distant), "seq", CORE)
    grads = attention_backward(place, packed, near + distant)

    section_out = (hidden_in[0].astype(F32) + gate_tok * (part + part_other)).astype(BF16)
    section_out = jnp.where(section == last_section, fresh, section_out)
    next_act = rotated(section_out, "pipe", 1)

    qkv_grads = unpack(exchange(grads))
    return (next_act[None], next_grad[None], qkv_grads[None])


def solution(mesh):
    in_specs = (
        P("pipe", "seq", None),
        P("pipe", None, "seq", None),
        P("pipe", None, "seq", None),
        P("pipe", None, "seq", None),
        P("pipe", None, "seq"),
        P("pipe", None, None, None),
        P("pipe", "seq", None),
        P("pipe", "seq", None),
        P("seq", None),
        P("seq", None),
    )
    out_specs = (P("pipe", "seq", None), P("pipe", "seq", None), P("pipe", None, "seq", None))
    return jax.shard_map(body, mesh=mesh, in_specs=in_specs, out_specs=out_specs, check_vma=False)
```

```python
import functools

import jax
import jax.numpy as jnp
from jax import lax
from jax.experimental import pallas as pl
from jax.experimental.pallas import tpu as pltpu
from jax.sharding import PartitionSpec as P

HD = 128
SCALE = HD ** (-0.5)
EXP2 = SCALE * 1.4426950408889634
LOW = -1e30
QB = 256
KT = 512
SEG_ROWS = 16
F32 = jnp.float32
BF16 = jnp.bfloat16

XN, PER_X = 4, 4
OFFSETS = (0, 3, 1, 2)
CORE = [(i, i ^ 1) for i in range(XN * PER_X)]
YSWAP = [(i, i ^ 2) for i in range(XN * PER_X)]


def along_x(array, offset):
    if offset == 0:
        return array
    count = XN * PER_X
    return lax.ppermute(array, "seq", [(i, (i + PER_X * offset) % count) for i in range(count)])


def x_at(place_ref, offset):
    return (place_ref[0] // PER_X + offset) % XN


def rows_at(place_ref, bits, rows):
    return pl.ds(pl.multiple_of(((place_ref[0] % PER_X) ^ bits) * rows, rows), rows)


def params(mib):
    return pltpu.CompilerParams(vmem_limit_bytes=mib * 1024 * 1024)


def whole(count):
    return [pl.BlockSpec(memory_space=pltpu.VMEM)] * count


def anywhere(arrays):
    return [pl.BlockSpec(memory_space=pl.ANY)] * len(arrays)


def in_hbm(count):
    return [pl.BlockSpec(memory_space=pltpu.HBM)] * count


def cost(microseconds):
    return pl.CostEstimate(
        flops=int(microseconds * 1e9), bytes_accessed=0, transcendentals=0
    )


def dot(a, b, dims):
    return lax.dot_general(a, b, (dims, ((), ())), preferred_element_type=F32)


def pack_kernel(seg_ref, q_ref, k_ref, v_ref, *refs):
    out_ref = refs[-1]
    rows = q_ref.shape[0]
    ids = jnp.broadcast_to(seg_ref[...].astype(F32), (SEG_ROWS, HD)).astype(BF16)
    for h in range(out_ref.shape[0]):
        cols = slice(h * HD, (h + 1) * HD)
        out_ref[h, 0:rows, :] = q_ref[:, cols]
        out_ref[h, rows:2 * rows, :] = k_ref[:, cols]
        out_ref[h, 2 * rows:3 * rows, :] = v_ref[:, cols]
        out_ref[h, 3 * rows:, :] = ids


def pack(queries, keys, values, segments, batch, *later):
    rows, width = queries.shape[2], queries.shape[3]
    heads = width // HD
    height = 3 * rows + SEG_ROWS
    block = pl.BlockSpec((None, None, rows, width), lambda i: (0, batch, 0, 0))
    return pl.pallas_call(
        pack_kernel,
        grid=(1,),
        out_shape=jax.ShapeDtypeStruct((heads, height, HD), BF16),
        in_specs=[pl.BlockSpec((1, rows), lambda i: (0, 0)), block, block, block]
        + anywhere(later),
        out_specs=pl.BlockSpec((heads, height, HD), lambda i: (0, 0, 0)),
        compiler_params=params(16 if later else 60),
        cost_estimate=cost(2),
        name="pack",
    )(segments[0, batch][None], queries, keys, values, *later)


def follow_kernel(array_ref, *refs):
    pass


def follow(array, *later):
    return pl.pallas_call(
        follow_kernel,
        out_shape=jax.ShapeDtypeStruct(array.shape, array.dtype),
        in_specs=anywhere((array,) + later),
        out_specs=pl.BlockSpec(memory_space=pl.ANY),
        input_output_aliases={0: 0},
        compiler_params=params(1),
        cost_estimate=cost(0.01),
        name="follow",
    )(array, *later)


def sample_starts(in_ref, rows):
    ids = in_ref[:, 3 * rows:, :].astype(F32)
    return [
        jnp.sum(jnp.where(ids < s, 1.0, 0.0)).astype(jnp.int32) // SEG_ROWS for s in (1, 2, 3)
    ]


def sample_of(position, starts):
    return sum(jnp.where(position >= b, 1.0, 0.0) for b in starts)


def tile_range(first, last, starts, total):
    low, high = 0, total
    for b in starts:
        low = jnp.maximum(low, jnp.where(b <= first, b, 0))
        high = jnp.minimum(high, jnp.where(b > last, b, total))
    return low // KT, (high + KT - 1) // KT


def block_rows(ref, index, count, start, rows):
    per = count // rows
    return ref[pl.ds(index * per, per), start:start + rows, :].reshape(count, HD)


def fill_samples(seg_s, starts):
    total = seg_s.shape[0]
    for i in range(total // 256):
        position = i * 256 + lax.broadcasted_iota(jnp.int32, (256, HD), 0)
        seg_s[i * 256:(i + 1) * 256, :] = sample_of(position, starts)


def forward_kernel(place_ref, in_ref, *refs):
    outs, (out_s, vt_s, seg_s) = refs[-3 - XN:-3], refs[-3:]
    blocks, rows = in_ref.shape[0], 128
    total = blocks * rows
    starts = sample_starts(in_ref, rows)
    fill_samples(seg_s, starts)
    for i in range(blocks):
        vt_s[:, i * rows:(i + 1) * rows] = in_ref[i, 2 * rows:3 * rows, :].T

    def per_block(i, _):
        q = block_rows(in_ref, i, QB, 0, rows)
        first = i * QB
        seg_q = sample_of(first + lax.broadcasted_iota(jnp.int32, (1, QB), 1), starts)
        begin, end = tile_range(first, first + QB - 1, starts, total)

        def per_tile(t, carry):
            m, l, acc = carry
            k = block_rows(in_ref, t, KT, rows, rows)
            s = dot(k, q, ((1,), (1,)))
            seg_k = seg_s[pl.ds(pl.multiple_of(t * KT, KT), KT), :]
            s = jnp.where(jnp.concatenate([seg_k, seg_k], axis=1) == seg_q, s, LOW)
            m_new = jnp.maximum(m, jnp.max(s, axis=0, keepdims=True))
            p = jnp.exp2((s - m_new) * EXP2)
            alpha = jnp.exp2((m - m_new) * EXP2)
            l = l * alpha + jnp.sum(p, axis=0, keepdims=True)
            vt = vt_s[:, pl.ds(pl.multiple_of(t * KT, KT), KT)]
            acc = acc * alpha + dot(vt, p.astype(BF16), ((1,), (0,)))
            return m_new, l, acc

        m0 = jnp.full((1, QB), LOW, F32)
        l0 = jnp.zeros((1, QB), F32)
        m, l, acc = lax.fori_loop(begin, end, per_tile, (m0, l0, jnp.zeros((HD, QB), F32)))
        out_s[i] = (acc / l).T.astype(BF16)
        return 0

    lax.fori_loop(0, total // QB, per_block, 0)
    per = total // QB // XN
    for offset, ref in zip(OFFSETS, outs):
        ref[...] = out_s[pl.ds(x_at(place_ref, offset) * per, per)].reshape(per * QB, HD)


def attention_forward(place, packed, *later):
    total = packed.shape[0] * 128
    return pl.pallas_call(
        forward_kernel,
        out_shape=(jax.ShapeDtypeStruct((total // XN, HD), BF16),) * XN,
        in_specs=[pl.BlockSpec(memory_space=pltpu.SMEM)] + whole(1) + anywhere(later),
        out_specs=tuple(whole(XN)),
        scratch_shapes=[
            pltpu.VMEM((total // QB, QB, HD), BF16),
            pltpu.VMEM((HD, total), BF16),
            pltpu.VMEM((total, HD), F32),
        ],
        compiler_params=params(24),
        cost_estimate=cost(0.2),
        name="attention_forward",
    )(place, packed, *later)


def backward_kernel(place_ref, in_ref, *refs):
    g_refs = refs[:XN]
    out_ref, g_ref, out_s, kt_s, seg_s, s_s, dp_s, dk_s, dv_s, in_sems, out_sem = refs[-11:]
    blocks, rows = in_ref.shape[0], 128
    arriving = []
    for n, (offset, ref) in enumerate(zip(OFFSETS, g_refs)):
        source = x_at(place_ref, -offset % XN)
        arriving.append(pltpu.make_async_copy(ref, g_ref.at[source], in_sems.at[n]))
        arriving[-1].start()
    total = blocks * rows
    starts = sample_starts(in_ref, rows)
    fill_samples(seg_s, starts)
    for i in range(blocks):
        kt_s[:, i * rows:(i + 1) * rows] = in_ref[i, rows:2 * rows, :].T
    dk_s[...] = jnp.zeros_like(dk_s)
    dv_s[...] = jnp.zeros_like(dv_s)
    for copy in arriving:
        copy.wait()

    def per_block(i, _):
        q = block_rows(in_ref, i, QB, 0, rows)
        share = total // XN // QB
        g = g_ref[i // share, pl.ds(pl.multiple_of(i % share * QB, QB), QB), :]
        first = i * QB
        seg_q = sample_of(first + lax.broadcasted_iota(jnp.int32, (1, QB), 1), starts)
        begin, end = tile_range(first, first + QB - 1, starts, total)

        def scores(t, carry):
            m, l, d = carry
            here = pl.ds(pl.multiple_of(t * KT, KT), KT)
            s = dot(block_rows(in_ref, t, KT, rows, rows), q, ((1,), (1,)))
            dp = dot(block_rows(in_ref, t, KT, 2 * rows, rows), g, ((1,), (1,)))
            seg_k = seg_s[here, :]
            s = jnp.where(jnp.concatenate([seg_k, seg_k], axis=1) == seg_q, s, LOW)
            s_s[here, :] = s
            dp_s[here, :] = dp
            m_new = jnp.maximum(m, jnp.max(s, axis=0, keepdims=True))
            p = jnp.exp2((s - m_new) * EXP2)
            alpha = jnp.exp2((m - m_new) * EXP2)
            l = l * alpha + jnp.sum(p, axis=0, keepdims=True)
            d = d * alpha + jnp.sum(p * dp, axis=0, keepdims=True)
            return m_new, l, d

        zero = jnp.zeros((1, QB), F32)
        m, l, d = lax.fori_loop(begin, end, scores, (jnp.full((1, QB), LOW, F32), zero, zero))
        inverse = 1.0 / l
        delta = d * inverse

        def grads(t, acc):
            here = pl.ds(pl.multiple_of(t * KT, KT), KT)
            p = jnp.exp2((s_s[here, :] - m) * EXP2) * inverse
            ds = (p * (dp_s[here, :] - delta)).astype(BF16)
            dv_s[here, :] += dot(p.astype(BF16), g, ((1,), (0,)))
            dk_s[here, :] += dot(ds, q, ((1,), (0,)))
            return acc + dot(kt_s[:, here], ds, ((1,), (0,)))

        acc = lax.fori_loop(begin, end, grads, jnp.zeros((HD, QB), F32))
        dq = (acc * SCALE).T.astype(BF16)
        per = QB // rows
        out_s[pl.ds(i * per, per), 0:rows, :] = dq.reshape(per, rows, HD)
        return 0

    lax.fori_loop(0, total // QB, per_block, 0)
    for i in range(blocks):
        here = slice(i * rows, (i + 1) * rows)
        out_s[i, rows:2 * rows, :] = (dk_s[here, :] * SCALE).astype(BF16)
        out_s[i, 2 * rows:3 * rows, :] = dv_s[here, :].astype(BF16)
        pltpu.make_async_copy(out_s.at[i], out_ref.at[i], out_sem).start()
    pltpu.make_async_copy(out_s, out_ref, out_sem).wait()


def attention_backward(place, packed, grads, *later):
    blocks = packed.shape[0]
    total = blocks * 128
    return pl.pallas_call(
        backward_kernel,
        out_shape=jax.ShapeDtypeStruct((blocks, 3 * 128, HD), BF16),
        in_specs=[pl.BlockSpec(memory_space=pltpu.SMEM)]
        + whole(1)
        + in_hbm(XN)
        + anywhere(later),
        out_specs=in_hbm(1)[0],
        scratch_shapes=[
            pltpu.VMEM((XN, total // XN, HD), BF16),
            pltpu.VMEM((blocks, 3 * 128, HD), BF16),
            pltpu.VMEM((HD, total), BF16),
            pltpu.VMEM((total, HD), F32),
            pltpu.VMEM((total, QB), F32),
            pltpu.VMEM((total, QB), F32),
            pltpu.VMEM((total, HD), F32),
            pltpu.VMEM((total, HD), F32),
            pltpu.SemaphoreType.DMA((XN,)),
            pltpu.SemaphoreType.DMA,
        ],
        compiler_params=params(60),
        cost_estimate=cost(30),
        name="attention_backward",
    )(place, packed, *grads, *later)


def grad_kernel(place_ref, *refs):
    grads, pieces, outs, g_s = refs[:PER_X], refs[PER_X:PER_X + XN], refs[-1 - XN:-1], refs[-1]
    rows = grads[0].shape[0]
    for bits, ref in enumerate(grads):
        g_s[rows_at(place_ref, bits, rows), :] = ref[...]
    for j in range(0, XN, 2):
        w = jnp.concatenate([pieces[j][...], pieces[j + 1][...]], axis=0)
        r = dot(g_s[...], w, ((1,), (1,))).astype(BF16)
        outs[j][...] = r[:, :HD]
        outs[j + 1][...] = r[:, HD:]


def attention_grad(place, grads, pieces, *later):
    rows, width = grads[0].shape
    return pl.pallas_call(
        grad_kernel,
        out_shape=(jax.ShapeDtypeStruct((PER_X * rows, HD), BF16),) * XN,
        in_specs=[pl.BlockSpec(memory_space=pltpu.SMEM)] + whole(PER_X + XN) + anywhere(later),
        out_specs=tuple(whole(XN)),
        scratch_shapes=[pltpu.VMEM((PER_X * rows, width), BF16)],
        compiler_params=params(24),
        cost_estimate=cost(0.2),
        name="attention_grad",
    )(place, *grads, *pieces, *later)


def project_kernel(place_ref, *refs):
    attns, pieces = refs[:XN], refs[XN:2 * XN]
    own_ref, across_ref, send_ref, a_s = refs[-4:]
    rows, width = own_ref.shape
    for n, bits in enumerate((0, 2, 1, 3)):
        for j in range(XN):
            a_s[n * rows:(n + 1) * rows, j * HD:(j + 1) * HD] = attns[j][
                rows_at(place_ref, bits, rows), :
            ]
    step = 256
    for n in range(0, width, step):
        w = jnp.concatenate([ref[:, n:n + step] for ref in pieces], axis=0)
        acc = dot(a_s[...], w, ((1,), (0,)))
        own_ref[:, n:n + step] = acc[:rows]
        across_ref[:, n:n + step] = acc[rows:2 * rows]
        send_ref[:, n:n + step] = acc[2 * rows:].astype(send_ref.dtype)


def project(place, attns, pieces, *later):
    rows, width = pieces[0].shape
    return pl.pallas_call(
        project_kernel,
        out_shape=(
            jax.ShapeDtypeStruct((rows, width), F32),
            jax.ShapeDtypeStruct((rows, width), F32),
            jax.ShapeDtypeStruct((2 * rows, width), BF16),
        ),
        in_specs=[pl.BlockSpec(memory_space=pltpu.SMEM)] + whole(2 * XN) + anywhere(later),
        out_specs=tuple(whole(3)),
        scratch_shapes=[pltpu.VMEM((PER_X * rows, XN * HD), BF16)],
        compiler_params=params(24),
        cost_estimate=cost(0.2),
        name="project",
    )(place, *attns, *pieces, *later)


def unpack_kernel(in_ref, out_ref):
    rows = out_ref.shape[1]
    for h in range(in_ref.shape[0]):
        for t in range(3):
            out_ref[t, :, h * HD:(h + 1) * HD] = in_ref[h, t * rows:(t + 1) * rows, :]


def unpack(received):
    heads, rows = received.shape[0], received.shape[1] // 3
    return pl.pallas_call(
        unpack_kernel,
        out_shape=jax.ShapeDtypeStruct((3, rows, heads * HD), BF16),
        in_specs=whole(1),
        out_specs=whole(1)[0],
        compiler_params=params(24),
        cost_estimate=cost(2),
        name="unpack",
    )(received)


def choose_kernel(section_ref, first_ref, second_ref, *refs):
    out_ref = refs[-1]
    out_ref[...] = jnp.where(section_ref[0] == section_ref[1], first_ref[...], second_ref[...])


def choose(sections, first, second, *later):
    return pl.pallas_call(
        choose_kernel,
        out_shape=jax.ShapeDtypeStruct(first.shape, first.dtype),
        in_specs=[pl.BlockSpec(memory_space=pltpu.SMEM)] + whole(2) + anywhere(later),
        out_specs=whole(1)[0],
        compiler_params=params(16),
        cost_estimate=cost(2),
        name="choose",
    )(sections, first, second, *later)


def settle_kernel(in_ref, out_ref):
    out_ref[...] = in_ref[...]


def settle(array):
    return pl.pallas_call(
        settle_kernel,
        out_shape=jax.ShapeDtypeStruct(array.shape, array.dtype),
        in_specs=whole(1),
        out_specs=whole(1)[0],
        compiler_params=params(8),
        cost_estimate=cost(0.2),
        name="settle",
    )(array)


def rotated(array, axis, by):
    length = lax.axis_size(axis)
    return lax.ppermute(array, axis, [(i, (i + by) % length) for i in range(length)])


def per_sample(seg, table):
    onehot = (seg[:, None] == jnp.arange(table.shape[0], dtype=jnp.int32)[None, :]).astype(F32)
    return jnp.sum(onehot[:, :, None] * table[None, :, :], axis=1)


def exchange(array):
    return lax.all_to_all(array, "seq", 0, 0, tiled=True)


def body(hidden_in, queries, keys, values, segments, gates, out_weight, upstream, fresh, loss_grad):
    section = lax.axis_index("pipe")
    last_section = lax.axis_size("pipe") - 1
    place = lax.axis_index("seq")[None]

    own = out_weight[0]
    pieces = tuple(along_x(own, -offset % XN) for offset in OFFSETS)

    fwd = exchange(pack(queries, keys, values, segments, 0))
    local_seg = segments[0]
    g_scaled = (per_sample(local_seg[1], gates[0, 1]) * upstream[0].astype(F32)).astype(BF16)
    g_across = lax.ppermute(g_scaled, "seq", YSWAP)
    g_core = lax.ppermute(g_scaled, "seq", CORE)
    g_both = lax.ppermute(g_across, "seq", CORE)
    packed = pack(queries, keys, values, segments, 1, g_across, *pieces[1:])
    bwd = exchange(packed)
    gate_tok = per_sample(local_seg[0], gates[0, 0])

    sections = jnp.stack([section, jnp.zeros_like(section)])
    turned = choose(sections, loss_grad, upstream[0], fwd)
    next_grad = rotated(turned, "pipe", -1)

    attns = attention_forward(place, fwd, packed, turned, gate_tok, g_both)
    attns = tuple(along_x(a, o) for a, o in zip(attns, OFFSETS))
    grads = attention_grad(place, (g_scaled, g_core, g_across, g_both), pieces, attns[0])
    grads = tuple(along_x(g, o) for g, o in zip(grads, OFFSETS))

    attns = (attns[0], attns[2], attns[1], attns[3])
    part, part_across, part_send = project(place, attns, pieces, bwd, next_grad)
    received = lax.ppermute(follow(part_send, *grads), "seq", CORE)
    rows = part.shape[0]
    across = lax.ppermute((part_across + received[rows:].astype(F32)).astype(BF16), "seq", YSWAP)
    proj = part + received[:rows].astype(F32) + across.astype(F32)
    section_out = (hidden_in[0].astype(F32) + gate_tok * proj).astype(BF16)
    section_out = jnp.where(section == last_section, fresh, section_out)

    grads = attention_backward(place, bwd, grads)
    next_act = rotated(section_out, "pipe", 1)

    qkv_grads = unpack(exchange(grads))
    return (next_act[None], settle(next_grad)[None], qkv_grads[None])


def solution(mesh):
    in_specs = (
        P("pipe", "seq", None),
        P("pipe", None, "seq", None),
        P("pipe", None, "seq", None),
        P("pipe", None, "seq", None),
        P("pipe", None, "seq"),
        P("pipe", None, None, None),
        P("pipe", "seq", None),
        P("pipe", "seq", None),
        P("seq", None),
        P("seq", None),
    )
    out_specs = (P("pipe", "seq", None), P("pipe", "seq", None), P("pipe", None, "seq", None))
    return jax.shard_map(body, mesh=mesh, in_specs=in_specs, out_specs=out_specs, check_vma=False)
```

```python
import functools

import jax
import jax.numpy as jnp
from jax import lax
from jax.experimental import pallas as pl
from jax.experimental.pallas import tpu as pltpu
from jax.sharding import PartitionSpec as P

HD = 128
SCALE = HD ** (-0.5)
EXP2 = SCALE * 1.4426950408889634
LOW = -1e30
QB = 256
KT = 512
SEG_ROWS = 16
F32 = jnp.float32
BF16 = jnp.bfloat16

XN, PER_X = 4, 4
OFFSETS = (0, 3, 1, 2)
CORE = [(i, i ^ 1) for i in range(XN * PER_X)]
YSWAP = [(i, i ^ 2) for i in range(XN * PER_X)]


def along_x(array, offset):
    if offset == 0:
        return array
    count = XN * PER_X
    return lax.ppermute(array, "seq", [(i, (i + PER_X * offset) % count) for i in range(count)])


def x_at(place_ref, offset):
    return (place_ref[0] // PER_X + offset) % XN


def rows_at(place_ref, bits, rows):
    return pl.ds(pl.multiple_of(((place_ref[0] % PER_X) ^ bits) * rows, rows), rows)


def params(mib):
    return pltpu.CompilerParams(vmem_limit_bytes=mib * 1024 * 1024)


def whole(count):
    return [pl.BlockSpec(memory_space=pltpu.VMEM)] * count


def anywhere(arrays):
    return [pl.BlockSpec(memory_space=pl.ANY)] * len(arrays)


def in_hbm(count):
    return [pl.BlockSpec(memory_space=pltpu.HBM)] * count


def cost(microseconds):
    return pl.CostEstimate(
        flops=int(microseconds * 1e9), bytes_accessed=0, transcendentals=0
    )


def dot(a, b, dims):
    return lax.dot_general(a, b, (dims, ((), ())), preferred_element_type=F32)


def pack_kernel(seg_ref, q_ref, k_ref, v_ref, *refs):
    out_ref = refs[-1]
    rows = q_ref.shape[0]
    ids = jnp.broadcast_to(seg_ref[...].astype(F32), (SEG_ROWS, HD)).astype(BF16)
    for h in range(out_ref.shape[0]):
        cols = slice(h * HD, (h + 1) * HD)
        out_ref[h, 0:rows, :] = q_ref[:, cols]
        out_ref[h, rows:2 * rows, :] = k_ref[:, cols]
        out_ref[h, 2 * rows:3 * rows, :] = v_ref[:, cols]
        out_ref[h, 3 * rows:, :] = ids


def pack(queries, keys, values, segments, batch, *later):
    rows, width = queries.shape[2], queries.shape[3]
    heads = width // HD
    height = 3 * rows + SEG_ROWS
    block = pl.BlockSpec((None, None, rows, width), lambda i: (0, batch, 0, 0))
    return pl.pallas_call(
        pack_kernel,
        grid=(1,),
        out_shape=jax.ShapeDtypeStruct((heads, height, HD), BF16),
        in_specs=[pl.BlockSpec((1, rows), lambda i: (0, 0)), block, block, block]
        + anywhere(later),
        out_specs=pl.BlockSpec((heads, height, HD), lambda i: (0, 0, 0)),
        compiler_params=params(60),
        cost_estimate=cost(2),
        name="pack",
    )(segments[0, batch][None], queries, keys, values, *later)


def follow_kernel(array_ref, *refs):
    pass


def follow(array, *later):
    return pl.pallas_call(
        follow_kernel,
        out_shape=jax.ShapeDtypeStruct(array.shape, array.dtype),
        in_specs=anywhere((array,) + later),
        out_specs=pl.BlockSpec(memory_space=pl.ANY),
        input_output_aliases={0: 0},
        compiler_params=params(1),
        cost_estimate=cost(0.01),
        name="follow",
    )(array, *later)


def sample_starts(in_ref, rows):
    ids = in_ref[:, 3 * rows:, :].astype(F32)
    return [
        jnp.sum(jnp.where(ids < s, 1.0, 0.0)).astype(jnp.int32) // SEG_ROWS for s in (1, 2, 3)
    ]


def sample_of(position, starts):
    return sum(jnp.where(position >= b, 1.0, 0.0) for b in starts)


def tile_range(first, last, starts, total):
    low, high = 0, total
    for b in starts:
        low = jnp.maximum(low, jnp.where(b <= first, b, 0))
        high = jnp.minimum(high, jnp.where(b > last, b, total))
    return low // KT, (high + KT - 1) // KT


def block_rows(ref, index, count, start, rows):
    per = count // rows
    return ref[pl.ds(index * per, per), start:start + rows, :].reshape(count, HD)


def fill_samples(seg_s, starts):
    total = seg_s.shape[0]
    for i in range(total // 256):
        position = i * 256 + lax.broadcasted_iota(jnp.int32, (256, HD), 0)
        seg_s[i * 256:(i + 1) * 256, :] = sample_of(position, starts)


def forward_kernel(place_ref, in_hbm_ref, *refs):
    outs, (in_ref, out_s, vt_s, seg_s, in_sem, out_sems) = refs[-6 - XN:-6], refs[-6:]
    arriving = pltpu.make_async_copy(in_hbm_ref, in_ref, in_sem)
    arriving.start()
    arriving.wait()
    blocks, rows = in_ref.shape[0], 128
    total = blocks * rows
    starts = sample_starts(in_ref, rows)
    fill_samples(seg_s, starts)
    for i in range(blocks):
        vt_s[:, i * rows:(i + 1) * rows] = in_ref[i, 2 * rows:3 * rows, :].T

    def per_block(i, _):
        q = block_rows(in_ref, i, QB, 0, rows)
        first = i * QB
        seg_q = sample_of(first + lax.broadcasted_iota(jnp.int32, (1, QB), 1), starts)
        begin, end = tile_range(first, first + QB - 1, starts, total)

        def per_tile(t, carry):
            m, l, acc = carry
            k = block_rows(in_ref, t, KT, rows, rows)
            s = dot(k, q, ((1,), (1,)))
            seg_k = seg_s[pl.ds(pl.multiple_of(t * KT, KT), KT), :]
            s = jnp.where(jnp.concatenate([seg_k, seg_k], axis=1) == seg_q, s, LOW)
            m_new = jnp.maximum(m, jnp.max(s, axis=0, keepdims=True))
            p = jnp.exp2((s - m_new) * EXP2)
            alpha = jnp.exp2((m - m_new) * EXP2)
            l = l * alpha + jnp.sum(p, axis=0, keepdims=True)
            vt = vt_s[:, pl.ds(pl.multiple_of(t * KT, KT), KT)]
            acc = acc * alpha + dot(vt, p.astype(BF16), ((1,), (0,)))
            return m_new, l, acc

        m0 = jnp.full((1, QB), LOW, F32)
        l0 = jnp.zeros((1, QB), F32)
        m, l, acc = lax.fori_loop(begin, end, per_tile, (m0, l0, jnp.zeros((HD, QB), F32)))
        share = total // XN // QB
        here = pl.ds(pl.multiple_of(i % share * QB, QB), QB)
        out_s[i // share, here, :] = (acc / l).T.astype(BF16)
        return 0

    lax.fori_loop(0, total // QB, per_block, 0)
    leaving = [
        pltpu.make_async_copy(out_s.at[x_at(place_ref, offset)], ref, out_sems.at[n])
        for n, (offset, ref) in enumerate(zip(OFFSETS, outs))
    ]
    for copy in leaving:
        copy.start()
    for copy in leaving:
        copy.wait()


def attention_forward(place, packed, *later):
    total = packed.shape[0] * 128
    return pl.pallas_call(
        forward_kernel,
        out_shape=(jax.ShapeDtypeStruct((total // XN, HD), BF16),) * XN,
        in_specs=[pl.BlockSpec(memory_space=pltpu.SMEM)] + in_hbm(1) + anywhere(later),
        out_specs=tuple(in_hbm(XN)),
        scratch_shapes=[
            pltpu.VMEM(packed.shape, BF16),
            pltpu.VMEM((XN, total // XN, HD), BF16),
            pltpu.VMEM((HD, total), BF16),
            pltpu.VMEM((total, HD), F32),
            pltpu.SemaphoreType.DMA,
            pltpu.SemaphoreType.DMA((XN,)),
        ],
        compiler_params=params(60),
        cost_estimate=cost(0.2),
        name="attention_forward",
    )(place, packed, *later)


def backward_kernel(place_ref, in_hbm_ref, *refs):
    g_refs = refs[:XN]
    out_ref, in_ref, g_ref, out_s, kt_s, seg_s, s_s, dp_s, dk_s, dv_s, in_sems, out_sem = refs[-12:]
    packed = pltpu.make_async_copy(in_hbm_ref, in_ref, in_sems.at[XN])
    packed.start()
    blocks, rows = in_ref.shape[0], 128
    arriving = []
    for n, (offset, ref) in enumerate(zip(OFFSETS, g_refs)):
        source = x_at(place_ref, -offset % XN)
        arriving.append(pltpu.make_async_copy(ref, g_ref.at[source], in_sems.at[n]))
        arriving[-1].start()
    total = blocks * rows
    packed.wait()
    starts = sample_starts(in_ref, rows)
    fill_samples(seg_s, starts)
    for i in range(blocks):
        kt_s[:, i * rows:(i + 1) * rows] = in_ref[i, rows:2 * rows, :].T
    dk_s[...] = jnp.zeros_like(dk_s)
    dv_s[...] = jnp.zeros_like(dv_s)
    for copy in arriving:
        copy.wait()

    def per_block(i, _):
        q = block_rows(in_ref, i, QB, 0, rows)
        share = total // XN // QB
        g = g_ref[i // share, pl.ds(pl.multiple_of(i % share * QB, QB), QB), :]
        first = i * QB
        seg_q = sample_of(first + lax.broadcasted_iota(jnp.int32, (1, QB), 1), starts)
        begin, end = tile_range(first, first + QB - 1, starts, total)

        def scores(t, carry):
            m, l, d = carry
            here = pl.ds(pl.multiple_of(t * KT, KT), KT)
            s = dot(block_rows(in_ref, t, KT, rows, rows), q, ((1,), (1,)))
            dp = dot(block_rows(in_ref, t, KT, 2 * rows, rows), g, ((1,), (1,)))
            seg_k = seg_s[here, :]
            s = jnp.where(jnp.concatenate([seg_k, seg_k], axis=1) == seg_q, s, LOW)
            s_s[here, :] = s
            dp_s[here, :] = dp
            m_new = jnp.maximum(m, jnp.max(s, axis=0, keepdims=True))
            p = jnp.exp2((s - m_new) * EXP2)
            alpha = jnp.exp2((m - m_new) * EXP2)
            l = l * alpha + jnp.sum(p, axis=0, keepdims=True)
            d = d * alpha + jnp.sum(p * dp, axis=0, keepdims=True)
            return m_new, l, d

        zero = jnp.zeros((1, QB), F32)
        m, l, d = lax.fori_loop(begin, end, scores, (jnp.full((1, QB), LOW, F32), zero, zero))
        inverse = 1.0 / l
        delta = d * inverse

        def grads(t, acc):
            here = pl.ds(pl.multiple_of(t * KT, KT), KT)
            p = jnp.exp2((s_s[here, :] - m) * EXP2) * inverse
            ds = (p * (dp_s[here, :] - delta)).astype(BF16)
            dv_s[here, :] += dot(p.astype(BF16), g, ((1,), (0,)))
            dk_s[here, :] += dot(ds, q, ((1,), (0,)))
            return acc + dot(kt_s[:, here], ds, ((1,), (0,)))

        acc = lax.fori_loop(begin, end, grads, jnp.zeros((HD, QB), F32))
        dq = (acc * SCALE).T.astype(BF16)
        per = QB // rows
        out_s[pl.ds(i * per, per), 0:rows, :] = dq.reshape(per, rows, HD)
        return 0

    lax.fori_loop(0, total // QB, per_block, 0)
    for i in range(blocks):
        here = slice(i * rows, (i + 1) * rows)
        out_s[i, rows:2 * rows, :] = (dk_s[here, :] * SCALE).astype(BF16)
        out_s[i, 2 * rows:3 * rows, :] = dv_s[here, :].astype(BF16)
        pltpu.make_async_copy(out_s.at[i], out_ref.at[i], out_sem).start()
    pltpu.make_async_copy(out_s, out_ref, out_sem).wait()


def attention_backward(place, packed, grads, *later):
    blocks = packed.shape[0]
    total = blocks * 128
    return pl.pallas_call(
        backward_kernel,
        out_shape=jax.ShapeDtypeStruct((blocks, 3 * 128, HD), BF16),
        in_specs=[pl.BlockSpec(memory_space=pltpu.SMEM)]
        + in_hbm(1 + XN)
        + anywhere(later),
        out_specs=in_hbm(1)[0],
        scratch_shapes=[
            pltpu.VMEM(packed.shape, BF16),
            pltpu.VMEM((XN, total // XN, HD), BF16),
            pltpu.VMEM((blocks, 3 * 128, HD), BF16),
            pltpu.VMEM((HD, total), BF16),
            pltpu.VMEM((total, HD), F32),
            pltpu.VMEM((total, QB), F32),
            pltpu.VMEM((total, QB), F32),
            pltpu.VMEM((total, HD), F32),
            pltpu.VMEM((total, HD), F32),
            pltpu.SemaphoreType.DMA((XN + 1,)),
            pltpu.SemaphoreType.DMA,
        ],
        compiler_params=params(60),
        cost_estimate=cost(30),
        name="attention_backward",
    )(place, packed, *grads, *later)


def grad_kernel(place_ref, *refs):
    grads, pieces, outs = refs[:PER_X], refs[PER_X:PER_X + XN], refs[-5 - XN:-5]
    g_s, w_s, out_s, in_sems, out_sems = refs[-5:]
    rows = grads[0].shape[0]
    arriving = []
    for bits, ref in enumerate(grads):
        target = g_s.at[rows_at(place_ref, bits, rows), :]
        arriving.append(pltpu.make_async_copy(ref, target, in_sems.at[bits]))
    for j, ref in enumerate(pieces):
        target = w_s.at[j * HD:(j + 1) * HD, :]
        arriving.append(pltpu.make_async_copy(ref, target, in_sems.at[PER_X + j]))
    for copy in arriving:
        copy.start()
    for copy in arriving:
        copy.wait()
    leaving = []
    for j in range(0, XN, 2):
        r = dot(g_s[...], w_s[j * HD:(j + 2) * HD, :], ((1,), (1,))).astype(BF16)
        out_s[j] = r[:, :HD]
        out_s[j + 1] = r[:, HD:]
        for n in (j, j + 1):
            leaving.append(pltpu.make_async_copy(out_s.at[n], outs[n], out_sems.at[n]))
            leaving[-1].start()
    for copy in leaving:
        copy.wait()


def attention_grad(place, grads, pieces, *later):
    rows, width = grads[0].shape
    return pl.pallas_call(
        grad_kernel,
        out_shape=(jax.ShapeDtypeStruct((PER_X * rows, HD), BF16),) * XN,
        in_specs=[pl.BlockSpec(memory_space=pltpu.SMEM)] + in_hbm(PER_X + XN) + anywhere(later),
        out_specs=tuple(in_hbm(XN)),
        scratch_shapes=[
            pltpu.VMEM((PER_X * rows, width), BF16),
            pltpu.VMEM((XN * HD, width), BF16),
            pltpu.VMEM((XN, PER_X * rows, HD), BF16),
            pltpu.SemaphoreType.DMA((PER_X + XN,)),
            pltpu.SemaphoreType.DMA((XN,)),
        ],
        compiler_params=params(60),
        cost_estimate=cost(0.2),
        name="attention_grad",
    )(place, *grads, *pieces, *later)


def project_kernel(place_ref, *refs):
    attns, pieces, outs = refs[:XN], refs[XN:2 * XN], refs[-11:-8]
    a_in, w_s, a_s, own_s, across_s, send_s, in_sems, out_sems = refs[-8:]
    rows, width = outs[0].shape
    arriving = []
    for j in range(XN):
        target = w_s.at[j * HD:(j + 1) * HD, :]
        arriving.append(pltpu.make_async_copy(attns[j], a_in.at[j], in_sems.at[j]))
        arriving.append(pltpu.make_async_copy(pieces[j], target, in_sems.at[XN + j]))
    for copy in arriving:
        copy.start()
    for copy in arriving:
        copy.wait()
    for n, bits in enumerate((0, 2, 1, 3)):
        for j in range(XN):
            a_s[n * rows:(n + 1) * rows, j * HD:(j + 1) * HD] = a_in[
                j, rows_at(place_ref, bits, rows), :
            ]
    step = 512
    for n in range(0, width, step):
        cols = slice(n, n + step)
        acc = dot(a_s[...], w_s[:, cols], ((1,), (0,)))
        own_s[:, cols] = acc[:rows]
        across_s[:, cols] = acc[rows:2 * rows]
        send_s[:, cols] = acc[2 * rows:].astype(BF16)
        for k, (result, out) in enumerate(zip((own_s, across_s, send_s), outs)):
            pltpu.make_async_copy(result.at[:, cols], out.at[:, cols], out_sems.at[k]).start()
    for k, (result, out) in enumerate(zip((own_s, across_s, send_s), outs)):
        pltpu.make_async_copy(result, out, out_sems.at[k]).wait()


def project(place, attns, pieces, *later):
    rows, width = pieces[0].shape
    shapes = (((rows, width), F32), ((rows, width), F32), ((2 * rows, width), BF16))
    return pl.pallas_call(
        project_kernel,
        out_shape=tuple(jax.ShapeDtypeStruct(*shape) for shape in shapes),
        in_specs=[pl.BlockSpec(memory_space=pltpu.SMEM)] + in_hbm(2 * XN) + anywhere(later),
        out_specs=tuple(in_hbm(3)),
        scratch_shapes=[
            pltpu.VMEM((XN, PER_X * rows, HD), BF16),
            pltpu.VMEM((XN * HD, width), BF16),
            pltpu.VMEM((PER_X * rows, XN * HD), BF16),
        ]
        + [pltpu.VMEM(*shape) for shape in shapes]
        + [pltpu.SemaphoreType.DMA((2 * XN,)), pltpu.SemaphoreType.DMA((3,))],
        compiler_params=params(60),
        cost_estimate=cost(0.2),
        name="project",
    )(place, *attns, *pieces, *later)


def unpack_kernel(in_ref, out_ref):
    rows = out_ref.shape[1]
    for h in range(in_ref.shape[0]):
        for t in range(3):
            out_ref[t, :, h * HD:(h + 1) * HD] = in_ref[h, t * rows:(t + 1) * rows, :]


def unpack(received):
    heads, rows = received.shape[0], received.shape[1] // 3
    return pl.pallas_call(
        unpack_kernel,
        out_shape=jax.ShapeDtypeStruct((3, rows, heads * HD), BF16),
        in_specs=whole(1),
        out_specs=whole(1)[0],
        compiler_params=params(24),
        cost_estimate=cost(2),
        name="unpack",
    )(received)


def choose_kernel(section_ref, first_ref, second_ref, *refs):
    out_ref = refs[-1]
    out_ref[...] = jnp.where(section_ref[0] == section_ref[1], first_ref[...], second_ref[...])


def choose(sections, first, second, *later):
    return pl.pallas_call(
        choose_kernel,
        out_shape=jax.ShapeDtypeStruct(first.shape, first.dtype),
        in_specs=[pl.BlockSpec(memory_space=pltpu.SMEM)] + whole(2) + anywhere(later),
        out_specs=whole(1)[0],
        compiler_params=params(16),
        cost_estimate=cost(2),
        name="choose",
    )(sections, first, second, *later)


def shifted(array, axis, by):
    length = lax.axis_size(axis)
    pairs = [(i, i + by) for i in range(length) if 0 <= i + by < length]
    return lax.ppermute(array, axis, pairs)


def rotated(array, axis, by):
    length = lax.axis_size(axis)
    return lax.ppermute(array, axis, [(i, (i + by) % length) for i in range(length)])


def per_sample(seg, table):
    onehot = (seg[:, None] == jnp.arange(table.shape[0], dtype=jnp.int32)[None, :]).astype(F32)
    return jnp.sum(onehot[:, :, None] * table[None, :, :], axis=1)


def exchange(array):
    return lax.all_to_all(array, "seq", 0, 0, tiled=True)


def body(hidden_in, queries, keys, values, segments, gates, out_weight, upstream, fresh, loss_grad):
    section = lax.axis_index("pipe")
    last_section = lax.axis_size("pipe") - 1
    place = lax.axis_index("seq")[None]

    own = out_weight[0]
    pieces = tuple(along_x(own, -offset % XN) for offset in OFFSETS)
    moved = shifted(upstream[0], "pipe", -1)

    fwd = exchange(pack(queries, keys, values, segments, 0))
    local_seg = segments[0]
    g_scaled = (per_sample(local_seg[1], gates[0, 1]) * upstream[0].astype(F32)).astype(BF16)
    g_across = lax.ppermute(g_scaled, "seq", YSWAP)
    g_core = lax.ppermute(g_scaled, "seq", CORE)
    g_both = lax.ppermute(g_across, "seq", CORE)
    packed = pack(queries, keys, values, segments, 1, g_across, moved, *pieces[1:])
    bwd = exchange(packed)
    gate_tok = per_sample(local_seg[0], gates[0, 0])

    grads = attention_grad(place, (g_scaled, g_core, g_across, g_both), pieces, packed)
    attns = attention_forward(place, fwd, grads[0], gate_tok)
    grads = tuple(along_x(g, o) for g, o in zip(grads, OFFSETS))
    attns = (attns[0], follow(attns[1], *grads[1:])) + attns[2:]
    attns = tuple(along_x(a, o) for a, o in zip(attns, OFFSETS))

    attns = (attns[0], attns[2], attns[1], attns[3])
    part, part_across, part_send = project(place, attns, pieces, bwd)
    received = lax.ppermute(part_send, "seq", CORE)
    rows = part.shape[0]
    across = (part_across + received[rows:].astype(F32)).astype(BF16)
    grads = attention_backward(place, bwd, grads, across)
    across = lax.ppermute(across, "seq", YSWAP)
    proj = part + received[:rows].astype(F32) + across.astype(F32)
    section_out = (hidden_in[0].astype(F32) + gate_tok * proj).astype(BF16)
    section_out = jnp.where(section == last_section, fresh, section_out)
    next_act = rotated(section_out, "pipe", 1)

    sections = jnp.stack([section, last_section * jnp.ones_like(section)])
    next_grad = choose(sections, loss_grad, moved)
    qkv_grads = unpack(exchange(grads))
    return (next_act[None], next_grad[None], qkv_grads[None])


def solution(mesh):
    in_specs = (
        P("pipe", "seq", None),
        P("pipe", None, "seq", None),
        P("pipe", None, "seq", None),
        P("pipe", None, "seq", None),
        P("pipe", None, "seq"),
        P("pipe", None, None, None),
        P("pipe", "seq", None),
        P("pipe", "seq", None),
        P("seq", None),
        P("seq", None),
    )
    out_specs = (P("pipe", "seq", None), P("pipe", "seq", None), P("pipe", None, "seq", None))
    return jax.shard_map(body, mesh=mesh, in_specs=in_specs, out_specs=out_specs, check_vma=False)
```

```python
import functools

import jax
import jax.numpy as jnp
from jax import lax
from jax.experimental import pallas as pl
from jax.experimental.pallas import tpu as pltpu
from jax.sharding import PartitionSpec as P

HD = 128
SCALE = HD ** (-0.5)
EXP2 = SCALE * 1.4426950408889634
LOW = -1e30
QB = 512
KT = 512
SEG_ROWS = 16
F32 = jnp.float32
BF16 = jnp.bfloat16

XN, PER_X = 4, 4
OFFSETS = (0, 3, 1, 2)
CORE = [(i, i ^ 1) for i in range(XN * PER_X)]
YSWAP = [(i, i ^ 2) for i in range(XN * PER_X)]


def along_x(array, offset):
    if offset == 0:
        return array
    count = XN * PER_X
    return lax.ppermute(array, "seq", [(i, (i + PER_X * offset) % count) for i in range(count)])


def x_at(place_ref, offset):
    return (place_ref[0] // PER_X + offset) % XN


def rows_at(place_ref, bits, rows):
    return pl.ds(pl.multiple_of(((place_ref[0] % PER_X) ^ bits) * rows, rows), rows)


def params(mib):
    return pltpu.CompilerParams(vmem_limit_bytes=mib * 1024 * 1024)


def whole(count):
    return [pl.BlockSpec(memory_space=pltpu.VMEM)] * count


def anywhere(arrays):
    return [pl.BlockSpec(memory_space=pl.ANY)] * len(arrays)


def in_hbm(count):
    return [pl.BlockSpec(memory_space=pltpu.HBM)] * count


def cost(microseconds):
    return pl.CostEstimate(
        flops=int(microseconds * 1e9), bytes_accessed=0, transcendentals=0
    )


def dot(a, b, dims):
    return lax.dot_general(a, b, (dims, ((), ())), preferred_element_type=F32)


def pack_kernel(seg_ref, q_ref, k_ref, v_ref, *refs):
    out_ref = refs[-1]
    rows = q_ref.shape[0]
    ids = jnp.broadcast_to(seg_ref[...].astype(F32), (SEG_ROWS, HD)).astype(BF16)
    for h in range(out_ref.shape[0]):
        cols = slice(h * HD, (h + 1) * HD)
        out_ref[h, 0:rows, :] = q_ref[:, cols]
        out_ref[h, rows:2 * rows, :] = k_ref[:, cols]
        out_ref[h, 2 * rows:3 * rows, :] = v_ref[:, cols]
        out_ref[h, 3 * rows:, :] = ids


def pack(queries, keys, values, segments, batch, *later):
    rows, width = queries.shape[2], queries.shape[3]
    heads = width // HD
    height = 3 * rows + SEG_ROWS
    block = pl.BlockSpec((None, None, rows, width), lambda i: (0, batch, 0, 0))
    return pl.pallas_call(
        pack_kernel,
        grid=(1,),
        out_shape=jax.ShapeDtypeStruct((heads, height, HD), BF16),
        in_specs=[pl.BlockSpec((1, rows), lambda i: (0, 0)), block, block, block]
        + anywhere(later),
        out_specs=pl.BlockSpec((heads, height, HD), lambda i: (0, 0, 0)),
        compiler_params=params(60),
        cost_estimate=cost(2),
        name="pack",
    )(segments[0, batch][None], queries, keys, values, *later)


def follow_kernel(array_ref, *refs):
    pass


def follow(array, *later):
    return pl.pallas_call(
        follow_kernel,
        out_shape=jax.ShapeDtypeStruct(array.shape, array.dtype),
        in_specs=anywhere((array,) + later),
        out_specs=pl.BlockSpec(memory_space=pl.ANY),
        input_output_aliases={0: 0},
        compiler_params=params(1),
        cost_estimate=cost(0.01),
        name="follow",
    )(array, *later)


def sample_starts(in_ref, rows):
    ids = in_ref[:, 3 * rows:, :].astype(F32)
    return [
        jnp.sum(jnp.where(ids < s, 1.0, 0.0)).astype(jnp.int32) // SEG_ROWS for s in (1, 2, 3)
    ]


def sample_of(position, starts):
    return sum(jnp.where(position >= b, 1.0, 0.0) for b in starts)


def tile_range(first, last, starts, total):
    low, high = 0, total
    for b in starts:
        low = jnp.maximum(low, jnp.where(b <= first, b, 0))
        high = jnp.minimum(high, jnp.where(b > last, b, total))
    return low // KT, (high + KT - 1) // KT


def block_rows(ref, index, count, start, rows):
    per = count // rows
    return ref[pl.ds(index * per, per), start:start + rows, :].reshape(count, HD)


def fill_samples(seg_s, starts):
    for i in range(seg_s.shape[0] // 256):
        position = i * 256 + lax.broadcasted_iota(jnp.int32, (256, HD), 0)
        seg_s[i * 256:(i + 1) * 256, :] = sample_of(position, starts)


def masked_scores(k, q, seg_k, seg_q):
    same = jnp.concatenate([seg_k] * (QB // HD), axis=1) == seg_q
    return jnp.where(same, dot(k, q, ((1,), (0,))), LOW)


def forward_kernel(place_ref, in_hbm_ref, *refs):
    outs, (in_ref, out_s, vt_s, seg_s, qt_s, in_sem, out_sems) = refs[-7 - XN:-7], refs[-7:]
    arriving = pltpu.make_async_copy(in_hbm_ref, in_ref, in_sem)
    arriving.start()
    arriving.wait()
    blocks, rows = in_ref.shape[0], 128
    total = blocks * rows
    starts = sample_starts(in_ref, rows)
    fill_samples(seg_s, starts)
    for i in range(blocks):
        vt_s[:, i * rows:(i + 1) * rows] = in_ref[i, 2 * rows:3 * rows, :].T

    def per_block(i, _):
        q = block_rows(in_ref, i, QB, 0, rows)
        first = i * QB
        seg_q = sample_of(first + lax.broadcasted_iota(jnp.int32, (1, QB), 1), starts)
        qt_s[...] = q.T
        begin, end = tile_range(first, first + QB - 1, starts, total)

        def per_tile(t, carry):
            m, l, acc = carry
            here = pl.ds(pl.multiple_of(t * KT, KT), KT)
            s = masked_scores(
                block_rows(in_ref, t, KT, rows, rows), qt_s[...], seg_s[here, :], seg_q
            )
            m_new = jnp.maximum(m, jnp.max(s, axis=0, keepdims=True))
            p = jnp.exp2((s - m_new) * EXP2)
            alpha = jnp.exp2((m - m_new) * EXP2)
            l = l * alpha + jnp.sum(p, axis=0, keepdims=True)
            vt = vt_s[:, pl.ds(pl.multiple_of(t * KT, KT), KT)]
            acc = acc * alpha + dot(vt, p.astype(BF16), ((1,), (0,)))
            return m_new, l, acc

        m0 = jnp.full((1, QB), LOW, F32)
        l0 = jnp.zeros((1, QB), F32)
        m, l, acc = lax.fori_loop(begin, end, per_tile, (m0, l0, jnp.zeros((HD, QB), F32)))
        share = total // XN // QB
        here = pl.ds(pl.multiple_of(i % share * QB, QB), QB)
        out_s[i // share, here, :] = (acc / l).T.astype(BF16)
        return 0

    lax.fori_loop(0, total // QB, per_block, 0)
    leaving = [
        pltpu.make_async_copy(out_s.at[x_at(place_ref, offset)], ref, out_sems.at[n])
        for n, (offset, ref) in enumerate(zip(OFFSETS, outs))
    ]
    for copy in leaving:
        copy.start()
    for copy in leaving:
        copy.wait()


def attention_forward(place, packed, *later):
    total = packed.shape[0] * 128
    return pl.pallas_call(
        forward_kernel,
        out_shape=(jax.ShapeDtypeStruct((total // XN, HD), BF16),) * XN,
        in_specs=[pl.BlockSpec(memory_space=pltpu.SMEM)] + in_hbm(1) + anywhere(later),
        out_specs=tuple(in_hbm(XN)),
        scratch_shapes=[
            pltpu.VMEM(packed.shape, BF16),
            pltpu.VMEM((XN, total // XN, HD), BF16),
            pltpu.VMEM((HD, total), BF16),
            pltpu.VMEM((total, HD), F32),
            pltpu.VMEM((HD, QB), BF16),
            pltpu.SemaphoreType.DMA,
            pltpu.SemaphoreType.DMA((XN,)),
        ],
        compiler_params=params(60),
        cost_estimate=cost(0.2),
        name="attention_forward",
    )(place, packed, *later)


def backward_kernel(place_ref, in_hbm_ref, *refs):
    g_refs = refs[:XN]
    out_ref, in_ref, g_ref, out_s, kt_s, seg_s, qt_s, gt_s, p_s, dp_s, top_s, dk_s, dv_s, *sems = refs[-15:]
    in_sems, out_sem = sems
    packed = pltpu.make_async_copy(in_hbm_ref, in_ref, in_sems.at[XN])
    packed.start()
    blocks, rows = in_ref.shape[0], 128
    arriving = []
    for n, (offset, ref) in enumerate(zip(OFFSETS, g_refs)):
        source = x_at(place_ref, -offset % XN)
        arriving.append(pltpu.make_async_copy(ref, g_ref.at[source], in_sems.at[n]))
        arriving[-1].start()
    total = blocks * rows
    packed.wait()
    starts = sample_starts(in_ref, rows)
    fill_samples(seg_s, starts)
    for i in range(blocks):
        kt_s[:, i * rows:(i + 1) * rows] = in_ref[i, rows:2 * rows, :].T
    dk_s[...] = jnp.zeros_like(dk_s)
    dv_s[...] = jnp.zeros_like(dv_s)
    for copy in arriving:
        copy.wait()

    def per_block(i, _):
        q = block_rows(in_ref, i, QB, 0, rows)
        share = total // XN // QB
        g = g_ref[i // share, pl.ds(pl.multiple_of(i % share * QB, QB), QB), :]
        first = i * QB
        seg_q = sample_of(first + lax.broadcasted_iota(jnp.int32, (1, QB), 1), starts)
        qt_s[...] = q.T
        gt_s[...] = g.T
        begin, end = tile_range(first, first + QB - 1, starts, total)

        def scores(t, carry):
            m, l, d = carry
            here = pl.ds(pl.multiple_of(t * KT, KT), KT)
            s = masked_scores(
                block_rows(in_ref, t, KT, rows, rows), qt_s[...], seg_s[here, :], seg_q
            )
            dp = dot(block_rows(in_ref, t, KT, 2 * rows, rows), gt_s[...], ((1,), (0,)))
            dp_s[here, :] = dp
            m_new = jnp.maximum(m, jnp.max(s, axis=0, keepdims=True))
            p = jnp.exp2((s - m_new) * EXP2)
            p_s[here, :] = p
            top_s[t] = m_new
            alpha = jnp.exp2((m - m_new) * EXP2)
            l = l * alpha + jnp.sum(p, axis=0, keepdims=True)
            d = d * alpha + jnp.sum(p * dp, axis=0, keepdims=True)
            return m_new, l, d

        zero = jnp.zeros((1, QB), F32)
        m, l, d = lax.fori_loop(begin, end, scores, (jnp.full((1, QB), LOW, F32), zero, zero))
        inverse = 1.0 / l
        delta = d * inverse

        def grads(t, acc):
            here = pl.ds(pl.multiple_of(t * KT, KT), KT)
            p = p_s[here, :] * (jnp.exp2((top_s[t] - m) * EXP2) * inverse)
            ds = (p * (dp_s[here, :] - delta)).astype(BF16)
            dv_s[here, :] += dot(p.astype(BF16), g, ((1,), (0,)))
            dk_s[here, :] += dot(ds, q, ((1,), (0,)))
            return acc + dot(kt_s[:, here], ds, ((1,), (0,)))

        acc = lax.fori_loop(begin, end, grads, jnp.zeros((HD, QB), F32))
        dq = (acc * SCALE).T.astype(BF16)
        per = QB // rows
        out_s[pl.ds(i * per, per), 0:rows, :] = dq.reshape(per, rows, HD)
        return 0

    lax.fori_loop(0, total // QB, per_block, 0)
    for i in range(blocks):
        here = slice(i * rows, (i + 1) * rows)
        out_s[i, rows:2 * rows, :] = (dk_s[here, :] * SCALE).astype(BF16)
        out_s[i, 2 * rows:3 * rows, :] = dv_s[here, :].astype(BF16)
        pltpu.make_async_copy(out_s.at[i], out_ref.at[i], out_sem).start()
    pltpu.make_async_copy(out_s, out_ref, out_sem).wait()


def attention_backward(place, packed, grads, *later):
    blocks = packed.shape[0]
    total = blocks * 128
    return pl.pallas_call(
        backward_kernel,
        out_shape=jax.ShapeDtypeStruct((blocks, 3 * 128, HD), BF16),
        in_specs=[pl.BlockSpec(memory_space=pltpu.SMEM)]
        + in_hbm(1 + XN)
        + anywhere(later),
        out_specs=in_hbm(1)[0],
        scratch_shapes=[
            pltpu.VMEM(packed.shape, BF16),
            pltpu.VMEM((XN, total // XN, HD), BF16),
            pltpu.VMEM((blocks, 3 * 128, HD), BF16),
            pltpu.VMEM((HD, total), BF16),
            pltpu.VMEM((total, HD), F32),
            pltpu.VMEM((HD, QB), BF16),
            pltpu.VMEM((HD, QB), BF16),
            pltpu.VMEM((total, QB), F32),
            pltpu.VMEM((total, QB), F32),
            pltpu.VMEM((total // KT, 1, QB), F32),
            pltpu.VMEM((total, HD), F32),
            pltpu.VMEM((total, HD), F32),
            pltpu.SemaphoreType.DMA((XN + 1,)),
            pltpu.SemaphoreType.DMA,
        ],
        compiler_params=params(60),
        cost_estimate=cost(30),
        name="attention_backward",
    )(place, packed, *grads, *later)


def grad_kernel(place_ref, *refs):
    grads, pieces, outs = refs[:PER_X], refs[PER_X:PER_X + XN], refs[-5 - XN:-5]
    g_s, w_s, out_s, in_sems, out_sems = refs[-5:]
    rows = grads[0].shape[0]
    arriving = []
    for bits, ref in enumerate(grads):
        target = g_s.at[rows_at(place_ref, bits, rows), :]
        arriving.append(pltpu.make_async_copy(ref, target, in_sems.at[bits]))
    for j, ref in enumerate(pieces):
        target = w_s.at[j * HD:(j + 1) * HD, :]
        arriving.append(pltpu.make_async_copy(ref, target, in_sems.at[PER_X + j]))
    for copy in arriving:
        copy.start()
    for copy in arriving:
        copy.wait()
    leaving = []
    for j in range(0, XN, 2):
        r = dot(g_s[...], w_s[j * HD:(j + 2) * HD, :], ((1,), (1,))).astype(BF16)
        out_s[j] = r[:, :HD]
        out_s[j + 1] = r[:, HD:]
        for n in (j, j + 1):
            leaving.append(pltpu.make_async_copy(out_s.at[n], outs[n], out_sems.at[n]))
            leaving[-1].start()
    for copy in leaving:
        copy.wait()


def attention_grad(place, grads, pieces, *later):
    rows, width = grads[0].shape
    return pl.pallas_call(
        grad_kernel,
        out_shape=(jax.ShapeDtypeStruct((PER_X * rows, HD), BF16),) * XN,
        in_specs=[pl.BlockSpec(memory_space=pltpu.SMEM)] + in_hbm(PER_X + XN) + anywhere(later),
        out_specs=tuple(in_hbm(XN)),
        scratch_shapes=[
            pltpu.VMEM((PER_X * rows, width), BF16),
            pltpu.VMEM((XN * HD, width), BF16),
            pltpu.VMEM((XN, PER_X * rows, HD), BF16),
            pltpu.SemaphoreType.DMA((PER_X + XN,)),
            pltpu.SemaphoreType.DMA((XN,)),
        ],
        compiler_params=params(60),
        cost_estimate=cost(0.2),
        name="attention_grad",
    )(place, *grads, *pieces, *later)


def project_kernel(place_ref, *refs):
    attns, pieces, outs = refs[:XN], refs[XN:2 * XN], refs[-11:-8]
    a_in, w_s, a_s, own_s, across_s, send_s, in_sems, out_sems = refs[-8:]
    rows, width = outs[0].shape
    arriving = []
    for j in range(XN):
        target = w_s.at[j * HD:(j + 1) * HD, :]
        arriving.append(pltpu.make_async_copy(attns[j], a_in.at[j], in_sems.at[j]))
        arriving.append(pltpu.make_async_copy(pieces[j], target, in_sems.at[XN + j]))
    for copy in arriving:
        copy.start()
    for copy in arriving:
        copy.wait()
    for n, bits in enumerate((0, 2, 1, 3)):
        for j in range(XN):
            a_s[n * rows:(n + 1) * rows, j * HD:(j + 1) * HD] = a_in[
                j, rows_at(place_ref, bits, rows), :
            ]
    step = 512
    for n in range(0, width, step):
        cols = slice(n, n + step)
        acc = dot(a_s[...], w_s[:, cols], ((1,), (0,)))
        own_s[:, cols] = acc[:rows]
        across_s[:, cols] = acc[rows:2 * rows]
        send_s[:, cols] = acc[2 * rows:].astype(BF16)
        for k, (result, out) in enumerate(zip((own_s, across_s, send_s), outs)):
            pltpu.make_async_copy(result.at[:, cols], out.at[:, cols], out_sems.at[k]).start()
    for k, (result, out) in enumerate(zip((own_s, across_s, send_s), outs)):
        pltpu.make_async_copy(result, out, out_sems.at[k]).wait()


def project(place, attns, pieces, *later):
    rows, width = pieces[0].shape
    shapes = (((rows, width), F32), ((rows, width), F32), ((2 * rows, width), BF16))
    return pl.pallas_call(
        project_kernel,
        out_shape=tuple(jax.ShapeDtypeStruct(*shape) for shape in shapes),
        in_specs=[pl.BlockSpec(memory_space=pltpu.SMEM)] + in_hbm(2 * XN) + anywhere(later),
        out_specs=tuple(in_hbm(3)),
        scratch_shapes=[
            pltpu.VMEM((XN, PER_X * rows, HD), BF16),
            pltpu.VMEM((XN * HD, width), BF16),
            pltpu.VMEM((PER_X * rows, XN * HD), BF16),
        ]
        + [pltpu.VMEM(*shape) for shape in shapes]
        + [pltpu.SemaphoreType.DMA((2 * XN,)), pltpu.SemaphoreType.DMA((3,))],
        compiler_params=params(60),
        cost_estimate=cost(0.2),
        name="project",
    )(place, *attns, *pieces, *later)


def unpack_kernel(in_ref, out_ref):
    rows = out_ref.shape[1]
    for h in range(in_ref.shape[0]):
        for t in range(3):
            out_ref[t, :, h * HD:(h + 1) * HD] = in_ref[h, t * rows:(t + 1) * rows, :]


def unpack(received):
    heads, rows = received.shape[0], received.shape[1] // 3
    return pl.pallas_call(
        unpack_kernel,
        out_shape=jax.ShapeDtypeStruct((3, rows, heads * HD), BF16),
        in_specs=whole(1),
        out_specs=whole(1)[0],
        compiler_params=params(24),
        cost_estimate=cost(2),
        name="unpack",
    )(received)


def choose_kernel(section_ref, first_ref, second_ref, *refs):
    out_ref = refs[-1]
    out_ref[...] = jnp.where(section_ref[0] == section_ref[1], first_ref[...], second_ref[...])


def choose(sections, first, second, *later):
    return pl.pallas_call(
        choose_kernel,
        out_shape=jax.ShapeDtypeStruct(first.shape, first.dtype),
        in_specs=[pl.BlockSpec(memory_space=pltpu.SMEM)] + whole(2) + anywhere(later),
        out_specs=whole(1)[0],
        compiler_params=params(16),
        cost_estimate=cost(2),
        name="choose",
    )(sections, first, second, *later)


def shifted(array, axis, by):
    length = lax.axis_size(axis)
    pairs = [(i, i + by) for i in range(length) if 0 <= i + by < length]
    return lax.ppermute(array, axis, pairs)


def rotated(array, axis, by):
    length = lax.axis_size(axis)
    return lax.ppermute(array, axis, [(i, (i + by) % length) for i in range(length)])


def per_sample(seg, table):
    onehot = (seg[:, None] == jnp.arange(table.shape[0], dtype=jnp.int32)[None, :]).astype(F32)
    return jnp.sum(onehot[:, :, None] * table[None, :, :], axis=1)


def exchange(array):
    return lax.all_to_all(array, "seq", 0, 0, tiled=True)


def body(hidden_in, queries, keys, values, segments, gates, out_weight, upstream, fresh, loss_grad):
    section = lax.axis_index("pipe")
    last_section = lax.axis_size("pipe") - 1
    place = lax.axis_index("seq")[None]

    own = out_weight[0]
    pieces = tuple(along_x(own, -offset % XN) for offset in OFFSETS)

    fwd = exchange(pack(queries, keys, values, segments, 0))
    local_seg = segments[0]
    g_scaled = (per_sample(local_seg[1], gates[0, 1]) * upstream[0].astype(F32)).astype(BF16)
    g_across = lax.ppermute(g_scaled, "seq", YSWAP)
    g_core = lax.ppermute(g_scaled, "seq", CORE)
    g_both = lax.ppermute(g_across, "seq", CORE)
    packed = pack(queries, keys, values, segments, 1, g_across, *pieces[1:])
    bwd = exchange(packed)
    gate_tok = per_sample(local_seg[0], gates[0, 0])

    grads = attention_grad(place, (g_scaled, g_core, g_across, g_both), pieces, packed)
    turned = follow(upstream[0], grads[0])
    moved = shifted(turned, "pipe", -1)
    attns = attention_forward(place, fwd, grads[0], gate_tok, turned)
    grads = tuple(along_x(g, o) for g, o in zip(grads, OFFSETS))
    attns = (attns[0], follow(attns[1], *grads[1:])) + attns[2:]
    attns = tuple(along_x(a, o) for a, o in zip(attns, OFFSETS))

    attns = (attns[0], attns[2], attns[1], attns[3])
    part, part_across, part_send = project(place, attns, pieces, bwd, moved)
    received = lax.ppermute(part_send, "seq", CORE)
    rows = part.shape[0]
    across = (part_across + received[rows:].astype(F32)).astype(BF16)
    grads = attention_backward(place, bwd, grads, across)
    across = lax.ppermute(across, "seq", YSWAP)
    proj = part + received[:rows].astype(F32) + across.astype(F32)
    section_out = (hidden_in[0].astype(F32) + gate_tok * proj).astype(BF16)
    section_out = jnp.where(section == last_section, fresh, section_out)
    next_act = rotated(section_out, "pipe", 1)

    sections = jnp.stack([section, last_section * jnp.ones_like(section)])
    next_grad = choose(sections, loss_grad, moved)
    qkv_grads = unpack(exchange(grads))
    return (next_act[None], next_grad[None], qkv_grads[None])


def solution(mesh):
    in_specs = (
        P("pipe", "seq", None),
        P("pipe", None, "seq", None),
        P("pipe", None, "seq", None),
        P("pipe", None, "seq", None),
        P("pipe", None, "seq"),
        P("pipe", None, None, None),
        P("pipe", "seq", None),
        P("pipe", "seq", None),
        P("seq", None),
        P("seq", None),
    )
    out_specs = (P("pipe", "seq", None), P("pipe", "seq", None), P("pipe", None, "seq", None))
    return jax.shard_map(body, mesh=mesh, in_specs=in_specs, out_specs=out_specs, check_vma=False)
```

```python
import functools

import jax
import jax.numpy as jnp
from jax import lax
from jax.experimental import pallas as pl
from jax.experimental.pallas import tpu as pltpu
from jax.sharding import PartitionSpec as P

HD = 128
SCALE = HD ** (-0.5)
EXP2 = SCALE * 1.4426950408889634
LOW = -1e30
QB = 512
KT = 512
SEG_ROWS = 16
F32 = jnp.float32
BF16 = jnp.bfloat16

XN, PER_X = 4, 4
OFFSETS = (0, 3, 1, 2)
PIECES = 5
CORE = [(i, i ^ 1) for i in range(XN * PER_X)]
YSWAP = [(i, i ^ 2) for i in range(XN * PER_X)]


def along_x(array, offset):
    if offset == 0:
        return array
    count = XN * PER_X
    return lax.ppermute(array, "seq", [(i, (i + PER_X * offset) % count) for i in range(count)])


def x_at(place_ref, offset):
    return (place_ref[0] // PER_X + offset) % XN


def rows_at(place_ref, bits, rows):
    return pl.ds(pl.multiple_of(((place_ref[0] % PER_X) ^ bits) * rows, rows), rows)


def params(mib):
    return pltpu.CompilerParams(vmem_limit_bytes=mib * 1024 * 1024)


def whole(count):
    return [pl.BlockSpec(memory_space=pltpu.VMEM)] * count


def anywhere(arrays):
    return [pl.BlockSpec(memory_space=pl.ANY)] * len(arrays)


def in_hbm(count):
    return [pl.BlockSpec(memory_space=pltpu.HBM)] * count


def cost(microseconds):
    return pl.CostEstimate(
        flops=int(microseconds * 1e9), bytes_accessed=0, transcendentals=0
    )


def dot(a, b, dims):
    return lax.dot_general(a, b, (dims, ((), ())), preferred_element_type=F32)


def pack_kernel(seg_ref, q_ref, k_ref, v_ref, *refs):
    out_ref = refs[-1]
    rows = q_ref.shape[0]
    ids = jnp.broadcast_to(seg_ref[...].astype(F32), (SEG_ROWS, HD)).astype(BF16)
    for h in range(out_ref.shape[0]):
        cols = slice(h * HD, (h + 1) * HD)
        out_ref[h, 0:rows, :] = q_ref[:, cols]
        out_ref[h, rows:2 * rows, :] = k_ref[:, cols]
        out_ref[h, 2 * rows:3 * rows, :] = v_ref[:, cols]
        out_ref[h, 3 * rows:, :] = ids


def pack(queries, keys, values, segments, batch, *later):
    rows, width = queries.shape[2], queries.shape[3]
    heads = width // HD
    height = 3 * rows + SEG_ROWS
    block = pl.BlockSpec((None, None, rows, width), lambda i: (0, batch, 0, 0))
    return pl.pallas_call(
        pack_kernel,
        grid=(1,),
        out_shape=jax.ShapeDtypeStruct((heads, height, HD), BF16),
        in_specs=[pl.BlockSpec((1, rows), lambda i: (0, 0)), block, block, block]
        + anywhere(later),
        out_specs=pl.BlockSpec((heads, height, HD), lambda i: (0, 0, 0)),
        compiler_params=params(60),
        cost_estimate=cost(2),
        name="pack",
    )(segments[0, batch][None], queries, keys, values, *later)


def follow_kernel(array_ref, *refs):
    pass


def follow(array, *later):
    return pl.pallas_call(
        follow_kernel,
        out_shape=jax.ShapeDtypeStruct(array.shape, array.dtype),
        in_specs=anywhere((array,) + later),
        out_specs=pl.BlockSpec(memory_space=pl.ANY),
        input_output_aliases={0: 0},
        compiler_params=params(1),
        cost_estimate=cost(0.01),
        name="follow",
    )(array, *later)


def sample_starts(in_ref, rows):
    ids = in_ref[:, 3 * rows:, :].astype(F32)
    return [
        jnp.sum(jnp.where(ids < s, 1.0, 0.0)).astype(jnp.int32) // SEG_ROWS for s in (1, 2, 3)
    ]


def sample_of(position, starts):
    return sum(jnp.where(position >= b, 1.0, 0.0) for b in starts)


def tile_range(first, last, starts, total):
    low, high = 0, total
    for b in starts:
        low = jnp.maximum(low, jnp.where(b <= first, b, 0))
        high = jnp.minimum(high, jnp.where(b > last, b, total))
    return low // KT, (high + KT - 1) // KT


def block_rows(ref, index, count, start, rows):
    per = count // rows
    return ref[pl.ds(index * per, per), start:start + rows, :].reshape(count, HD)


def fill_samples(seg_s, starts):
    for i in range(seg_s.shape[0] // 256):
        position = i * 256 + lax.broadcasted_iota(jnp.int32, (256, HD), 0)
        seg_s[i * 256:(i + 1) * 256, :] = sample_of(position, starts)


def masked_scores(k, q, seg_k, seg_q):
    same = jnp.concatenate([seg_k] * (QB // HD), axis=1) == seg_q
    return jnp.where(same, dot(k, q, ((1,), (0,))), LOW)


def forward_kernel(place_ref, in_hbm_ref, *refs):
    outs, (in_ref, out_s, vt_s, seg_s, qt_s, in_sem, out_sems) = refs[-7 - XN:-7], refs[-7:]
    arriving = pltpu.make_async_copy(in_hbm_ref, in_ref, in_sem)
    arriving.start()
    arriving.wait()
    blocks, rows = in_ref.shape[0], 128
    total = blocks * rows
    starts = sample_starts(in_ref, rows)
    fill_samples(seg_s, starts)
    for i in range(blocks):
        vt_s[:, i * rows:(i + 1) * rows] = in_ref[i, 2 * rows:3 * rows, :].T

    def per_block(i, _):
        q = block_rows(in_ref, i, QB, 0, rows)
        first = i * QB
        seg_q = sample_of(first + lax.broadcasted_iota(jnp.int32, (1, QB), 1), starts)
        qt_s[...] = q.T
        begin, end = tile_range(first, first + QB - 1, starts, total)

        def per_tile(t, carry):
            m, l, acc = carry
            here = pl.ds(pl.multiple_of(t * KT, KT), KT)
            s = masked_scores(
                block_rows(in_ref, t, KT, rows, rows), qt_s[...], seg_s[here, :], seg_q
            )
            m_new = jnp.maximum(m, jnp.max(s, axis=0, keepdims=True))
            p = jnp.exp2((s - m_new) * EXP2)
            alpha = jnp.exp2((m - m_new) * EXP2)
            l = l * alpha + jnp.sum(p, axis=0, keepdims=True)
            vt = vt_s[:, pl.ds(pl.multiple_of(t * KT, KT), KT)]
            acc = acc * alpha + dot(vt, p.astype(BF16), ((1,), (0,)))
            return m_new, l, acc

        m0 = jnp.full((1, QB), LOW, F32)
        l0 = jnp.zeros((1, QB), F32)
        m, l, acc = lax.fori_loop(begin, end, per_tile, (m0, l0, jnp.zeros((HD, QB), F32)))
        share = total // XN // QB
        here = pl.ds(pl.multiple_of(i % share * QB, QB), QB)
        out_s[i // share, here, :] = (acc / l).T.astype(BF16)
        return 0

    lax.fori_loop(0, total // QB, per_block, 0)
    leaving = [
        pltpu.make_async_copy(out_s.at[x_at(place_ref, offset)], ref, out_sems.at[n])
        for n, (offset, ref) in enumerate(zip(OFFSETS, outs))
    ]
    for copy in leaving:
        copy.start()
    for copy in leaving:
        copy.wait()


def attention_forward(place, packed, *later):
    total = packed.shape[0] * 128
    return pl.pallas_call(
        forward_kernel,
        out_shape=(jax.ShapeDtypeStruct((total // XN, HD), BF16),) * XN,
        in_specs=[pl.BlockSpec(memory_space=pltpu.SMEM)] + in_hbm(1) + anywhere(later),
        out_specs=tuple(in_hbm(XN)),
        scratch_shapes=[
            pltpu.VMEM(packed.shape, BF16),
            pltpu.VMEM((XN, total // XN, HD), BF16),
            pltpu.VMEM((HD, total), BF16),
            pltpu.VMEM((total, HD), F32),
            pltpu.VMEM((HD, QB), BF16),
            pltpu.SemaphoreType.DMA,
            pltpu.SemaphoreType.DMA((XN,)),
        ],
        compiler_params=params(60),
        cost_estimate=cost(0.2),
        name="attention_forward",
    )(place, packed, *later)


def backward_kernel(place_ref, in_hbm_ref, *refs):
    g_refs = refs[:XN]
    out_ref, in_ref, g_ref, out_s, kt_s, seg_s, qt_s, gt_s, p_s, dp_s, top_s, dk_s, dv_s, *sems = refs[-15:]
    in_sems, out_sem = sems
    packed = pltpu.make_async_copy(in_hbm_ref, in_ref, in_sems.at[XN])
    packed.start()
    blocks, rows = in_ref.shape[0], 128
    arriving = []
    for n, (offset, ref) in enumerate(zip(OFFSETS, g_refs)):
        source = x_at(place_ref, -offset % XN)
        arriving.append(pltpu.make_async_copy(ref, g_ref.at[source], in_sems.at[n]))
        arriving[-1].start()
    total = blocks * rows
    packed.wait()
    starts = sample_starts(in_ref, rows)
    fill_samples(seg_s, starts)
    for i in range(blocks):
        kt_s[:, i * rows:(i + 1) * rows] = in_ref[i, rows:2 * rows, :].T
    dk_s[...] = jnp.zeros_like(dk_s)
    dv_s[...] = jnp.zeros_like(dv_s)
    for copy in arriving:
        copy.wait()

    def per_block(i, _):
        q = block_rows(in_ref, i, QB, 0, rows)
        share = total // XN // QB
        g = g_ref[i // share, pl.ds(pl.multiple_of(i % share * QB, QB), QB), :]
        first = i * QB
        seg_q = sample_of(first + lax.broadcasted_iota(jnp.int32, (1, QB), 1), starts)
        qt_s[...] = q.T
        gt_s[...] = g.T
        begin, end = tile_range(first, first + QB - 1, starts, total)

        def scores(t, carry):
            m, l, d = carry
            here = pl.ds(pl.multiple_of(t * KT, KT), KT)
            s = masked_scores(
                block_rows(in_ref, t, KT, rows, rows), qt_s[...], seg_s[here, :], seg_q
            )
            dp = dot(block_rows(in_ref, t, KT, 2 * rows, rows), gt_s[...], ((1,), (0,)))
            dp_s[here, :] = dp
            m_new = jnp.maximum(m, jnp.max(s, axis=0, keepdims=True))
            p = jnp.exp2((s - m_new) * EXP2)
            p_s[here, :] = p
            top_s[t] = m_new
            alpha = jnp.exp2((m - m_new) * EXP2)
            l = l * alpha + jnp.sum(p, axis=0, keepdims=True)
            d = d * alpha + jnp.sum(p * dp, axis=0, keepdims=True)
            return m_new, l, d

        zero = jnp.zeros((1, QB), F32)
        m, l, d = lax.fori_loop(begin, end, scores, (jnp.full((1, QB), LOW, F32), zero, zero))
        inverse = 1.0 / l
        delta = d * inverse

        def grads(t, acc):
            here = pl.ds(pl.multiple_of(t * KT, KT), KT)
            p = p_s[here, :] * (jnp.exp2((top_s[t] - m) * EXP2) * inverse)
            ds = (p * (dp_s[here, :] - delta)).astype(BF16)
            dv_s[here, :] += dot(p.astype(BF16), g, ((1,), (0,)))
            dk_s[here, :] += dot(ds, q, ((1,), (0,)))
            return acc + dot(kt_s[:, here], ds, ((1,), (0,)))

        acc = lax.fori_loop(begin, end, grads, jnp.zeros((HD, QB), F32))
        dq = (acc * SCALE).T.astype(BF16)
        per = QB // rows
        out_s[pl.ds(i * per, per), 0:rows, :] = dq.reshape(per, rows, HD)
        return 0

    lax.fori_loop(0, total // QB, per_block, 0)
    for i in range(blocks):
        here = slice(i * rows, (i + 1) * rows)
        out_s[i, rows:2 * rows, :] = (dk_s[here, :] * SCALE).astype(BF16)
        out_s[i, 2 * rows:3 * rows, :] = dv_s[here, :].astype(BF16)
        pltpu.make_async_copy(out_s.at[i], out_ref.at[i], out_sem).start()
    pltpu.make_async_copy(out_s, out_ref, out_sem).wait()


def attention_backward(place, packed, grads, *later):
    blocks = packed.shape[0]
    total = blocks * 128
    return pl.pallas_call(
        backward_kernel,
        out_shape=jax.ShapeDtypeStruct((blocks, 3 * 128, HD), BF16),
        in_specs=[pl.BlockSpec(memory_space=pltpu.SMEM)]
        + in_hbm(1 + XN)
        + anywhere(later),
        out_specs=in_hbm(1)[0],
        scratch_shapes=[
            pltpu.VMEM(packed.shape, BF16),
            pltpu.VMEM((XN, total // XN, HD), BF16),
            pltpu.VMEM((blocks, 3 * 128, HD), BF16),
            pltpu.VMEM((HD, total), BF16),
            pltpu.VMEM((total, HD), F32),
            pltpu.VMEM((HD, QB), BF16),
            pltpu.VMEM((HD, QB), BF16),
            pltpu.VMEM((total, QB), F32),
            pltpu.VMEM((total, QB), F32),
            pltpu.VMEM((total // KT, 1, QB), F32),
            pltpu.VMEM((total, HD), F32),
            pltpu.VMEM((total, HD), F32),
            pltpu.SemaphoreType.DMA((XN + 1,)),
            pltpu.SemaphoreType.DMA,
        ],
        compiler_params=params(60),
        cost_estimate=cost(30),
        name="attention_backward",
    )(place, packed, *grads, *later)


def weight_copies(pieces, w_s, sems, first_sem):
    copies, row = [], 0
    for j, ref in enumerate(pieces):
        target = w_s.at[row:row + ref.shape[0], :]
        copies.append(pltpu.make_async_copy(ref, target, sems.at[first_sem + j]))
        row += ref.shape[0]
    return copies


def grad_kernel(place_ref, *refs):
    grads, pieces, outs = refs[:PER_X], refs[PER_X:PER_X + PIECES], refs[-5 - XN:-5]
    g_s, w_s, out_s, in_sems, out_sems = refs[-5:]
    rows = grads[0].shape[0]
    arriving = []
    for bits, ref in enumerate(grads):
        target = g_s.at[rows_at(place_ref, bits, rows), :]
        arriving.append(pltpu.make_async_copy(ref, target, in_sems.at[bits]))
    arriving += weight_copies(pieces, w_s, in_sems, PER_X)
    for copy in arriving:
        copy.start()
    for copy in arriving:
        copy.wait()
    leaving = []
    for j in range(0, XN, 2):
        r = dot(g_s[...], w_s[j * HD:(j + 2) * HD, :], ((1,), (1,))).astype(BF16)
        out_s[j] = r[:, :HD]
        out_s[j + 1] = r[:, HD:]
        for n in (j, j + 1):
            leaving.append(pltpu.make_async_copy(out_s.at[n], outs[n], out_sems.at[n]))
            leaving[-1].start()
    for copy in leaving:
        copy.wait()


def attention_grad(place, grads, pieces, *later):
    rows, width = grads[0].shape
    return pl.pallas_call(
        grad_kernel,
        out_shape=(jax.ShapeDtypeStruct((PER_X * rows, HD), BF16),) * XN,
        in_specs=[pl.BlockSpec(memory_space=pltpu.SMEM)] + in_hbm(PER_X + PIECES) + anywhere(later),
        out_specs=tuple(in_hbm(XN)),
        scratch_shapes=[
            pltpu.VMEM((PER_X * rows, width), BF16),
            pltpu.VMEM((XN * HD, width), BF16),
            pltpu.VMEM((XN, PER_X * rows, HD), BF16),
            pltpu.SemaphoreType.DMA((PER_X + PIECES,)),
            pltpu.SemaphoreType.DMA((XN,)),
        ],
        compiler_params=params(60),
        cost_estimate=cost(0.2),
        name="attention_grad",
    )(place, *grads, *pieces, *later)


def project_kernel(place_ref, *refs):
    attns, pieces, outs = refs[:XN], refs[XN:XN + PIECES], refs[-11:-8]
    a_in, w_s, a_s, own_s, across_s, send_s, in_sems, out_sems = refs[-8:]
    rows, width = outs[0].shape
    arriving = weight_copies(pieces, w_s, in_sems, XN)
    for j in range(XN):
        arriving.append(pltpu.make_async_copy(attns[j], a_in.at[j], in_sems.at[j]))
    for copy in arriving:
        copy.start()
    for copy in arriving:
        copy.wait()
    for n, bits in enumerate((0, 2, 1, 3)):
        for j in range(XN):
            a_s[n * rows:(n + 1) * rows, j * HD:(j + 1) * HD] = a_in[
                j, rows_at(place_ref, bits, rows), :
            ]
    step = 512
    for n in range(0, width, step):
        cols = slice(n, n + step)
        acc = dot(a_s[...], w_s[:, cols], ((1,), (0,)))
        own_s[:, cols] = acc[:rows]
        across_s[:, cols] = acc[rows:2 * rows]
        send_s[:, cols] = acc[2 * rows:].astype(BF16)
        for k, (result, out) in enumerate(zip((own_s, across_s, send_s), outs)):
            pltpu.make_async_copy(result.at[:, cols], out.at[:, cols], out_sems.at[k]).start()
    for k, (result, out) in enumerate(zip((own_s, across_s, send_s), outs)):
        pltpu.make_async_copy(result, out, out_sems.at[k]).wait()


def project(place, attns, pieces, *later):
    rows, width = pieces[0].shape
    shapes = (((rows, width), F32), ((rows, width), F32), ((2 * rows, width), BF16))
    return pl.pallas_call(
        project_kernel,
        out_shape=tuple(jax.ShapeDtypeStruct(*shape) for shape in shapes),
        in_specs=[pl.BlockSpec(memory_space=pltpu.SMEM)] + in_hbm(XN + PIECES) + anywhere(later),
        out_specs=tuple(in_hbm(3)),
        scratch_shapes=[
            pltpu.VMEM((XN, PER_X * rows, HD), BF16),
            pltpu.VMEM((XN * HD, width), BF16),
            pltpu.VMEM((PER_X * rows, XN * HD), BF16),
        ]
        + [pltpu.VMEM(*shape) for shape in shapes]
        + [pltpu.SemaphoreType.DMA((XN + PIECES,)), pltpu.SemaphoreType.DMA((3,))],
        compiler_params=params(60),
        cost_estimate=cost(0.2),
        name="project",
    )(place, *attns, *pieces, *later)


def unpack_kernel(in_ref, out_ref):
    rows = out_ref.shape[1]
    for h in range(in_ref.shape[0]):
        for t in range(3):
            out_ref[t, :, h * HD:(h + 1) * HD] = in_ref[h, t * rows:(t + 1) * rows, :]


def unpack(received):
    heads, rows = received.shape[0], received.shape[1] // 3
    return pl.pallas_call(
        unpack_kernel,
        out_shape=jax.ShapeDtypeStruct((3, rows, heads * HD), BF16),
        in_specs=whole(1),
        out_specs=whole(1)[0],
        compiler_params=params(24),
        cost_estimate=cost(2),
        name="unpack",
    )(received)


def choose_kernel(section_ref, first_ref, second_ref, *refs):
    out_ref = refs[-1]
    out_ref[...] = jnp.where(section_ref[0] == section_ref[1], first_ref[...], second_ref[...])


def choose(sections, first, second, *later):
    return pl.pallas_call(
        choose_kernel,
        out_shape=jax.ShapeDtypeStruct(first.shape, first.dtype),
        in_specs=[pl.BlockSpec(memory_space=pltpu.SMEM)] + whole(2) + anywhere(later),
        out_specs=whole(1)[0],
        compiler_params=params(16),
        cost_estimate=cost(2),
        name="choose",
    )(sections, first, second, *later)


def settle_kernel(in_ref, out_ref):
    out_ref[...] = in_ref[...]


def settle(array):
    return pl.pallas_call(
        settle_kernel,
        out_shape=jax.ShapeDtypeStruct(array.shape, array.dtype),
        in_specs=whole(1),
        out_specs=whole(1)[0],
        compiler_params=params(8),
        cost_estimate=cost(0.2),
        name="settle",
    )(array)


def rotated(array, axis, by):
    length = lax.axis_size(axis)
    return lax.ppermute(array, axis, [(i, (i + by) % length) for i in range(length)])


def per_sample(seg, table):
    onehot = (seg[:, None] == jnp.arange(table.shape[0], dtype=jnp.int32)[None, :]).astype(F32)
    return jnp.sum(onehot[:, :, None] * table[None, :, :], axis=1)


def exchange(array):
    return lax.all_to_all(array, "seq", 0, 0, tiled=True)


def body(hidden_in, queries, keys, values, segments, gates, out_weight, upstream, fresh, loss_grad):
    section = lax.axis_index("pipe")
    last_section = lax.axis_size("pipe") - 1
    place = lax.axis_index("seq")[None]

    own = out_weight[0]
    left, right = along_x(own, 1), along_x(own, XN - 1)
    half = own.shape[0] // 2
    pieces = (own, left, right, along_x(left[:half], 1), along_x(right[half:], XN - 1))

    fwd = exchange(pack(queries, keys, values, segments, 0))
    local_seg = segments[0]
    g_scaled = (per_sample(local_seg[1], gates[0, 1]) * upstream[0].astype(F32)).astype(BF16)
    g_across = lax.ppermute(g_scaled, "seq", YSWAP)
    g_core = lax.ppermute(g_scaled, "seq", CORE)
    g_both = lax.ppermute(g_across, "seq", CORE)
    gate_tok = per_sample(local_seg[0], gates[0, 0])
    grads = attention_grad(place, (g_scaled, g_core, g_across, g_both), pieces)
    packed = pack(queries, keys, values, segments, 1, grads[0], gate_tok)
    bwd = exchange(packed)

    sections = jnp.stack([section, jnp.zeros_like(section)])
    turned = choose(sections, loss_grad, upstream[0], fwd)
    moved = rotated(turned, "pipe", -1)
    attns = attention_forward(place, fwd, grads[0], gate_tok, turned)
    grads = tuple(along_x(g, o) for g, o in zip(grads, OFFSETS))
    attns = (attns[0], follow(attns[1], *grads[1:])) + attns[2:]
    attns = tuple(along_x(a, o) for a, o in zip(attns, OFFSETS))

    attns = (attns[0], attns[2], attns[1], attns[3])
    part, part_across, part_send = project(place, attns, pieces, bwd, moved)
    received = lax.ppermute(part_send, "seq", CORE)
    rows = part.shape[0]
    across = (part_across + received[rows:].astype(F32)).astype(BF16)
    grads = attention_backward(place, bwd, grads, across)
    across = lax.ppermute(across, "seq", YSWAP)
    proj = part + received[:rows].astype(F32) + across.astype(F32)
    section_out = (hidden_in[0].astype(F32) + gate_tok * proj).astype(BF16)
    section_out = jnp.where(section == last_section, fresh, section_out)
    next_act = rotated(section_out, "pipe", 1)

    qkv_grads = unpack(exchange(grads))
    return (next_act[None], settle(moved)[None], qkv_grads[None])


def solution(mesh):
    in_specs = (
        P("pipe", "seq", None),
        P("pipe", None, "seq", None),
        P("pipe", None, "seq", None),
        P("pipe", None, "seq", None),
        P("pipe", None, "seq"),
        P("pipe", None, None, None),
        P("pipe", "seq", None),
        P("pipe", "seq", None),
        P("seq", None),
        P("seq", None),
    )
    out_specs = (P("pipe", "seq", None), P("pipe", "seq", None), P("pipe", None, "seq", None))
    return jax.shard_map(body, mesh=mesh, in_specs=in_specs, out_specs=out_specs, check_vma=False)
```

```python
import functools

import jax
import jax.numpy as jnp
from jax import lax
from jax.experimental import pallas as pl
from jax.experimental.pallas import tpu as pltpu
from jax.sharding import PartitionSpec as P

HD = 128
SCALE = HD ** (-0.5)
EXP2 = SCALE * 1.4426950408889634
LOW = -1e30
QB = 512
KT = 512
SEG_ROWS = 16
F32 = jnp.float32
BF16 = jnp.bfloat16

XN, PER_X = 4, 4
OFFSETS = (0, 3, 1, 2)
PIECES = XN
CORE = [(i, i ^ 1) for i in range(XN * PER_X)]
YSWAP = [(i, i ^ 2) for i in range(XN * PER_X)]


def along_x(array, offset):
    if offset == 0:
        return array
    count = XN * PER_X
    return lax.ppermute(array, "seq", [(i, (i + PER_X * offset) % count) for i in range(count)])


def x_at(place_ref, offset):
    return (place_ref[0] // PER_X + offset) % XN


def rows_at(place_ref, bits, rows):
    return pl.ds(pl.multiple_of(((place_ref[0] % PER_X) ^ bits) * rows, rows), rows)


def params(mib):
    return pltpu.CompilerParams(vmem_limit_bytes=mib * 1024 * 1024)


def whole(count):
    return [pl.BlockSpec(memory_space=pltpu.VMEM)] * count


def anywhere(arrays):
    return [pl.BlockSpec(memory_space=pl.ANY)] * len(arrays)


def in_hbm(count):
    return [pl.BlockSpec(memory_space=pltpu.HBM)] * count


def cost(microseconds):
    return pl.CostEstimate(
        flops=int(microseconds * 1e9), bytes_accessed=0, transcendentals=0
    )


def dot(a, b, dims):
    return lax.dot_general(a, b, (dims, ((), ())), preferred_element_type=F32)


def pack_kernel(seg_ref, q_ref, k_ref, v_ref, *refs):
    out_ref = refs[-1]
    rows = q_ref.shape[0]
    ids = jnp.broadcast_to(seg_ref[...].astype(F32), (SEG_ROWS, HD)).astype(BF16)
    for h in range(out_ref.shape[0]):
        cols = slice(h * HD, (h + 1) * HD)
        out_ref[h, 0:rows, :] = q_ref[:, cols]
        out_ref[h, rows:2 * rows, :] = k_ref[:, cols]
        out_ref[h, 2 * rows:3 * rows, :] = v_ref[:, cols]
        out_ref[h, 3 * rows:, :] = ids


def pack(queries, keys, values, segments, batch, *later):
    rows, width = queries.shape[2], queries.shape[3]
    heads = width // HD
    height = 3 * rows + SEG_ROWS
    block = pl.BlockSpec((None, None, rows, width), lambda i: (0, batch, 0, 0))
    return pl.pallas_call(
        pack_kernel,
        grid=(1,),
        out_shape=jax.ShapeDtypeStruct((heads, height, HD), BF16),
        in_specs=[pl.BlockSpec((1, rows), lambda i: (0, 0)), block, block, block]
        + anywhere(later),
        out_specs=pl.BlockSpec((heads, height, HD), lambda i: (0, 0, 0)),
        compiler_params=params(60),
        cost_estimate=cost(2),
        name="pack",
    )(segments[0, batch][None], queries, keys, values, *later)


def follow_kernel(array_ref, *refs):
    pass


def follow(array, *later):
    return pl.pallas_call(
        follow_kernel,
        out_shape=jax.ShapeDtypeStruct(array.shape, array.dtype),
        in_specs=anywhere((array,) + later),
        out_specs=pl.BlockSpec(memory_space=pl.ANY),
        input_output_aliases={0: 0},
        compiler_params=params(1),
        cost_estimate=cost(0.01),
        name="follow",
    )(array, *later)


def sample_starts(in_ref, rows):
    ids = in_ref[:, 3 * rows:, :].astype(F32)
    return [
        jnp.sum(jnp.where(ids < s, 1.0, 0.0)).astype(jnp.int32) // SEG_ROWS for s in (1, 2, 3)
    ]


def sample_of(position, starts):
    return sum(jnp.where(position >= b, 1.0, 0.0) for b in starts)


def tile_range(first, last, starts, total):
    low, high = 0, total
    for b in starts:
        low = jnp.maximum(low, jnp.where(b <= first, b, 0))
        high = jnp.minimum(high, jnp.where(b > last, b, total))
    return low // KT, (high + KT - 1) // KT


def block_rows(ref, index, count, start, rows):
    per = count // rows
    return ref[pl.ds(index * per, per), start:start + rows, :].reshape(count, HD)


def fill_samples(seg_s, starts):
    for i in range(seg_s.shape[0] // 256):
        position = i * 256 + lax.broadcasted_iota(jnp.int32, (256, HD), 0)
        seg_s[i * 256:(i + 1) * 256, :] = sample_of(position, starts)


def masked_scores(k, q, seg_k, seg_q):
    same = jnp.concatenate([seg_k] * (QB // HD), axis=1) == seg_q
    return jnp.where(same, dot(k, q, ((1,), (0,))), LOW)


def forward_kernel(place_ref, in_hbm_ref, *refs):
    outs, (in_ref, out_s, vt_s, seg_s, qt_s, in_sem, out_sems) = refs[-7 - XN:-7], refs[-7:]
    arriving = pltpu.make_async_copy(in_hbm_ref, in_ref, in_sem)
    arriving.start()
    arriving.wait()
    blocks, rows = in_ref.shape[0], 128
    total = blocks * rows
    starts = sample_starts(in_ref, rows)
    fill_samples(seg_s, starts)
    for i in range(blocks):
        vt_s[:, i * rows:(i + 1) * rows] = in_ref[i, 2 * rows:3 * rows, :].T

    def per_block(i, _):
        q = block_rows(in_ref, i, QB, 0, rows)
        first = i * QB
        seg_q = sample_of(first + lax.broadcasted_iota(jnp.int32, (1, QB), 1), starts)
        qt_s[...] = q.T
        begin, end = tile_range(first, first + QB - 1, starts, total)

        def per_tile(t, carry):
            m, l, acc = carry
            here = pl.ds(pl.multiple_of(t * KT, KT), KT)
            s = masked_scores(
                block_rows(in_ref, t, KT, rows, rows), qt_s[...], seg_s[here, :], seg_q
            )
            m_new = jnp.maximum(m, jnp.max(s, axis=0, keepdims=True))
            p = jnp.exp2((s - m_new) * EXP2)
            alpha = jnp.exp2((m - m_new) * EXP2)
            l = l * alpha + jnp.sum(p, axis=0, keepdims=True)
            vt = vt_s[:, pl.ds(pl.multiple_of(t * KT, KT), KT)]
            acc = acc * alpha + dot(vt, p.astype(BF16), ((1,), (0,)))
            return m_new, l, acc

        m0 = jnp.full((1, QB), LOW, F32)
        l0 = jnp.zeros((1, QB), F32)
        m, l, acc = lax.fori_loop(begin, end, per_tile, (m0, l0, jnp.zeros((HD, QB), F32)))
        share = total // XN // QB
        here = pl.ds(pl.multiple_of(i % share * QB, QB), QB)
        out_s[i // share, here, :] = (acc / l).T.astype(BF16)
        return 0

    lax.fori_loop(0, total // QB, per_block, 0)
    leaving = [
        pltpu.make_async_copy(out_s.at[x_at(place_ref, offset)], ref, out_sems.at[n])
        for n, (offset, ref) in enumerate(zip(OFFSETS, outs))
    ]
    for copy in leaving:
        copy.start()
    for copy in leaving:
        copy.wait()


def attention_forward(place, packed, *later):
    total = packed.shape[0] * 128
    return pl.pallas_call(
        forward_kernel,
        out_shape=(jax.ShapeDtypeStruct((total // XN, HD), BF16),) * XN,
        in_specs=[pl.BlockSpec(memory_space=pltpu.SMEM)] + in_hbm(1) + anywhere(later),
        out_specs=tuple(in_hbm(XN)),
        scratch_shapes=[
            pltpu.VMEM(packed.shape, BF16),
            pltpu.VMEM((XN, total // XN, HD), BF16),
            pltpu.VMEM((HD, total), BF16),
            pltpu.VMEM((total, HD), F32),
            pltpu.VMEM((HD, QB), BF16),
            pltpu.SemaphoreType.DMA,
            pltpu.SemaphoreType.DMA((XN,)),
        ],
        compiler_params=params(60),
        cost_estimate=cost(0.2),
        name="attention_forward",
    )(place, packed, *later)


def backward_kernel(place_ref, in_hbm_ref, *refs):
    g_refs = refs[:XN]
    out_ref, in_ref, g_ref, out_s, kt_s, seg_s, qt_s, gt_s, p_s, dp_s, top_s, dk_s, dv_s, *sems = refs[-15:]
    in_sems, out_sem = sems
    packed = pltpu.make_async_copy(in_hbm_ref, in_ref, in_sems.at[XN])
    packed.start()
    blocks, rows = in_ref.shape[0], 128
    arriving = []
    for n, (offset, ref) in enumerate(zip(OFFSETS, g_refs)):
        source = x_at(place_ref, -offset % XN)
        arriving.append(pltpu.make_async_copy(ref, g_ref.at[source], in_sems.at[n]))
        arriving[-1].start()
    total = blocks * rows
    packed.wait()
    starts = sample_starts(in_ref, rows)
    fill_samples(seg_s, starts)
    for i in range(blocks):
        kt_s[:, i * rows:(i + 1) * rows] = in_ref[i, rows:2 * rows, :].T
    dk_s[...] = jnp.zeros_like(dk_s)
    dv_s[...] = jnp.zeros_like(dv_s)
    for copy in arriving:
        copy.wait()

    def per_block(i, _):
        q = block_rows(in_ref, i, QB, 0, rows)
        share = total // XN // QB
        g = g_ref[i // share, pl.ds(pl.multiple_of(i % share * QB, QB), QB), :]
        first = i * QB
        seg_q = sample_of(first + lax.broadcasted_iota(jnp.int32, (1, QB), 1), starts)
        qt_s[...] = q.T
        gt_s[...] = g.T
        begin, end = tile_range(first, first + QB - 1, starts, total)

        def scores(t, carry):
            m, l, d = carry
            here = pl.ds(pl.multiple_of(t * KT, KT), KT)
            s = masked_scores(
                block_rows(in_ref, t, KT, rows, rows), qt_s[...], seg_s[here, :], seg_q
            )
            dp = dot(block_rows(in_ref, t, KT, 2 * rows, rows), gt_s[...], ((1,), (0,)))
            dp_s[here, :] = dp
            m_new = jnp.maximum(m, jnp.max(s, axis=0, keepdims=True))
            p = jnp.exp2((s - m_new) * EXP2)
            p_s[here, :] = p
            top_s[t] = m_new
            alpha = jnp.exp2((m - m_new) * EXP2)
            l = l * alpha + jnp.sum(p, axis=0, keepdims=True)
            d = d * alpha + jnp.sum(p * dp, axis=0, keepdims=True)
            return m_new, l, d

        zero = jnp.zeros((1, QB), F32)
        m, l, d = lax.fori_loop(begin, end, scores, (jnp.full((1, QB), LOW, F32), zero, zero))
        inverse = 1.0 / l
        delta = d * inverse

        def grads(t, acc):
            here = pl.ds(pl.multiple_of(t * KT, KT), KT)
            p = p_s[here, :] * (jnp.exp2((top_s[t] - m) * EXP2) * inverse)
            ds = (p * (dp_s[here, :] - delta)).astype(BF16)
            dv_s[here, :] += dot(p.astype(BF16), g, ((1,), (0,)))
            dk_s[here, :] += dot(ds, q, ((1,), (0,)))
            return acc + dot(kt_s[:, here], ds, ((1,), (0,)))

        acc = lax.fori_loop(begin, end, grads, jnp.zeros((HD, QB), F32))
        dq = (acc * SCALE).T.astype(BF16)
        per = QB // rows
        out_s[pl.ds(i * per, per), 0:rows, :] = dq.reshape(per, rows, HD)
        return 0

    lax.fori_loop(0, total // QB, per_block, 0)
    for i in range(blocks):
        here = slice(i * rows, (i + 1) * rows)
        out_s[i, rows:2 * rows, :] = (dk_s[here, :] * SCALE).astype(BF16)
        out_s[i, 2 * rows:3 * rows, :] = dv_s[here, :].astype(BF16)
        pltpu.make_async_copy(out_s.at[i], out_ref.at[i], out_sem).start()
    pltpu.make_async_copy(out_s, out_ref, out_sem).wait()


def attention_backward(place, packed, grads, *later):
    blocks = packed.shape[0]
    total = blocks * 128
    return pl.pallas_call(
        backward_kernel,
        out_shape=jax.ShapeDtypeStruct((blocks, 3 * 128, HD), BF16),
        in_specs=[pl.BlockSpec(memory_space=pltpu.SMEM)]
        + in_hbm(1 + XN)
        + anywhere(later),
        out_specs=in_hbm(1)[0],
        scratch_shapes=[
            pltpu.VMEM(packed.shape, BF16),
            pltpu.VMEM((XN, total // XN, HD), BF16),
            pltpu.VMEM((blocks, 3 * 128, HD), BF16),
            pltpu.VMEM((HD, total), BF16),
            pltpu.VMEM((total, HD), F32),
            pltpu.VMEM((HD, QB), BF16),
            pltpu.VMEM((HD, QB), BF16),
            pltpu.VMEM((total, QB), F32),
            pltpu.VMEM((total, QB), F32),
            pltpu.VMEM((total // KT, 1, QB), F32),
            pltpu.VMEM((total, HD), F32),
            pltpu.VMEM((total, HD), F32),
            pltpu.SemaphoreType.DMA((XN + 1,)),
            pltpu.SemaphoreType.DMA,
        ],
        compiler_params=params(60),
        cost_estimate=cost(30),
        name="attention_backward",
    )(place, packed, *grads, *later)


def weight_copies(pieces, w_s, sems, first_sem):
    copies, row = [], 0
    for j, ref in enumerate(pieces):
        target = w_s.at[row:row + ref.shape[0], :]
        copies.append(pltpu.make_async_copy(ref, target, sems.at[first_sem + j]))
        row += ref.shape[0]
    return copies


def grad_kernel(place_ref, *refs):
    grads, pieces, outs = refs[:PER_X], refs[PER_X:PER_X + PIECES], refs[-5 - XN:-5]
    g_s, w_s, out_s, in_sems, out_sems = refs[-5:]
    rows = grads[0].shape[0]
    arriving = []
    for bits, ref in enumerate(grads):
        target = g_s.at[rows_at(place_ref, bits, rows), :]
        arriving.append(pltpu.make_async_copy(ref, target, in_sems.at[bits]))
    arriving += weight_copies(pieces, w_s, in_sems, PER_X)
    for copy in arriving:
        copy.start()
    for copy in arriving:
        copy.wait()
    leaving = []
    for j in range(0, XN, 2):
        r = dot(g_s[...], w_s[j * HD:(j + 2) * HD, :], ((1,), (1,))).astype(BF16)
        out_s[j] = r[:, :HD]
        out_s[j + 1] = r[:, HD:]
        for n in (j, j + 1):
            leaving.append(pltpu.make_async_copy(out_s.at[n], outs[n], out_sems.at[n]))
            leaving[-1].start()
    for copy in leaving:
        copy.wait()


def attention_grad(place, grads, pieces, *later):
    rows, width = grads[0].shape
    return pl.pallas_call(
        grad_kernel,
        out_shape=(jax.ShapeDtypeStruct((PER_X * rows, HD), BF16),) * XN,
        in_specs=[pl.BlockSpec(memory_space=pltpu.SMEM)] + in_hbm(PER_X + PIECES) + anywhere(later),
        out_specs=tuple(in_hbm(XN)),
        scratch_shapes=[
            pltpu.VMEM((PER_X * rows, width), BF16),
            pltpu.VMEM((XN * HD, width), BF16),
            pltpu.VMEM((XN, PER_X * rows, HD), BF16),
            pltpu.SemaphoreType.DMA((PER_X + PIECES,)),
            pltpu.SemaphoreType.DMA((XN,)),
        ],
        compiler_params=params(60),
        cost_estimate=cost(0.2),
        name="attention_grad",
    )(place, *grads, *pieces, *later)


def project_kernel(place_ref, *refs):
    attns, pieces, outs = refs[:XN], refs[XN:XN + PIECES], refs[-11:-8]
    a_in, w_s, a_s, own_s, across_s, send_s, in_sems, out_sems = refs[-8:]
    rows, width = outs[0].shape
    arriving = weight_copies(pieces, w_s, in_sems, XN)
    for j in range(XN):
        arriving.append(pltpu.make_async_copy(attns[j], a_in.at[j], in_sems.at[j]))
    for copy in arriving:
        copy.start()
    for copy in arriving:
        copy.wait()
    for n, bits in enumerate((0, 2, 1, 3)):
        for j in range(XN):
            a_s[n * rows:(n + 1) * rows, j * HD:(j + 1) * HD] = a_in[
                j, rows_at(place_ref, bits, rows), :
            ]
    step = 512
    for n in range(0, width, step):
        cols = slice(n, n + step)
        acc = dot(a_s[...], w_s[:, cols], ((1,), (0,)))
        own_s[:, cols] = acc[:rows]
        across_s[:, cols] = acc[rows:2 * rows]
        send_s[:, cols] = acc[2 * rows:].astype(BF16)
        for k, (result, out) in enumerate(zip((own_s, across_s, send_s), outs)):
            pltpu.make_async_copy(result.at[:, cols], out.at[:, cols], out_sems.at[k]).start()
    for k, (result, out) in enumerate(zip((own_s, across_s, send_s), outs)):
        pltpu.make_async_copy(result, out, out_sems.at[k]).wait()


def project(place, attns, pieces, *later):
    rows, width = pieces[0].shape
    shapes = (((rows, width), F32), ((rows, width), F32), ((2 * rows, width), BF16))
    return pl.pallas_call(
        project_kernel,
        out_shape=tuple(jax.ShapeDtypeStruct(*shape) for shape in shapes),
        in_specs=[pl.BlockSpec(memory_space=pltpu.SMEM)] + in_hbm(XN + PIECES) + anywhere(later),
        out_specs=tuple(in_hbm(3)),
        scratch_shapes=[
            pltpu.VMEM((XN, PER_X * rows, HD), BF16),
            pltpu.VMEM((XN * HD, width), BF16),
            pltpu.VMEM((PER_X * rows, XN * HD), BF16),
        ]
        + [pltpu.VMEM(*shape) for shape in shapes]
        + [pltpu.SemaphoreType.DMA((XN + PIECES,)), pltpu.SemaphoreType.DMA((3,))],
        compiler_params=params(60),
        cost_estimate=cost(0.2),
        name="project",
    )(place, *attns, *pieces, *later)


def unpack_kernel(in_ref, out_ref):
    rows = out_ref.shape[1]
    for h in range(in_ref.shape[0]):
        for t in range(3):
            out_ref[t, :, h * HD:(h + 1) * HD] = in_ref[h, t * rows:(t + 1) * rows, :]


def unpack(received):
    heads, rows = received.shape[0], received.shape[1] // 3
    return pl.pallas_call(
        unpack_kernel,
        out_shape=jax.ShapeDtypeStruct((3, rows, heads * HD), BF16),
        in_specs=whole(1),
        out_specs=whole(1)[0],
        compiler_params=params(24),
        cost_estimate=cost(2),
        name="unpack",
    )(received)


def choose_kernel(section_ref, first_ref, second_ref, *refs):
    out_ref = refs[-1]
    out_ref[...] = jnp.where(section_ref[0] == section_ref[1], first_ref[...], second_ref[...])


def choose(sections, first, second, *later):
    return pl.pallas_call(
        choose_kernel,
        out_shape=jax.ShapeDtypeStruct(first.shape, first.dtype),
        in_specs=[pl.BlockSpec(memory_space=pltpu.SMEM)] + whole(2) + anywhere(later),
        out_specs=whole(1)[0],
        compiler_params=params(16),
        cost_estimate=cost(2),
        name="choose",
    )(sections, first, second, *later)


def settle_kernel(in_ref, *refs):
    out_ref = refs[-1]
    out_ref[...] = in_ref[...]


def settle(array, *later):
    return pl.pallas_call(
        settle_kernel,
        out_shape=jax.ShapeDtypeStruct(array.shape, array.dtype),
        in_specs=whole(1) + anywhere(later),
        out_specs=whole(1)[0],
        compiler_params=params(8),
        cost_estimate=cost(0.2),
        name="settle",
    )(array, *later)


def shifted(array, axis, by):
    length = lax.axis_size(axis)
    pairs = [(i, i + by) for i in range(length) if 0 <= i + by < length]
    return lax.ppermute(array, axis, pairs)


def rotated(array, axis, by):
    length = lax.axis_size(axis)
    return lax.ppermute(array, axis, [(i, (i + by) % length) for i in range(length)])


def per_sample(seg, table):
    onehot = (seg[:, None] == jnp.arange(table.shape[0], dtype=jnp.int32)[None, :]).astype(F32)
    return jnp.sum(onehot[:, :, None] * table[None, :, :], axis=1)


def exchange(array):
    return lax.all_to_all(array, "seq", 0, 0, tiled=True)


def body(hidden_in, queries, keys, values, segments, gates, out_weight, upstream, fresh, loss_grad):
    section = lax.axis_index("pipe")
    last_section = lax.axis_size("pipe") - 1
    place = lax.axis_index("seq")[None]

    own = out_weight[0]
    pieces = tuple(along_x(own, -offset % XN) for offset in OFFSETS)

    fwd = exchange(pack(queries, keys, values, segments, 0))
    local_seg = segments[0]
    g_scaled = (per_sample(local_seg[1], gates[0, 1]) * upstream[0].astype(F32)).astype(BF16)
    g_across = lax.ppermute(g_scaled, "seq", YSWAP)
    g_core = lax.ppermute(g_scaled, "seq", CORE)
    g_both = lax.ppermute(g_across, "seq", CORE)
    gate_tok = per_sample(local_seg[0], gates[0, 0])
    grads = attention_grad(place, (g_scaled, g_core, g_across, g_both), pieces)
    packed = pack(queries, keys, values, segments, 1, g_across, gate_tok, *pieces[1:])
    bwd = exchange(packed)

    turned = settle(upstream[0], fwd)
    moved = shifted(turned, "pipe", -1)
    attns = attention_forward(place, fwd, grads[0], gate_tok, turned)
    grads = tuple(along_x(g, o) for g, o in zip(grads, OFFSETS))
    attns = (attns[0], follow(attns[1], *grads[1:])) + attns[2:]
    attns = tuple(along_x(a, o) for a, o in zip(attns, OFFSETS))

    attns = (attns[0], attns[2], attns[1], follow(attns[3], bwd, moved))
    part, part_across, part_send = project(place, attns, pieces)
    received = lax.ppermute(part_send, "seq", CORE)
    rows = part.shape[0]
    across = (part_across + received[rows:].astype(F32)).astype(BF16)
    grads = attention_backward(place, bwd, grads, across)
    across = lax.ppermute(across, "seq", YSWAP)
    proj = part + received[:rows].astype(F32) + across.astype(F32)
    section_out = (hidden_in[0].astype(F32) + gate_tok * proj).astype(BF16)
    section_out = jnp.where(section == last_section, fresh, section_out)
    next_act = rotated(section_out, "pipe", 1)

    sections = jnp.stack([section, last_section * jnp.ones_like(section)])
    next_grad = choose(sections, loss_grad, moved)
    qkv_grads = unpack(exchange(grads))
    return (next_act[None], next_grad[None], qkv_grads[None])


def solution(mesh):
    in_specs = (
        P("pipe", "seq", None),
        P("pipe", None, "seq", None),
        P("pipe", None, "seq", None),
        P("pipe", None, "seq", None),
        P("pipe", None, "seq"),
        P("pipe", None, None, None),
        P("pipe", "seq", None),
        P("pipe", "seq", None),
        P("seq", None),
        P("seq", None),
    )
    out_specs = (P("pipe", "seq", None), P("pipe", "seq", None), P("pipe", None, "seq", None))
    return jax.shard_map(body, mesh=mesh, in_specs=in_specs, out_specs=out_specs, check_vma=False)
```

```python
import functools

import jax
import jax.numpy as jnp
from jax import lax
from jax.experimental import pallas as pl
from jax.experimental.pallas import tpu as pltpu
from jax.sharding import PartitionSpec as P

HD = 128
SCALE = HD ** (-0.5)
EXP2 = SCALE * 1.4426950408889634
LOW = -1e30
QB = 512
KT = 512
SEG_ROWS = 16
F32 = jnp.float32
BF16 = jnp.bfloat16

XN, PER_X = 4, 4
OFFSETS = (0, 3, 1, 2)
PIECES = XN
CORE = [(i, i ^ 1) for i in range(XN * PER_X)]
YSWAP = [(i, i ^ 2) for i in range(XN * PER_X)]


def along_x(array, offset):
    if offset == 0:
        return array
    count = XN * PER_X
    return lax.ppermute(array, "seq", [(i, (i + PER_X * offset) % count) for i in range(count)])


def x_at(place_ref, offset):
    return (place_ref[0] // PER_X + offset) % XN


def rows_at(place_ref, bits, rows):
    return pl.ds(pl.multiple_of(((place_ref[0] % PER_X) ^ bits) * rows, rows), rows)


def params(mib):
    return pltpu.CompilerParams(vmem_limit_bytes=mib * 1024 * 1024)


def whole(count):
    return [pl.BlockSpec(memory_space=pltpu.VMEM)] * count


def anywhere(arrays):
    return [pl.BlockSpec(memory_space=pl.ANY)] * len(arrays)


def in_hbm(count):
    return [pl.BlockSpec(memory_space=pltpu.HBM)] * count


def cost(microseconds):
    return pl.CostEstimate(
        flops=int(microseconds * 1e9), bytes_accessed=0, transcendentals=0
    )


def dot(a, b, dims):
    return lax.dot_general(a, b, (dims, ((), ())), preferred_element_type=F32)


def pack_kernel(seg_ref, q_ref, k_ref, v_ref, *refs):
    out_ref = refs[-1]
    rows = q_ref.shape[0]
    ids = jnp.broadcast_to(seg_ref[...].astype(F32), (SEG_ROWS, HD)).astype(BF16)
    for h in range(out_ref.shape[0]):
        cols = slice(h * HD, (h + 1) * HD)
        out_ref[h, 0:rows, :] = q_ref[:, cols]
        out_ref[h, rows:2 * rows, :] = k_ref[:, cols]
        out_ref[h, 2 * rows:3 * rows, :] = v_ref[:, cols]
        out_ref[h, 3 * rows:, :] = ids


def pack(queries, keys, values, segments, batch, *later):
    rows, width = queries.shape[2], queries.shape[3]
    heads = width // HD
    height = 3 * rows + SEG_ROWS
    block = pl.BlockSpec((None, None, rows, width), lambda i: (0, batch, 0, 0))
    return pl.pallas_call(
        pack_kernel,
        grid=(1,),
        out_shape=jax.ShapeDtypeStruct((heads, height, HD), BF16),
        in_specs=[pl.BlockSpec((1, rows), lambda i: (0, 0)), block, block, block]
        + anywhere(later),
        out_specs=pl.BlockSpec((heads, height, HD), lambda i: (0, 0, 0)),
        compiler_params=params(60),
        cost_estimate=cost(2),
        name="pack",
    )(segments[0, batch][None], queries, keys, values, *later)


def follow_kernel(array_ref, *refs):
    pass


def follow(array, *later):
    return pl.pallas_call(
        follow_kernel,
        out_shape=jax.ShapeDtypeStruct(array.shape, array.dtype),
        in_specs=anywhere((array,) + later),
        out_specs=pl.BlockSpec(memory_space=pl.ANY),
        input_output_aliases={0: 0},
        compiler_params=params(1),
        cost_estimate=cost(0.01),
        name="follow",
    )(array, *later)


def sample_starts(in_ref, rows):
    ids = in_ref[:, 3 * rows:, :].astype(F32)
    return [
        jnp.sum(jnp.where(ids < s, 1.0, 0.0)).astype(jnp.int32) // SEG_ROWS for s in (1, 2, 3)
    ]


def sample_of(position, starts):
    return sum(jnp.where(position >= b, 1.0, 0.0) for b in starts)


def tile_range(first, last, starts, total):
    low, high = 0, total
    for b in starts:
        low = jnp.maximum(low, jnp.where(b <= first, b, 0))
        high = jnp.minimum(high, jnp.where(b > last, b, total))
    return low // KT, (high + KT - 1) // KT


def block_rows(ref, index, count, start, rows):
    per = count // rows
    return ref[pl.ds(index * per, per), start:start + rows, :].reshape(count, HD)


def fill_samples(seg_s, starts):
    for i in range(seg_s.shape[0] // 256):
        position = i * 256 + lax.broadcasted_iota(jnp.int32, (256, HD), 0)
        seg_s[i * 256:(i + 1) * 256, :] = sample_of(position, starts)


def masked_scores(k, q, seg_k, seg_q):
    same = jnp.concatenate([seg_k] * (QB // HD), axis=1) == seg_q
    return jnp.where(same, dot(k, q, ((1,), (0,))), LOW)


def forward_kernel(place_ref, in_hbm_ref, *refs):
    outs, (in_ref, out_s, vt_s, seg_s, qt_s, in_sem, out_sems) = refs[-7 - XN:-7], refs[-7:]
    arriving = pltpu.make_async_copy(in_hbm_ref, in_ref, in_sem)
    arriving.start()
    arriving.wait()
    blocks, rows = in_ref.shape[0], 128
    total = blocks * rows
    starts = sample_starts(in_ref, rows)
    fill_samples(seg_s, starts)
    for i in range(blocks):
        vt_s[:, i * rows:(i + 1) * rows] = in_ref[i, 2 * rows:3 * rows, :].T

    def per_block(i, _):
        q = block_rows(in_ref, i, QB, 0, rows)
        first = i * QB
        seg_q = sample_of(first + lax.broadcasted_iota(jnp.int32, (1, QB), 1), starts)
        qt_s[...] = q.T
        begin, end = tile_range(first, first + QB - 1, starts, total)

        def per_tile(t, carry):
            m, l, acc = carry
            here = pl.ds(pl.multiple_of(t * KT, KT), KT)
            s = masked_scores(
                block_rows(in_ref, t, KT, rows, rows), qt_s[...], seg_s[here, :], seg_q
            )
            m_new = jnp.maximum(m, jnp.max(s, axis=0, keepdims=True))
            p = jnp.exp2((s - m_new) * EXP2)
            alpha = jnp.exp2((m - m_new) * EXP2)
            l = l * alpha + jnp.sum(p, axis=0, keepdims=True)
            vt = vt_s[:, pl.ds(pl.multiple_of(t * KT, KT), KT)]
            acc = acc * alpha + dot(vt, p.astype(BF16), ((1,), (0,)))
            return m_new, l, acc

        m0 = jnp.full((1, QB), LOW, F32)
        l0 = jnp.zeros((1, QB), F32)
        m, l, acc = lax.fori_loop(begin, end, per_tile, (m0, l0, jnp.zeros((HD, QB), F32)))
        share = total // XN // QB
        here = pl.ds(pl.multiple_of(i % share * QB, QB), QB)
        out_s[i // share, here, :] = (acc / l).T.astype(BF16)
        return 0

    lax.fori_loop(0, total // QB, per_block, 0)
    leaving = [
        pltpu.make_async_copy(out_s.at[x_at(place_ref, offset)], ref, out_sems.at[n])
        for n, (offset, ref) in enumerate(zip(OFFSETS, outs))
    ]
    for copy in leaving:
        copy.start()
    for copy in leaving:
        copy.wait()


def attention_forward(place, packed, *later):
    total = packed.shape[0] * 128
    return pl.pallas_call(
        forward_kernel,
        out_shape=(jax.ShapeDtypeStruct((total // XN, HD), BF16),) * XN,
        in_specs=[pl.BlockSpec(memory_space=pltpu.SMEM)] + in_hbm(1) + anywhere(later),
        out_specs=tuple(in_hbm(XN)),
        scratch_shapes=[
            pltpu.VMEM(packed.shape, BF16),
            pltpu.VMEM((XN, total // XN, HD), BF16),
            pltpu.VMEM((HD, total), BF16),
            pltpu.VMEM((total, HD), F32),
            pltpu.VMEM((HD, QB), BF16),
            pltpu.SemaphoreType.DMA,
            pltpu.SemaphoreType.DMA((XN,)),
        ],
        compiler_params=params(60),
        cost_estimate=cost(0.2),
        name="attention_forward",
    )(place, packed, *later)


def backward_kernel(place_ref, in_hbm_ref, *refs):
    g_refs = refs[:XN]
    out_ref, in_ref, g_ref, out_s, kt_s, seg_s, qt_s, gt_s, p_s, dp_s, top_s, dk_s, dv_s, *sems = refs[-15:]
    in_sems, out_sem = sems
    packed = pltpu.make_async_copy(in_hbm_ref, in_ref, in_sems.at[XN])
    packed.start()
    blocks, rows = in_ref.shape[0], 128
    arriving = []
    for n, (offset, ref) in enumerate(zip(OFFSETS, g_refs)):
        source = x_at(place_ref, -offset % XN)
        arriving.append(pltpu.make_async_copy(ref, g_ref.at[source], in_sems.at[n]))
        arriving[-1].start()
    total = blocks * rows
    packed.wait()
    starts = sample_starts(in_ref, rows)
    fill_samples(seg_s, starts)
    for i in range(blocks):
        kt_s[:, i * rows:(i + 1) * rows] = in_ref[i, rows:2 * rows, :].T
    dk_s[...] = jnp.zeros_like(dk_s)
    dv_s[...] = jnp.zeros_like(dv_s)
    for copy in arriving:
        copy.wait()

    def per_block(i, _):
        q = block_rows(in_ref, i, QB, 0, rows)
        share = total // XN // QB
        g = g_ref[i // share, pl.ds(pl.multiple_of(i % share * QB, QB), QB), :]
        first = i * QB
        seg_q = sample_of(first + lax.broadcasted_iota(jnp.int32, (1, QB), 1), starts)
        qt_s[...] = q.T
        gt_s[...] = g.T
        begin, end = tile_range(first, first + QB - 1, starts, total)

        def scores(t, carry):
            m, l, d = carry
            here = pl.ds(pl.multiple_of(t * KT, KT), KT)
            s = masked_scores(
                block_rows(in_ref, t, KT, rows, rows), qt_s[...], seg_s[here, :], seg_q
            )
            dp = dot(block_rows(in_ref, t, KT, 2 * rows, rows), gt_s[...], ((1,), (0,)))
            dp_s[here, :] = dp
            m_new = jnp.maximum(m, jnp.max(s, axis=0, keepdims=True))
            p = jnp.exp2((s - m_new) * EXP2)
            p_s[here, :] = p
            top_s[t] = m_new
            alpha = jnp.exp2((m - m_new) * EXP2)
            l = l * alpha + jnp.sum(p, axis=0, keepdims=True)
            d = d * alpha + jnp.sum(p * dp, axis=0, keepdims=True)
            return m_new, l, d

        zero = jnp.zeros((1, QB), F32)
        m, l, d = lax.fori_loop(begin, end, scores, (jnp.full((1, QB), LOW, F32), zero, zero))
        inverse = 1.0 / l
        delta = d * inverse

        def grads(t, acc):
            here = pl.ds(pl.multiple_of(t * KT, KT), KT)
            p = p_s[here, :] * (jnp.exp2((top_s[t] - m) * EXP2) * inverse)
            ds = (p * (dp_s[here, :] - delta)).astype(BF16)
            dv_s[here, :] += dot(p.astype(BF16), g, ((1,), (0,)))
            dk_s[here, :] += dot(ds, q, ((1,), (0,)))
            return acc + dot(kt_s[:, here], ds, ((1,), (0,)))

        acc = lax.fori_loop(begin, end, grads, jnp.zeros((HD, QB), F32))
        dq = (acc * SCALE).T.astype(BF16)
        per = QB // rows
        out_s[pl.ds(i * per, per), 0:rows, :] = dq.reshape(per, rows, HD)
        return 0

    lax.fori_loop(0, total // QB, per_block, 0)
    for i in range(blocks):
        here = slice(i * rows, (i + 1) * rows)
        out_s[i, rows:2 * rows, :] = (dk_s[here, :] * SCALE).astype(BF16)
        out_s[i, 2 * rows:3 * rows, :] = dv_s[here, :].astype(BF16)
        pltpu.make_async_copy(out_s.at[i], out_ref.at[i], out_sem).start()
    pltpu.make_async_copy(out_s, out_ref, out_sem).wait()


def attention_backward(place, packed, grads, *later):
    blocks = packed.shape[0]
    total = blocks * 128
    return pl.pallas_call(
        backward_kernel,
        out_shape=jax.ShapeDtypeStruct((blocks, 3 * 128, HD), BF16),
        in_specs=[pl.BlockSpec(memory_space=pltpu.SMEM)]
        + in_hbm(1 + XN)
        + anywhere(later),
        out_specs=in_hbm(1)[0],
        scratch_shapes=[
            pltpu.VMEM(packed.shape, BF16),
            pltpu.VMEM((XN, total // XN, HD), BF16),
            pltpu.VMEM((blocks, 3 * 128, HD), BF16),
            pltpu.VMEM((HD, total), BF16),
            pltpu.VMEM((total, HD), F32),
            pltpu.VMEM((HD, QB), BF16),
            pltpu.VMEM((HD, QB), BF16),
            pltpu.VMEM((total, QB), F32),
            pltpu.VMEM((total, QB), F32),
            pltpu.VMEM((total // KT, 1, QB), F32),
            pltpu.VMEM((total, HD), F32),
            pltpu.VMEM((total, HD), F32),
            pltpu.SemaphoreType.DMA((XN + 1,)),
            pltpu.SemaphoreType.DMA,
        ],
        compiler_params=params(60),
        cost_estimate=cost(30),
        name="attention_backward",
    )(place, packed, *grads, *later)


def weight_copies(pieces, w_s, sems, first_sem):
    copies, row = [], 0
    for j, ref in enumerate(pieces):
        target = w_s.at[row:row + ref.shape[0], :]
        copies.append(pltpu.make_async_copy(ref, target, sems.at[first_sem + j]))
        row += ref.shape[0]
    return copies


def grad_kernel(place_ref, *refs):
    grads, pieces, outs = refs[:PER_X], refs[PER_X:PER_X + PIECES], refs[-5 - XN:-5]
    g_s, w_s, out_s, in_sems, out_sems = refs[-5:]
    rows = grads[0].shape[0]
    arriving = []
    for bits, ref in enumerate(grads):
        target = g_s.at[rows_at(place_ref, bits, rows), :]
        arriving.append(pltpu.make_async_copy(ref, target, in_sems.at[bits]))
    arriving += weight_copies(pieces, w_s, in_sems, PER_X)
    for copy in arriving:
        copy.start()
    for copy in arriving:
        copy.wait()
    leaving = []
    for j in range(0, XN, 2):
        r = dot(g_s[...], w_s[j * HD:(j + 2) * HD, :], ((1,), (1,))).astype(BF16)
        out_s[j] = r[:, :HD]
        out_s[j + 1] = r[:, HD:]
        for n in (j, j + 1):
            leaving.append(pltpu.make_async_copy(out_s.at[n], outs[n], out_sems.at[n]))
            leaving[-1].start()
    for copy in leaving:
        copy.wait()


def attention_grad(place, grads, pieces, *later):
    rows, width = grads[0].shape
    return pl.pallas_call(
        grad_kernel,
        out_shape=(jax.ShapeDtypeStruct((PER_X * rows, HD), BF16),) * XN,
        in_specs=[pl.BlockSpec(memory_space=pltpu.SMEM)] + in_hbm(PER_X + PIECES) + anywhere(later),
        out_specs=tuple(in_hbm(XN)),
        scratch_shapes=[
            pltpu.VMEM((PER_X * rows, width), BF16),
            pltpu.VMEM((XN * HD, width), BF16),
            pltpu.VMEM((XN, PER_X * rows, HD), BF16),
            pltpu.SemaphoreType.DMA((PER_X + PIECES,)),
            pltpu.SemaphoreType.DMA((XN,)),
        ],
        compiler_params=params(60),
        cost_estimate=cost(0.2),
        name="attention_grad",
    )(place, *grads, *pieces, *later)


def project_kernel(place_ref, *refs):
    attns, pieces, outs = refs[:XN], refs[XN:XN + PIECES], refs[-11:-8]
    a_in, w_s, a_s, own_s, across_s, send_s, in_sems, out_sems = refs[-8:]
    rows, width = outs[0].shape
    arriving = weight_copies(pieces, w_s, in_sems, XN)
    for j in range(XN):
        arriving.append(pltpu.make_async_copy(attns[j], a_in.at[j], in_sems.at[j]))
    for copy in arriving:
        copy.start()
    for copy in arriving:
        copy.wait()
    for n, bits in enumerate((0, 2, 1, 3)):
        for j in range(XN):
            a_s[n * rows:(n + 1) * rows, j * HD:(j + 1) * HD] = a_in[
                j, rows_at(place_ref, bits, rows), :
            ]
    step = 512
    for n in range(0, width, step):
        cols = slice(n, n + step)
        acc = dot(a_s[...], w_s[:, cols], ((1,), (0,)))
        own_s[:, cols] = acc[:rows]
        across_s[:, cols] = acc[rows:2 * rows]
        send_s[:, cols] = acc[2 * rows:].astype(BF16)
        for k, (result, out) in enumerate(zip((own_s, across_s, send_s), outs)):
            pltpu.make_async_copy(result.at[:, cols], out.at[:, cols], out_sems.at[k]).start()
    for k, (result, out) in enumerate(zip((own_s, across_s, send_s), outs)):
        pltpu.make_async_copy(result, out, out_sems.at[k]).wait()


def project(place, attns, pieces, *later):
    rows, width = pieces[0].shape
    shapes = (((rows, width), F32), ((rows, width), F32), ((2 * rows, width), BF16))
    return pl.pallas_call(
        project_kernel,
        out_shape=tuple(jax.ShapeDtypeStruct(*shape) for shape in shapes),
        in_specs=[pl.BlockSpec(memory_space=pltpu.SMEM)] + in_hbm(XN + PIECES) + anywhere(later),
        out_specs=tuple(in_hbm(3)),
        scratch_shapes=[
            pltpu.VMEM((XN, PER_X * rows, HD), BF16),
            pltpu.VMEM((XN * HD, width), BF16),
            pltpu.VMEM((PER_X * rows, XN * HD), BF16),
        ]
        + [pltpu.VMEM(*shape) for shape in shapes]
        + [pltpu.SemaphoreType.DMA((XN + PIECES,)), pltpu.SemaphoreType.DMA((3,))],
        compiler_params=params(60),
        cost_estimate=cost(0.2),
        name="project",
    )(place, *attns, *pieces, *later)


def unpack_kernel(in_ref, out_ref):
    rows = out_ref.shape[1]
    for h in range(in_ref.shape[0]):
        for t in range(3):
            out_ref[t, :, h * HD:(h + 1) * HD] = in_ref[h, t * rows:(t + 1) * rows, :]


def unpack(received):
    heads, rows = received.shape[0], received.shape[1] // 3
    return pl.pallas_call(
        unpack_kernel,
        out_shape=jax.ShapeDtypeStruct((3, rows, heads * HD), BF16),
        in_specs=whole(1),
        out_specs=whole(1)[0],
        compiler_params=params(24),
        cost_estimate=cost(2),
        name="unpack",
    )(received)


def choose_kernel(section_ref, first_ref, second_ref, *refs):
    out_ref = refs[-1]
    out_ref[...] = jnp.where(section_ref[0] == section_ref[1], first_ref[...], second_ref[...])


def choose(sections, first, second, *later):
    return pl.pallas_call(
        choose_kernel,
        out_shape=jax.ShapeDtypeStruct(first.shape, first.dtype),
        in_specs=[pl.BlockSpec(memory_space=pltpu.SMEM)] + whole(2) + anywhere(later),
        out_specs=whole(1)[0],
        compiler_params=params(16),
        cost_estimate=cost(2),
        name="choose",
    )(sections, first, second, *later)


def settle_kernel(in_ref, *refs):
    out_ref = refs[-1]
    out_ref[...] = in_ref[...]


def settle(array, *later):
    return pl.pallas_call(
        settle_kernel,
        out_shape=jax.ShapeDtypeStruct(array.shape, array.dtype),
        in_specs=whole(1) + anywhere(later),
        out_specs=whole(1)[0],
        compiler_params=params(8),
        cost_estimate=cost(0.2),
        name="settle",
    )(array, *later)


def shifted(array, axis, by):
    length = lax.axis_size(axis)
    pairs = [(i, i + by) for i in range(length) if 0 <= i + by < length]
    return lax.ppermute(array, axis, pairs)


def rotated(array, axis, by):
    length = lax.axis_size(axis)
    return lax.ppermute(array, axis, [(i, (i + by) % length) for i in range(length)])


def per_sample(seg, table):
    onehot = (seg[:, None] == jnp.arange(table.shape[0], dtype=jnp.int32)[None, :]).astype(F32)
    return jnp.sum(onehot[:, :, None] * table[None, :, :], axis=1)


def exchange(array):
    return lax.all_to_all(array, "seq", 0, 0, tiled=True)


def body(hidden_in, queries, keys, values, segments, gates, out_weight, upstream, fresh, loss_grad):
    section = lax.axis_index("pipe")
    last_section = lax.axis_size("pipe") - 1
    place = lax.axis_index("seq")[None]

    own = out_weight[0]
    pieces = tuple(along_x(own, -offset % XN) for offset in OFFSETS)

    fwd = exchange(pack(queries, keys, values, segments, 0))
    local_seg = segments[0]
    g_scaled = (per_sample(local_seg[1], gates[0, 1]) * upstream[0].astype(F32)).astype(BF16)
    g_across = lax.ppermute(g_scaled, "seq", YSWAP)
    g_core = lax.ppermute(g_scaled, "seq", CORE)
    g_across = follow(g_across, *pieces[1:])
    g_both = lax.ppermute(g_across, "seq", CORE)
    gate_tok = per_sample(local_seg[0], gates[0, 0])
    grads = attention_grad(place, (g_scaled, g_core, g_across, g_both), pieces)
    packed = pack(queries, keys, values, segments, 1, grads[0], gate_tok)
    bwd = exchange(packed)

    turned = settle(upstream[0], fwd)
    moved = shifted(turned, "pipe", -1)
    attns = attention_forward(place, fwd, grads[0], gate_tok, turned)
    grads = tuple(along_x(g, o) for g, o in zip(grads, OFFSETS))
    attns = (attns[0], follow(attns[1], *grads[1:])) + attns[2:]
    attns = tuple(along_x(a, o) for a, o in zip(attns, OFFSETS))

    attns = (attns[0], attns[2], attns[1], follow(attns[3], bwd))
    part, part_across, part_send = project(place, attns, pieces)
    received = lax.ppermute(follow(part_send, moved), "seq", CORE)
    rows = part.shape[0]
    across = (part_across + received[rows:].astype(F32)).astype(BF16)
    grads = attention_backward(place, bwd, grads, across)
    across = lax.ppermute(across, "seq", YSWAP)
    proj = part + received[:rows].astype(F32) + across.astype(F32)
    section_out = (hidden_in[0].astype(F32) + gate_tok * proj).astype(BF16)
    section_out = jnp.where(section == last_section, fresh, section_out)
    next_act = rotated(section_out, "pipe", 1)

    sections = jnp.stack([section, last_section * jnp.ones_like(section)])
    next_grad = choose(sections, loss_grad, moved)
    qkv_grads = unpack(exchange(grads))
    return (next_act[None], next_grad[None], qkv_grads[None])


def solution(mesh):
    in_specs = (
        P("pipe", "seq", None),
        P("pipe", None, "seq", None),
        P("pipe", None, "seq", None),
        P("pipe", None, "seq", None),
        P("pipe", None, "seq"),
        P("pipe", None, None, None),
        P("pipe", "seq", None),
        P("pipe", "seq", None),
        P("seq", None),
        P("seq", None),
    )
    out_specs = (P("pipe", "seq", None), P("pipe", "seq", None), P("pipe", None, "seq", None))
    return jax.shard_map(body, mesh=mesh, in_specs=in_specs, out_specs=out_specs, check_vma=False)
```

```python
import functools

import jax
import jax.numpy as jnp
from jax import lax
from jax.experimental import pallas as pl
from jax.experimental.pallas import tpu as pltpu
from jax.sharding import PartitionSpec as P

HD = 128
SCALE = HD ** (-0.5)
EXP2 = SCALE * 1.4426950408889634
LOW = -1e30
QB = 512
KT = 512
SEG_ROWS = 16
F32 = jnp.float32
BF16 = jnp.bfloat16

XN, PER_X = 4, 4
OFFSETS = (0, 3, 1, 2)
PIECES = XN
CORE = [(i, i ^ 1) for i in range(XN * PER_X)]
YSWAP = [(i, i ^ 2) for i in range(XN * PER_X)]


def along_x(array, offset):
    if offset == 0:
        return array
    count = XN * PER_X
    return lax.ppermute(array, "seq", [(i, (i + PER_X * offset) % count) for i in range(count)])


def x_at(place_ref, offset):
    return (place_ref[0] // PER_X + offset) % XN


def rows_at(place_ref, bits, rows):
    return pl.ds(pl.multiple_of(((place_ref[0] % PER_X) ^ bits) * rows, rows), rows)


def params(mib):
    return pltpu.CompilerParams(vmem_limit_bytes=mib * 1024 * 1024)


def whole(count):
    return [pl.BlockSpec(memory_space=pltpu.VMEM)] * count


def anywhere(arrays):
    return [pl.BlockSpec(memory_space=pl.ANY)] * len(arrays)


def in_hbm(count):
    return [pl.BlockSpec(memory_space=pltpu.HBM)] * count


def cost(microseconds):
    return pl.CostEstimate(
        flops=int(microseconds * 1e9), bytes_accessed=0, transcendentals=0
    )


def dot(a, b, dims):
    return lax.dot_general(a, b, (dims, ((), ())), preferred_element_type=F32)


def pack_kernel(seg_ref, q_ref, k_ref, v_ref, *refs):
    out_ref = refs[-1]
    rows = q_ref.shape[0]
    ids = jnp.broadcast_to(seg_ref[...].astype(F32), (SEG_ROWS, HD)).astype(BF16)
    for h in range(out_ref.shape[0]):
        cols = slice(h * HD, (h + 1) * HD)
        out_ref[h, 0:rows, :] = q_ref[:, cols]
        out_ref[h, rows:2 * rows, :] = k_ref[:, cols]
        out_ref[h, 2 * rows:3 * rows, :] = v_ref[:, cols]
        out_ref[h, 3 * rows:, :] = ids


def pack(queries, keys, values, segments, batch, *later):
    rows, width = queries.shape[2], queries.shape[3]
    heads = width // HD
    height = 3 * rows + SEG_ROWS
    block = pl.BlockSpec((None, None, rows, width), lambda i: (0, batch, 0, 0))
    return pl.pallas_call(
        pack_kernel,
        grid=(1,),
        out_shape=jax.ShapeDtypeStruct((heads, height, HD), BF16),
        in_specs=[pl.BlockSpec((1, rows), lambda i: (0, 0)), block, block, block]
        + anywhere(later),
        out_specs=pl.BlockSpec((heads, height, HD), lambda i: (0, 0, 0)),
        compiler_params=params(60),
        cost_estimate=cost(2),
        name="pack",
    )(segments[0, batch][None], queries, keys, values, *later)


def follow_kernel(array_ref, *refs):
    pass


def follow(array, *later):
    return pl.pallas_call(
        follow_kernel,
        out_shape=jax.ShapeDtypeStruct(array.shape, array.dtype),
        in_specs=anywhere((array,) + later),
        out_specs=pl.BlockSpec(memory_space=pl.ANY),
        input_output_aliases={0: 0},
        compiler_params=params(1),
        cost_estimate=cost(0.01),
        name="follow",
    )(array, *later)


def sample_starts(in_ref, rows):
    ids = in_ref[:, 3 * rows:, :].astype(F32)
    return [
        jnp.sum(jnp.where(ids < s, 1.0, 0.0)).astype(jnp.int32) // SEG_ROWS for s in (1, 2, 3)
    ]


def sample_of(position, starts):
    return sum(jnp.where(position >= b, 1.0, 0.0) for b in starts)


def tile_range(first, last, starts, total):
    low, high = 0, total
    for b in starts:
        low = jnp.maximum(low, jnp.where(b <= first, b, 0))
        high = jnp.minimum(high, jnp.where(b > last, b, total))
    return low // KT, (high + KT - 1) // KT


def block_rows(ref, index, count, start, rows):
    per = count // rows
    return ref[pl.ds(index * per, per), start:start + rows, :].reshape(count, HD)


def fill_samples(seg_s, starts):
    for i in range(seg_s.shape[0] // 256):
        position = i * 256 + lax.broadcasted_iota(jnp.int32, (256, HD), 0)
        seg_s[i * 256:(i + 1) * 256, :] = sample_of(position, starts)


def masked_scores(k, q, seg_k, seg_q):
    same = jnp.concatenate([seg_k] * (QB // HD), axis=1) == seg_q
    return jnp.where(same, dot(k, q, ((1,), (0,))), LOW)


def forward_kernel(place_ref, in_hbm_ref, *refs):
    outs, (in_ref, out_s, vt_s, seg_s, qt_s, in_sem, out_sems) = refs[-7 - XN:-7], refs[-7:]
    arriving = pltpu.make_async_copy(in_hbm_ref, in_ref, in_sem)
    arriving.start()
    arriving.wait()
    blocks, rows = in_ref.shape[0], 128
    total = blocks * rows
    starts = sample_starts(in_ref, rows)
    fill_samples(seg_s, starts)
    for i in range(blocks):
        vt_s[:, i * rows:(i + 1) * rows] = in_ref[i, 2 * rows:3 * rows, :].T

    def per_block(i, _):
        q = block_rows(in_ref, i, QB, 0, rows)
        first = i * QB
        seg_q = sample_of(first + lax.broadcasted_iota(jnp.int32, (1, QB), 1), starts)
        qt_s[...] = q.T
        begin, end = tile_range(first, first + QB - 1, starts, total)

        def per_tile(t, carry):
            m, l, acc = carry
            here = pl.ds(pl.multiple_of(t * KT, KT), KT)
            s = masked_scores(
                block_rows(in_ref, t, KT, rows, rows), qt_s[...], seg_s[here, :], seg_q
            )
            m_new = jnp.maximum(m, jnp.max(s, axis=0, keepdims=True))
            p = jnp.exp2((s - m_new) * EXP2)
            alpha = jnp.exp2((m - m_new) * EXP2)
            l = l * alpha + jnp.sum(p, axis=0, keepdims=True)
            vt = vt_s[:, pl.ds(pl.multiple_of(t * KT, KT), KT)]
            acc = acc * alpha + dot(vt, p.astype(BF16), ((1,), (0,)))
            return m_new, l, acc

        m0 = jnp.full((1, QB), LOW, F32)
        l0 = jnp.zeros((1, QB), F32)
        m, l, acc = lax.fori_loop(begin, end, per_tile, (m0, l0, jnp.zeros((HD, QB), F32)))
        share = total // XN // QB
        here = pl.ds(pl.multiple_of(i % share * QB, QB), QB)
        out_s[i // share, here, :] = (acc / l).T.astype(BF16)
        return 0

    lax.fori_loop(0, total // QB, per_block, 0)
    leaving = [
        pltpu.make_async_copy(out_s.at[x_at(place_ref, offset)], ref, out_sems.at[n])
        for n, (offset, ref) in enumerate(zip(OFFSETS, outs))
    ]
    for copy in leaving:
        copy.start()
    for copy in leaving:
        copy.wait()


def attention_forward(place, packed, *later):
    total = packed.shape[0] * 128
    return pl.pallas_call(
        forward_kernel,
        out_shape=(jax.ShapeDtypeStruct((total // XN, HD), BF16),) * XN,
        in_specs=[pl.BlockSpec(memory_space=pltpu.SMEM)] + in_hbm(1) + anywhere(later),
        out_specs=tuple(in_hbm(XN)),
        scratch_shapes=[
            pltpu.VMEM(packed.shape, BF16),
            pltpu.VMEM((XN, total // XN, HD), BF16),
            pltpu.VMEM((HD, total), BF16),
            pltpu.VMEM((total, HD), F32),
            pltpu.VMEM((HD, QB), BF16),
            pltpu.SemaphoreType.DMA,
            pltpu.SemaphoreType.DMA((XN,)),
        ],
        compiler_params=params(60),
        cost_estimate=cost(0.2),
        name="attention_forward",
    )(place, packed, *later)


def backward_kernel(place_ref, in_hbm_ref, *refs):
    g_refs = refs[:XN]
    out_ref, in_ref, g_ref, out_s, kt_s, seg_s, qt_s, gt_s, p_s, dp_s, top_s, dk_s, dv_s, *sems = refs[-15:]
    in_sems, out_sem = sems
    packed = pltpu.make_async_copy(in_hbm_ref, in_ref, in_sems.at[XN])
    packed.start()
    blocks, rows = in_ref.shape[0], 128
    arriving = []
    for n, (offset, ref) in enumerate(zip(OFFSETS, g_refs)):
        source = x_at(place_ref, -offset % XN)
        arriving.append(pltpu.make_async_copy(ref, g_ref.at[source], in_sems.at[n]))
        arriving[-1].start()
    total = blocks * rows
    packed.wait()
    starts = sample_starts(in_ref, rows)
    fill_samples(seg_s, starts)
    for i in range(blocks):
        kt_s[:, i * rows:(i + 1) * rows] = in_ref[i, rows:2 * rows, :].T
    dk_s[...] = jnp.zeros_like(dk_s)
    dv_s[...] = jnp.zeros_like(dv_s)
    for copy in arriving:
        copy.wait()

    def per_block(i, _):
        q = block_rows(in_ref, i, QB, 0, rows)
        share = total // XN // QB
        g = g_ref[i // share, pl.ds(pl.multiple_of(i % share * QB, QB), QB), :]
        first = i * QB
        seg_q = sample_of(first + lax.broadcasted_iota(jnp.int32, (1, QB), 1), starts)
        qt_s[...] = q.T
        gt_s[...] = g.T
        begin, end = tile_range(first, first + QB - 1, starts, total)

        def scores(t, carry):
            m, l, d = carry
            here = pl.ds(pl.multiple_of(t * KT, KT), KT)
            s = masked_scores(
                block_rows(in_ref, t, KT, rows, rows), qt_s[...], seg_s[here, :], seg_q
            )
            dp = dot(block_rows(in_ref, t, KT, 2 * rows, rows), gt_s[...], ((1,), (0,)))
            dp_s[here, :] = dp
            m_new = jnp.maximum(m, jnp.max(s, axis=0, keepdims=True))
            p = jnp.exp2((s - m_new) * EXP2)
            p_s[here, :] = p
            top_s[t] = m_new
            alpha = jnp.exp2((m - m_new) * EXP2)
            l = l * alpha + jnp.sum(p, axis=0, keepdims=True)
            d = d * alpha + jnp.sum(p * dp, axis=0, keepdims=True)
            return m_new, l, d

        zero = jnp.zeros((1, QB), F32)
        m, l, d = lax.fori_loop(begin, end, scores, (jnp.full((1, QB), LOW, F32), zero, zero))
        inverse = 1.0 / l
        delta = d * inverse

        def grads(t, acc):
            here = pl.ds(pl.multiple_of(t * KT, KT), KT)
            p = p_s[here, :] * (jnp.exp2((top_s[t] - m) * EXP2) * inverse)
            ds = (p * (dp_s[here, :] - delta)).astype(BF16)
            dv_s[here, :] += dot(p.astype(BF16), g, ((1,), (0,)))
            dk_s[here, :] += dot(ds, q, ((1,), (0,)))
            return acc + dot(kt_s[:, here], ds, ((1,), (0,)))

        acc = lax.fori_loop(begin, end, grads, jnp.zeros((HD, QB), F32))
        dq = (acc * SCALE).T.astype(BF16)
        per = QB // rows
        out_s[pl.ds(i * per, per), 0:rows, :] = dq.reshape(per, rows, HD)
        return 0

    lax.fori_loop(0, total // QB, per_block, 0)
    for i in range(blocks):
        here = slice(i * rows, (i + 1) * rows)
        out_s[i, rows:2 * rows, :] = (dk_s[here, :] * SCALE).astype(BF16)
        out_s[i, 2 * rows:3 * rows, :] = dv_s[here, :].astype(BF16)
        pltpu.make_async_copy(out_s.at[i], out_ref.at[i], out_sem).start()
    pltpu.make_async_copy(out_s, out_ref, out_sem).wait()


def attention_backward(place, packed, grads, *later):
    blocks = packed.shape[0]
    total = blocks * 128
    return pl.pallas_call(
        backward_kernel,
        out_shape=jax.ShapeDtypeStruct((blocks, 3 * 128, HD), BF16),
        in_specs=[pl.BlockSpec(memory_space=pltpu.SMEM)]
        + in_hbm(1 + XN)
        + anywhere(later),
        out_specs=in_hbm(1)[0],
        scratch_shapes=[
            pltpu.VMEM(packed.shape, BF16),
            pltpu.VMEM((XN, total // XN, HD), BF16),
            pltpu.VMEM((blocks, 3 * 128, HD), BF16),
            pltpu.VMEM((HD, total), BF16),
            pltpu.VMEM((total, HD), F32),
            pltpu.VMEM((HD, QB), BF16),
            pltpu.VMEM((HD, QB), BF16),
            pltpu.VMEM((total, QB), F32),
            pltpu.VMEM((total, QB), F32),
            pltpu.VMEM((total // KT, 1, QB), F32),
            pltpu.VMEM((total, HD), F32),
            pltpu.VMEM((total, HD), F32),
            pltpu.SemaphoreType.DMA((XN + 1,)),
            pltpu.SemaphoreType.DMA,
        ],
        compiler_params=params(60),
        cost_estimate=cost(30),
        name="attention_backward",
    )(place, packed, *grads, *later)


def weight_copies(pieces, w_s, sems, first_sem):
    copies, row = [], 0
    for j, ref in enumerate(pieces):
        target = w_s.at[row:row + ref.shape[0], :]
        copies.append(pltpu.make_async_copy(ref, target, sems.at[first_sem + j]))
        row += ref.shape[0]
    return copies


def grad_kernel(place_ref, *refs):
    grads, pieces, outs = refs[:PER_X], refs[PER_X:PER_X + PIECES], refs[-5 - XN:-5]
    g_s, w_s, out_s, in_sems, out_sems = refs[-5:]
    rows = grads[0].shape[0]
    arriving = []
    for bits, ref in enumerate(grads):
        target = g_s.at[rows_at(place_ref, bits, rows), :]
        arriving.append(pltpu.make_async_copy(ref, target, in_sems.at[bits]))
    arriving += weight_copies(pieces, w_s, in_sems, PER_X)
    for copy in arriving:
        copy.start()
    for copy in arriving:
        copy.wait()
    leaving = []
    for j in range(0, XN, 2):
        r = dot(g_s[...], w_s[j * HD:(j + 2) * HD, :], ((1,), (1,))).astype(BF16)
        out_s[j] = r[:, :HD]
        out_s[j + 1] = r[:, HD:]
        for n in (j, j + 1):
            leaving.append(pltpu.make_async_copy(out_s.at[n], outs[n], out_sems.at[n]))
            leaving[-1].start()
    for copy in leaving:
        copy.wait()


def attention_grad(place, grads, pieces, *later):
    rows, width = grads[0].shape
    return pl.pallas_call(
        grad_kernel,
        out_shape=(jax.ShapeDtypeStruct((PER_X * rows, HD), BF16),) * XN,
        in_specs=[pl.BlockSpec(memory_space=pltpu.SMEM)] + in_hbm(PER_X + PIECES) + anywhere(later),
        out_specs=tuple(in_hbm(XN)),
        scratch_shapes=[
            pltpu.VMEM((PER_X * rows, width), BF16),
            pltpu.VMEM((XN * HD, width), BF16),
            pltpu.VMEM((XN, PER_X * rows, HD), BF16),
            pltpu.SemaphoreType.DMA((PER_X + PIECES,)),
            pltpu.SemaphoreType.DMA((XN,)),
        ],
        compiler_params=params(60),
        cost_estimate=cost(0.2),
        name="attention_grad",
    )(place, *grads, *pieces, *later)


def project_kernel(place_ref, *refs):
    attns, pieces, outs = refs[:XN], refs[XN:XN + PIECES], refs[-11:-8]
    a_in, w_s, a_s, own_s, across_s, send_s, in_sems, out_sems = refs[-8:]
    rows, width = outs[0].shape
    arriving = weight_copies(pieces, w_s, in_sems, XN)
    for j in range(XN):
        arriving.append(pltpu.make_async_copy(attns[j], a_in.at[j], in_sems.at[j]))
    for copy in arriving:
        copy.start()
    for copy in arriving:
        copy.wait()
    for n, bits in enumerate((0, 2, 1, 3)):
        for j in range(XN):
            a_s[n * rows:(n + 1) * rows, j * HD:(j + 1) * HD] = a_in[
                j, rows_at(place_ref, bits, rows), :
            ]
    step = 512
    for n in range(0, width, step):
        cols = slice(n, n + step)
        acc = dot(a_s[...], w_s[:, cols], ((1,), (0,)))
        own_s[:, cols] = acc[:rows]
        across_s[:, cols] = acc[rows:2 * rows]
        send_s[:, cols] = acc[2 * rows:].astype(BF16)
        for k, (result, out) in enumerate(zip((own_s, across_s, send_s), outs)):
            pltpu.make_async_copy(result.at[:, cols], out.at[:, cols], out_sems.at[k]).start()
    for k, (result, out) in enumerate(zip((own_s, across_s, send_s), outs)):
        pltpu.make_async_copy(result, out, out_sems.at[k]).wait()


def project(place, attns, pieces, *later):
    rows, width = pieces[0].shape
    shapes = (((rows, width), F32), ((rows, width), F32), ((2 * rows, width), BF16))
    return pl.pallas_call(
        project_kernel,
        out_shape=tuple(jax.ShapeDtypeStruct(*shape) for shape in shapes),
        in_specs=[pl.BlockSpec(memory_space=pltpu.SMEM)] + in_hbm(XN + PIECES) + anywhere(later),
        out_specs=tuple(in_hbm(3)),
        scratch_shapes=[
            pltpu.VMEM((XN, PER_X * rows, HD), BF16),
            pltpu.VMEM((XN * HD, width), BF16),
            pltpu.VMEM((PER_X * rows, XN * HD), BF16),
        ]
        + [pltpu.VMEM(*shape) for shape in shapes]
        + [pltpu.SemaphoreType.DMA((XN + PIECES,)), pltpu.SemaphoreType.DMA((3,))],
        compiler_params=params(60),
        cost_estimate=cost(0.2),
        name="project",
    )(place, *attns, *pieces, *later)


def unpack_kernel(in_ref, out_ref):
    rows = out_ref.shape[1]
    for h in range(in_ref.shape[0]):
        for t in range(3):
            out_ref[t, :, h * HD:(h + 1) * HD] = in_ref[h, t * rows:(t + 1) * rows, :]


def unpack(received):
    heads, rows = received.shape[0], received.shape[1] // 3
    return pl.pallas_call(
        unpack_kernel,
        out_shape=jax.ShapeDtypeStruct((3, rows, heads * HD), BF16),
        in_specs=whole(1),
        out_specs=whole(1)[0],
        compiler_params=params(24),
        cost_estimate=cost(2),
        name="unpack",
    )(received)


def choose_kernel(section_ref, first_ref, second_ref, *refs):
    out_ref = refs[-1]
    out_ref[...] = jnp.where(section_ref[0] == section_ref[1], first_ref[...], second_ref[...])


def choose(sections, first, second, *later):
    return pl.pallas_call(
        choose_kernel,
        out_shape=jax.ShapeDtypeStruct(first.shape, first.dtype),
        in_specs=[pl.BlockSpec(memory_space=pltpu.SMEM)] + whole(2) + anywhere(later),
        out_specs=whole(1)[0],
        compiler_params=params(16),
        cost_estimate=cost(2),
        name="choose",
    )(sections, first, second, *later)


def settle_kernel(in_ref, *refs):
    out_ref = refs[-1]
    out_ref[...] = in_ref[...]


def settle(array, *later):
    return pl.pallas_call(
        settle_kernel,
        out_shape=jax.ShapeDtypeStruct(array.shape, array.dtype),
        in_specs=whole(1) + anywhere(later),
        out_specs=whole(1)[0],
        compiler_params=params(8),
        cost_estimate=cost(0.2),
        name="settle",
    )(array, *later)


def shifted(array, axis, by):
    length = lax.axis_size(axis)
    pairs = [(i, i + by) for i in range(length) if 0 <= i + by < length]
    return lax.ppermute(array, axis, pairs)


def rotated(array, axis, by):
    length = lax.axis_size(axis)
    return lax.ppermute(array, axis, [(i, (i + by) % length) for i in range(length)])


def per_sample(seg, table):
    onehot = (seg[:, None] == jnp.arange(table.shape[0], dtype=jnp.int32)[None, :]).astype(F32)
    return jnp.sum(onehot[:, :, None] * table[None, :, :], axis=1)


def exchange(array):
    return lax.all_to_all(array, "seq", 0, 0, tiled=True)


def body(hidden_in, queries, keys, values, segments, gates, out_weight, upstream, fresh, loss_grad):
    section = lax.axis_index("pipe")
    last_section = lax.axis_size("pipe") - 1
    place = lax.axis_index("seq")[None]

    own = out_weight[0]
    pieces = tuple(along_x(own, -offset % XN) for offset in OFFSETS)

    fwd = exchange(pack(queries, keys, values, segments, 0))
    local_seg = segments[0]
    g_scaled = (per_sample(local_seg[1], gates[0, 1]) * upstream[0].astype(F32)).astype(BF16)
    g_across = lax.ppermute(g_scaled, "seq", YSWAP)
    g_core = lax.ppermute(g_scaled, "seq", CORE)
    g_both = lax.ppermute(g_across, "seq", CORE)
    gate_tok = per_sample(local_seg[0], gates[0, 0])
    grads = attention_grad(place, (g_scaled, g_core, g_across, g_both), pieces)
    packed = pack(queries, keys, values, segments, 1, g_across, gate_tok, *pieces[1:])
    bwd = exchange(packed)

    turned = settle(upstream[0], fwd)
    moved = shifted(turned, "pipe", -1)
    attns = attention_forward(place, fwd, grads[0], gate_tok, turned)
    grads = tuple(along_x(g, o) for g, o in zip(grads, OFFSETS))
    attns = tuple(along_x(a, o) for a, o in zip(attns, OFFSETS))

    attns = (attns[0], attns[2], attns[1], follow(attns[3], bwd, moved, *grads[1:]))
    part, part_across, part_send = project(place, attns, pieces)
    received = lax.ppermute(part_send, "seq", CORE)
    rows = part.shape[0]
    across = (part_across + received[rows:].astype(F32)).astype(BF16)
    grads = attention_backward(place, bwd, grads, across)
    across = lax.ppermute(across, "seq", YSWAP)
    proj = part + received[:rows].astype(F32) + across.astype(F32)
    section_out = (hidden_in[0].astype(F32) + gate_tok * proj).astype(BF16)
    section_out = jnp.where(section == last_section, fresh, section_out)
    next_act = rotated(section_out, "pipe", 1)

    sections = jnp.stack([section, last_section * jnp.ones_like(section)])
    next_grad = choose(sections, loss_grad, moved)
    qkv_grads = unpack(exchange(grads))
    return (next_act[None], next_grad[None], qkv_grads[None])


def solution(mesh):
    in_specs = (
        P("pipe", "seq", None),
        P("pipe", None, "seq", None),
        P("pipe", None, "seq", None),
        P("pipe", None, "seq", None),
        P("pipe", None, "seq"),
        P("pipe", None, None, None),
        P("pipe", "seq", None),
        P("pipe", "seq", None),
        P("seq", None),
        P("seq", None),
    )
    out_specs = (P("pipe", "seq", None), P("pipe", "seq", None), P("pipe", None, "seq", None))
    return jax.shard_map(body, mesh=mesh, in_specs=in_specs, out_specs=out_specs, check_vma=False)
```

```python
import functools

import jax
import jax.numpy as jnp
from jax import lax
from jax.experimental import pallas as pl
from jax.experimental.pallas import tpu as pltpu
from jax.sharding import PartitionSpec as P

HD = 128
SCALE = HD ** (-0.5)
EXP2 = SCALE * 1.4426950408889634
LOW = -1e30
QB = 512
KT = 512
SEG_ROWS = 16
F32 = jnp.float32
BF16 = jnp.bfloat16

XN, PER_X = 4, 4
OFFSETS = (0, 3, 1, 2)
PIECES = XN
CORE = [(i, i ^ 1) for i in range(XN * PER_X)]
YSWAP = [(i, i ^ 2) for i in range(XN * PER_X)]


def along_x(array, offset):
    if offset == 0:
        return array
    count = XN * PER_X
    return lax.ppermute(array, "seq", [(i, (i + PER_X * offset) % count) for i in range(count)])


def x_at(place_ref, offset):
    return (place_ref[0] // PER_X + offset) % XN


def rows_at(place_ref, bits, rows):
    return pl.ds(pl.multiple_of(((place_ref[0] % PER_X) ^ bits) * rows, rows), rows)


def params(mib):
    return pltpu.CompilerParams(vmem_limit_bytes=mib * 1024 * 1024)


def whole(count):
    return [pl.BlockSpec(memory_space=pltpu.VMEM)] * count


def anywhere(arrays):
    return [pl.BlockSpec(memory_space=pl.ANY)] * len(arrays)


def in_hbm(count):
    return [pl.BlockSpec(memory_space=pltpu.HBM)] * count


def cost(microseconds):
    return pl.CostEstimate(
        flops=int(microseconds * 1e9), bytes_accessed=0, transcendentals=0
    )


def dot(a, b, dims):
    return lax.dot_general(a, b, (dims, ((), ())), preferred_element_type=F32)


def pack_kernel(seg_ref, q_ref, k_ref, v_ref, *refs):
    out_ref = refs[-1]
    rows = q_ref.shape[0]
    ids = jnp.broadcast_to(seg_ref[...].astype(F32), (SEG_ROWS, HD)).astype(BF16)
    for h in range(out_ref.shape[0]):
        cols = slice(h * HD, (h + 1) * HD)
        out_ref[h, 0:rows, :] = q_ref[:, cols]
        out_ref[h, rows:2 * rows, :] = k_ref[:, cols]
        out_ref[h, 2 * rows:3 * rows, :] = v_ref[:, cols]
        out_ref[h, 3 * rows:, :] = ids


def pack(queries, keys, values, segments, batch, *later):
    rows, width = queries.shape[2], queries.shape[3]
    heads = width // HD
    height = 3 * rows + SEG_ROWS
    block = pl.BlockSpec((None, None, rows, width), lambda i: (0, batch, 0, 0))
    return pl.pallas_call(
        pack_kernel,
        grid=(1,),
        out_shape=jax.ShapeDtypeStruct((heads, height, HD), BF16),
        in_specs=[pl.BlockSpec((1, rows), lambda i: (0, 0)), block, block, block]
        + anywhere(later),
        out_specs=pl.BlockSpec((heads, height, HD), lambda i: (0, 0, 0)),
        compiler_params=params(60),
        cost_estimate=cost(2),
        name="pack",
    )(segments[0, batch][None], queries, keys, values, *later)


def follow_kernel(array_ref, *refs):
    pass


def follow(array, *later):
    return pl.pallas_call(
        follow_kernel,
        out_shape=jax.ShapeDtypeStruct(array.shape, array.dtype),
        in_specs=anywhere((array,) + later),
        out_specs=pl.BlockSpec(memory_space=pl.ANY),
        input_output_aliases={0: 0},
        compiler_params=params(1),
        cost_estimate=cost(0.01),
        name="follow",
    )(array, *later)


def sample_starts(in_ref, rows):
    ids = in_ref[:, 3 * rows:, :].astype(F32)
    return [
        jnp.sum(jnp.where(ids < s, 1.0, 0.0)).astype(jnp.int32) // SEG_ROWS for s in (1, 2, 3)
    ]


def sample_of(position, starts):
    return sum(jnp.where(position >= b, 1.0, 0.0) for b in starts)


def tile_range(first, last, starts, total):
    low, high = 0, total
    for b in starts:
        low = jnp.maximum(low, jnp.where(b <= first, b, 0))
        high = jnp.minimum(high, jnp.where(b > last, b, total))
    return low // KT, (high + KT - 1) // KT


def block_rows(ref, index, count, start, rows):
    per = count // rows
    return ref[pl.ds(index * per, per), start:start + rows, :].reshape(count, HD)


def fill_samples(seg_s, starts):
    for i in range(seg_s.shape[0] // 256):
        position = i * 256 + lax.broadcasted_iota(jnp.int32, (256, HD), 0)
        seg_s[i * 256:(i + 1) * 256, :] = sample_of(position, starts)


def masked_scores(k, q, seg_k, seg_q):
    same = jnp.concatenate([seg_k] * (QB // HD), axis=1) == seg_q
    return jnp.where(same, dot(k, q, ((1,), (0,))), LOW)


def forward_kernel(place_ref, in_hbm_ref, *refs):
    outs, (in_ref, out_s, vt_s, seg_s, qt_s, in_sem, out_sems) = refs[-7 - XN:-7], refs[-7:]
    arriving = pltpu.make_async_copy(in_hbm_ref, in_ref, in_sem)
    arriving.start()
    arriving.wait()
    blocks, rows = in_ref.shape[0], 128
    total = blocks * rows
    starts = sample_starts(in_ref, rows)
    fill_samples(seg_s, starts)
    for i in range(blocks):
        vt_s[:, i * rows:(i + 1) * rows] = in_ref[i, 2 * rows:3 * rows, :].T

    def per_block(i, _):
        q = block_rows(in_ref, i, QB, 0, rows)
        first = i * QB
        seg_q = sample_of(first + lax.broadcasted_iota(jnp.int32, (1, QB), 1), starts)
        qt_s[...] = q.T
        begin, end = tile_range(first, first + QB - 1, starts, total)

        def per_tile(t, carry):
            m, l, acc = carry
            here = pl.ds(pl.multiple_of(t * KT, KT), KT)
            s = masked_scores(
                block_rows(in_ref, t, KT, rows, rows), qt_s[...], seg_s[here, :], seg_q
            )
            m_new = jnp.maximum(m, jnp.max(s, axis=0, keepdims=True))
            p = jnp.exp2((s - m_new) * EXP2)
            alpha = jnp.exp2((m - m_new) * EXP2)
            l = l * alpha + jnp.sum(p, axis=0, keepdims=True)
            vt = vt_s[:, pl.ds(pl.multiple_of(t * KT, KT), KT)]
            acc = acc * alpha + dot(vt, p.astype(BF16), ((1,), (0,)))
            return m_new, l, acc

        m0 = jnp.full((1, QB), LOW, F32)
        l0 = jnp.zeros((1, QB), F32)
        m, l, acc = lax.fori_loop(begin, end, per_tile, (m0, l0, jnp.zeros((HD, QB), F32)))
        share = total // XN // QB
        here = pl.ds(pl.multiple_of(i % share * QB, QB), QB)
        out_s[i // share, here, :] = (acc / l).T.astype(BF16)
        return 0

    lax.fori_loop(0, total // QB, per_block, 0)
    leaving = [
        pltpu.make_async_copy(out_s.at[x_at(place_ref, offset)], ref, out_sems.at[n])
        for n, (offset, ref) in enumerate(zip(OFFSETS, outs))
    ]
    for copy in leaving:
        copy.start()
    for copy in leaving:
        copy.wait()


def attention_forward(place, packed, *later):
    total = packed.shape[0] * 128
    return pl.pallas_call(
        forward_kernel,
        out_shape=(jax.ShapeDtypeStruct((total // XN, HD), BF16),) * XN,
        in_specs=[pl.BlockSpec(memory_space=pltpu.SMEM)] + in_hbm(1) + anywhere(later),
        out_specs=tuple(in_hbm(XN)),
        scratch_shapes=[
            pltpu.VMEM(packed.shape, BF16),
            pltpu.VMEM((XN, total // XN, HD), BF16),
            pltpu.VMEM((HD, total), BF16),
            pltpu.VMEM((total, HD), F32),
            pltpu.VMEM((HD, QB), BF16),
            pltpu.SemaphoreType.DMA,
            pltpu.SemaphoreType.DMA((XN,)),
        ],
        compiler_params=params(60),
        cost_estimate=cost(0.2),
        name="attention_forward",
    )(place, packed, *later)


def backward_kernel(place_ref, in_hbm_ref, *refs):
    g_refs = refs[:XN]
    out_ref, in_ref, g_ref, out_s, kt_s, seg_s, qt_s, gt_s, p_s, dp_s, top_s, dk_s, dv_s, *sems = refs[-15:]
    in_sems, out_sem = sems
    packed = pltpu.make_async_copy(in_hbm_ref, in_ref, in_sems.at[XN])
    packed.start()
    blocks, rows = in_ref.shape[0], 128
    arriving = []
    for n, (offset, ref) in enumerate(zip(OFFSETS, g_refs)):
        source = x_at(place_ref, -offset % XN)
        arriving.append(pltpu.make_async_copy(ref, g_ref.at[source], in_sems.at[n]))
        arriving[-1].start()
    total = blocks * rows
    packed.wait()
    starts = sample_starts(in_ref, rows)
    fill_samples(seg_s, starts)
    for i in range(blocks):
        kt_s[:, i * rows:(i + 1) * rows] = in_ref[i, rows:2 * rows, :].T
    dk_s[...] = jnp.zeros_like(dk_s)
    dv_s[...] = jnp.zeros_like(dv_s)
    for copy in arriving:
        copy.wait()

    def per_block(i, _):
        q = block_rows(in_ref, i, QB, 0, rows)
        share = total // XN // QB
        g = g_ref[i // share, pl.ds(pl.multiple_of(i % share * QB, QB), QB), :]
        first = i * QB
        seg_q = sample_of(first + lax.broadcasted_iota(jnp.int32, (1, QB), 1), starts)
        qt_s[...] = q.T
        gt_s[...] = g.T
        begin, end = tile_range(first, first + QB - 1, starts, total)

        def scores(t, carry):
            m, l, d = carry
            here = pl.ds(pl.multiple_of(t * KT, KT), KT)
            s = masked_scores(
                block_rows(in_ref, t, KT, rows, rows), qt_s[...], seg_s[here, :], seg_q
            )
            dp = dot(block_rows(in_ref, t, KT, 2 * rows, rows), gt_s[...], ((1,), (0,)))
            dp_s[here, :] = dp
            m_new = jnp.maximum(m, jnp.max(s, axis=0, keepdims=True))
            p = jnp.exp2((s - m_new) * EXP2)
            p_s[here, :] = p
            top_s[t] = m_new
            alpha = jnp.exp2((m - m_new) * EXP2)
            l = l * alpha + jnp.sum(p, axis=0, keepdims=True)
            d = d * alpha + jnp.sum(p * dp, axis=0, keepdims=True)
            return m_new, l, d

        zero = jnp.zeros((1, QB), F32)
        m, l, d = lax.fori_loop(begin, end, scores, (jnp.full((1, QB), LOW, F32), zero, zero))
        inverse = 1.0 / l
        delta = d * inverse

        def grads(t, acc):
            here = pl.ds(pl.multiple_of(t * KT, KT), KT)
            p = p_s[here, :] * (jnp.exp2((top_s[t] - m) * EXP2) * inverse)
            ds = (p * (dp_s[here, :] - delta)).astype(BF16)
            dv_s[here, :] += dot(p.astype(BF16), g, ((1,), (0,)))
            dk_s[here, :] += dot(ds, q, ((1,), (0,)))
            return acc + dot(kt_s[:, here], ds, ((1,), (0,)))

        acc = lax.fori_loop(begin, end, grads, jnp.zeros((HD, QB), F32))
        dq = (acc * SCALE).T.astype(BF16)
        per = QB // rows
        out_s[pl.ds(i * per, per), 0:rows, :] = dq.reshape(per, rows, HD)
        return 0

    lax.fori_loop(0, total // QB, per_block, 0)
    for i in range(blocks):
        here = slice(i * rows, (i + 1) * rows)
        out_s[i, rows:2 * rows, :] = (dk_s[here, :] * SCALE).astype(BF16)
        out_s[i, 2 * rows:3 * rows, :] = dv_s[here, :].astype(BF16)
        pltpu.make_async_copy(out_s.at[i], out_ref.at[i], out_sem).start()
    pltpu.make_async_copy(out_s, out_ref, out_sem).wait()


def attention_backward(place, packed, grads, *later):
    blocks = packed.shape[0]
    total = blocks * 128
    return pl.pallas_call(
        backward_kernel,
        out_shape=jax.ShapeDtypeStruct((blocks, 3 * 128, HD), BF16),
        in_specs=[pl.BlockSpec(memory_space=pltpu.SMEM)]
        + in_hbm(1 + XN)
        + anywhere(later),
        out_specs=in_hbm(1)[0],
        scratch_shapes=[
            pltpu.VMEM(packed.shape, BF16),
            pltpu.VMEM((XN, total // XN, HD), BF16),
            pltpu.VMEM((blocks, 3 * 128, HD), BF16),
            pltpu.VMEM((HD, total), BF16),
            pltpu.VMEM((total, HD), F32),
            pltpu.VMEM((HD, QB), BF16),
            pltpu.VMEM((HD, QB), BF16),
            pltpu.VMEM((total, QB), F32),
            pltpu.VMEM((total, QB), F32),
            pltpu.VMEM((total // KT, 1, QB), F32),
            pltpu.VMEM((total, HD), F32),
            pltpu.VMEM((total, HD), F32),
            pltpu.SemaphoreType.DMA((XN + 1,)),
            pltpu.SemaphoreType.DMA,
        ],
        compiler_params=params(60),
        cost_estimate=cost(30),
        name="attention_backward",
    )(place, packed, *grads, *later)


def weight_copies(pieces, w_s, sems, first_sem):
    copies, row = [], 0
    for j, ref in enumerate(pieces):
        target = w_s.at[row:row + ref.shape[0], :]
        copies.append(pltpu.make_async_copy(ref, target, sems.at[first_sem + j]))
        row += ref.shape[0]
    return copies


def grad_kernel(place_ref, *refs):
    grads, pieces, outs = refs[:PER_X], refs[PER_X:PER_X + PIECES], refs[-5 - XN:-5]
    g_s, w_s, out_s, in_sems, out_sems = refs[-5:]
    rows = grads[0].shape[0]
    arriving = []
    for bits, ref in enumerate(grads):
        target = g_s.at[rows_at(place_ref, bits, rows), :]
        arriving.append(pltpu.make_async_copy(ref, target, in_sems.at[bits]))
    arriving += weight_copies(pieces, w_s, in_sems, PER_X)
    for copy in arriving:
        copy.start()
    for copy in arriving:
        copy.wait()
    leaving = []
    for j in range(0, XN, 2):
        r = dot(g_s[...], w_s[j * HD:(j + 2) * HD, :], ((1,), (1,))).astype(BF16)
        out_s[j] = r[:, :HD]
        out_s[j + 1] = r[:, HD:]
        for n in (j, j + 1):
            leaving.append(pltpu.make_async_copy(out_s.at[n], outs[n], out_sems.at[n]))
            leaving[-1].start()
    for copy in leaving:
        copy.wait()


def attention_grad(place, grads, pieces, *later):
    rows, width = grads[0].shape
    return pl.pallas_call(
        grad_kernel,
        out_shape=(jax.ShapeDtypeStruct((PER_X * rows, HD), BF16),) * XN,
        in_specs=[pl.BlockSpec(memory_space=pltpu.SMEM)] + in_hbm(PER_X + PIECES) + anywhere(later),
        out_specs=tuple(in_hbm(XN)),
        scratch_shapes=[
            pltpu.VMEM((PER_X * rows, width), BF16),
            pltpu.VMEM((XN * HD, width), BF16),
            pltpu.VMEM((XN, PER_X * rows, HD), BF16),
            pltpu.SemaphoreType.DMA((PER_X + PIECES,)),
            pltpu.SemaphoreType.DMA((XN,)),
        ],
        compiler_params=params(60),
        cost_estimate=cost(0.2),
        name="attention_grad",
    )(place, *grads, *pieces, *later)


def project_kernel(place_ref, *refs):
    attns, pieces, outs = refs[:XN], refs[XN:XN + PIECES], refs[-11:-8]
    a_in, w_s, a_s, own_s, across_s, send_s, in_sems, out_sems = refs[-8:]
    rows, width = outs[0].shape
    arriving = weight_copies(pieces, w_s, in_sems, XN)
    for j in range(XN):
        arriving.append(pltpu.make_async_copy(attns[j], a_in.at[j], in_sems.at[j]))
    for copy in arriving:
        copy.start()
    for copy in arriving:
        copy.wait()
    for n, bits in enumerate((0, 2, 1, 3)):
        for j in range(XN):
            a_s[n * rows:(n + 1) * rows, j * HD:(j + 1) * HD] = a_in[
                j, rows_at(place_ref, bits, rows), :
            ]
    step = 512
    for n in range(0, width, step):
        cols = slice(n, n + step)
        acc = dot(a_s[...], w_s[:, cols], ((1,), (0,)))
        own_s[:, cols] = acc[:rows]
        across_s[:, cols] = acc[rows:2 * rows].astype(BF16)
        send_s[:, cols] = acc[2 * rows:].astype(BF16)
        for k, (result, out) in enumerate(zip((own_s, across_s, send_s), outs)):
            pltpu.make_async_copy(result.at[:, cols], out.at[:, cols], out_sems.at[k]).start()
    for k, (result, out) in enumerate(zip((own_s, across_s, send_s), outs)):
        pltpu.make_async_copy(result, out, out_sems.at[k]).wait()


def project(place, attns, pieces, *later):
    rows, width = pieces[0].shape
    shapes = (((rows, width), F32), ((rows, width), BF16), ((2 * rows, width), BF16))
    return pl.pallas_call(
        project_kernel,
        out_shape=tuple(jax.ShapeDtypeStruct(*shape) for shape in shapes),
        in_specs=[pl.BlockSpec(memory_space=pltpu.SMEM)] + in_hbm(XN + PIECES) + anywhere(later),
        out_specs=tuple(in_hbm(3)),
        scratch_shapes=[
            pltpu.VMEM((XN, PER_X * rows, HD), BF16),
            pltpu.VMEM((XN * HD, width), BF16),
            pltpu.VMEM((PER_X * rows, XN * HD), BF16),
        ]
        + [pltpu.VMEM(*shape) for shape in shapes]
        + [pltpu.SemaphoreType.DMA((XN + PIECES,)), pltpu.SemaphoreType.DMA((3,))],
        compiler_params=params(60),
        cost_estimate=cost(0.2),
        name="project",
    )(place, *attns, *pieces, *later)


def unpack_kernel(in_ref, out_ref):
    rows = out_ref.shape[1]
    for h in range(in_ref.shape[0]):
        for t in range(3):
            out_ref[t, :, h * HD:(h + 1) * HD] = in_ref[h, t * rows:(t + 1) * rows, :]


def unpack(received):
    heads, rows = received.shape[0], received.shape[1] // 3
    return pl.pallas_call(
        unpack_kernel,
        out_shape=jax.ShapeDtypeStruct((3, rows, heads * HD), BF16),
        in_specs=whole(1),
        out_specs=whole(1)[0],
        compiler_params=params(24),
        cost_estimate=cost(2),
        name="unpack",
    )(received)


def choose_kernel(section_ref, first_ref, second_ref, *refs):
    out_ref = refs[-1]
    out_ref[...] = jnp.where(section_ref[0] == section_ref[1], first_ref[...], second_ref[...])


def choose(sections, first, second, *later):
    return pl.pallas_call(
        choose_kernel,
        out_shape=jax.ShapeDtypeStruct(first.shape, first.dtype),
        in_specs=[pl.BlockSpec(memory_space=pltpu.SMEM)] + whole(2) + anywhere(later),
        out_specs=whole(1)[0],
        compiler_params=params(16),
        cost_estimate=cost(2),
        name="choose",
    )(sections, first, second, *later)


def settle_kernel(in_ref, *refs):
    out_ref = refs[-1]
    out_ref[...] = in_ref[...]


def settle(array, *later):
    return pl.pallas_call(
        settle_kernel,
        out_shape=jax.ShapeDtypeStruct(array.shape, array.dtype),
        in_specs=whole(1) + anywhere(later),
        out_specs=whole(1)[0],
        compiler_params=params(8),
        cost_estimate=cost(0.2),
        name="settle",
    )(array, *later)


def shifted(array, axis, by):
    length = lax.axis_size(axis)
    pairs = [(i, i + by) for i in range(length) if 0 <= i + by < length]
    return lax.ppermute(array, axis, pairs)


def rotated(array, axis, by):
    length = lax.axis_size(axis)
    return lax.ppermute(array, axis, [(i, (i + by) % length) for i in range(length)])


def per_sample(seg, table):
    onehot = (seg[:, None] == jnp.arange(table.shape[0], dtype=jnp.int32)[None, :]).astype(F32)
    return jnp.sum(onehot[:, :, None] * table[None, :, :], axis=1)


def exchange(array):
    return lax.all_to_all(array, "seq", 0, 0, tiled=True)


def body(hidden_in, queries, keys, values, segments, gates, out_weight, upstream, fresh, loss_grad):
    section = lax.axis_index("pipe")
    last_section = lax.axis_size("pipe") - 1
    place = lax.axis_index("seq")[None]

    own = out_weight[0]
    pieces = tuple(along_x(own, -offset % XN) for offset in OFFSETS)

    fwd = exchange(pack(queries, keys, values, segments, 0))
    local_seg = segments[0]
    g_scaled = (per_sample(local_seg[1], gates[0, 1]) * upstream[0].astype(F32)).astype(BF16)
    g_across = lax.ppermute(g_scaled, "seq", YSWAP)
    g_core = lax.ppermute(g_scaled, "seq", CORE)
    g_both = lax.ppermute(g_across, "seq", CORE)
    gate_tok = per_sample(local_seg[0], gates[0, 0])
    grads = attention_grad(place, (g_scaled, g_core, g_across, g_both), pieces)
    packed = pack(queries, keys, values, segments, 1, g_across, gate_tok, *pieces[1:])
    bwd = exchange(packed)

    turned = settle(upstream[0], fwd)
    moved = shifted(turned, "pipe", -1)
    attns = attention_forward(place, fwd, grads[0], gate_tok, turned)
    grads = tuple(along_x(g, o) for g, o in zip(grads, OFFSETS))
    attns = tuple(along_x(a, o) for a, o in zip(attns, OFFSETS))

    attns = (attns[0], attns[2], attns[1], follow(attns[3], bwd, moved, *grads[1:]))
    part, part_across, part_send = project(place, attns, pieces)
    received = lax.ppermute(part_send, "seq", CORE)
    rows = part.shape[0]
    across = (part_across.astype(F32) + received[rows:].astype(F32)).astype(BF16)
    grads = attention_backward(place, bwd, grads, across)
    across = lax.ppermute(across, "seq", YSWAP)
    proj = part + received[:rows].astype(F32) + across.astype(F32)
    section_out = (hidden_in[0].astype(F32) + gate_tok * proj).astype(BF16)
    section_out = jnp.where(section == last_section, fresh, section_out)
    next_act = rotated(section_out, "pipe", 1)

    sections = jnp.stack([section, last_section * jnp.ones_like(section)])
    next_grad = choose(sections, loss_grad, moved)
    qkv_grads = unpack(exchange(grads))
    return (next_act[None], next_grad[None], qkv_grads[None])


def solution(mesh):
    in_specs = (
        P("pipe", "seq", None),
        P("pipe", None, "seq", None),
        P("pipe", None, "seq", None),
        P("pipe", None, "seq", None),
        P("pipe", None, "seq"),
        P("pipe", None, None, None),
        P("pipe", "seq", None),
        P("pipe", "seq", None),
        P("seq", None),
        P("seq", None),
    )
    out_specs = (P("pipe", "seq", None), P("pipe", "seq", None), P("pipe", None, "seq", None))
    return jax.shard_map(body, mesh=mesh, in_specs=in_specs, out_specs=out_specs, check_vma=False)
```
